32 devices in a mesh: rows: 4 (over y, x), feat: 8 (over z, core).
Axes of the slice: x: 2, y: 2, z: 4, core: 2. Of those that a mesh axis runs over, the one named last changes fastest.
Arguments:
- pool_a: bfloat16 [5120, 9216], P('rows', 'feat'), may hold values from -6 to 6
- pool_b: bfloat16 [5120, 9216], P('rows', 'feat'), may hold values from -6 to 6
- weight_a: bfloat16 [9216, 4096], P('feat'), may hold values from -0.09375 to 0.09375
- weight_b: bfloat16 [9216, 4096], P('feat'), may hold values from -0.09375 to 0.09375
- bias_a: float32 [4096], P('feat'), may hold values from -3 to 3
- bias_b: float32 [4096], P('feat'), may hold values from -3 to 3
- stitch: float32 [2, 2, 4096], P(None, None, 'feat'), may hold values from 0.1 to 1
- crop_count: int32 [5120], P('rows'), may hold values from 1 to 4
- row_mask: int32 [5120], P('rows'), may hold values from 0 to 1, as said below
- outgrad_a: bfloat16 [5120, 4096], P('rows', 'feat'), may hold values from -6 to 6
- outgrad_b: bfloat16 [5120, 4096], P('rows', 'feat'), may hold values from -6 to 6
Outputs:
- mixed_a: bfloat16 [5120, 4096], P('rows', 'feat')
- mixed_b: bfloat16 [5120, 4096], P('rows', 'feat')
- pool_grad_a: bfloat16 [5120, 9216], P('rows', 'feat')
- pool_grad_b: bfloat16 [5120, 9216], P('rows', 'feat')
- weight_grad_a: float32 [9216, 4096], P('feat', 'rows')
- weight_grad_b: float32 [9216, 4096], P('feat', 'rows')
- bias_grad_a: float32 [4096], P(('feat', 'rows'))
- bias_grad_b: float32 [4096], P(('feat', 'rows'))
- stitch_grad: float32 [2, 2, 4096], P(None, None, ('feat', 'rows'))
The draws below stay inside these ranges and needn't reach their ends.
Inputs may be any that keep to these rules, and one draw needn't show every extreme that they name: `row_mask`: in each aligned block of 1280 rows (the rows of one device) the rows with mask 1 come first and fill half of the block or more; some block is all ones.
All inputs are finite; a program needn't handle non-finite values.
Results may differ from the reference program's by a relative error of at most 0.017.
Values may be sent and summed in bfloat16 or wider, within the bound.
A program may use at most 256 MiB of HBM per device.

```python
import jax
import jax.numpy as jnp
from jax import lax

IN = 9216
CH = 4096
ROWS_DEV = 1280
ROWS = 5120


def draw_row_mask(key, part):
    key = jax.random.fold_in(key, 7)
    key_live, key_full = jax.random.split(key)
    blocks = ROWS // ROWS_DEV
    live = jax.random.randint(key_live, (blocks,), ROWS_DEV // 2, ROWS_DEV + 1)
    full_block = jax.random.randint(key_full, (), 0, blocks)
    live = jnp.where(jnp.arange(blocks) == full_block, ROWS_DEV, live)
    packed = (jnp.arange(ROWS_DEV)[None, :] < live[:, None]).astype(jnp.int32)
    return packed.reshape(ROWS)


def place_ends(entries, own_key, low, high):
    extent = entries.shape
    spot = [jax.random.randint(jax.random.fold_in(own_key, axis), (), 0, extent[axis]) for axis in range(len(extent))]
    entries = entries.at[tuple(spot)].set(low)
    longest = extent.index(max(extent))
    spot[longest] = (spot[longest] + 1) % extent[longest]
    return entries.at[tuple(spot)].set(high)


def spiked(values, rng, source, target, shards_of, factor):
    def block_of(dim):
        return (jnp.arange(values.shape[dim]) // (values.shape[dim] // shards_of)).reshape((-1,) + (1,) * (values.ndim - 1 - dim))

    first = jax.random.permutation(rng, shards_of)[block_of(target)]
    far = (block_of(target) + shards_of // 2) % shards_of
    return jnp.where((block_of(source) == first) | (block_of(source) == far), factor * values, values)


def levels(own_key, dims, cuts, smallest, largest):
    factor_of, own = 1.0, jax.random.fold_in(own_key, 6)
    for position, shards_of in cuts:
        heights = jnp.exp(jax.random.uniform(jax.random.fold_in(own, position), (shards_of,), jnp.float32, smallest / len(cuts), largest / len(cuts)))
        factor_of = factor_of * jnp.repeat(heights, dims[position] // shards_of).reshape([-1 if axis == position else 1 for axis in range(len(dims))])
    return factor_of


def scatter_about(rng, shape, width, reach, cuts=(), kind=jnp.bfloat16):
    array = jax.random.normal(rng, shape, jnp.float32) * width
    if len(cuts) > 0:
        array = levels(rng, shape, cuts, -0.22, 0.18) * array
    return jnp.clip(array, min=-reach, max=reach).astype(kind)


def noise_with(key, dims, spread, bound, cuts, heavy, kind=jnp.bfloat16):
    array = spread * jax.random.normal(key, dims, jnp.float32)
    if cuts:
        array = array * levels(key, dims, cuts, -0.22, 0.18)
    return jnp.clip(spiked(array, jax.random.fold_in(key, 3), *heavy), -bound, bound).astype(kind)


def setup_inputs(seed: int = 0) -> dict:
    arg_keys = jax.random.split(jax.random.key(seed), 12)
    pool_a = scatter_about(arg_keys[0], (ROWS, IN), 1.0, 6.0, ((0, 4), (1, 8)))
    pool_b = scatter_about(arg_keys[1], (ROWS, IN), 1.0, 6.0, ((0, 4), (1, 8)))
    weight_a = noise_with(arg_keys[2], (IN, CH), IN ** -0.5, 0.09375, ((0, 8),), (0, 1, 8, 2.0))
    weight_b = noise_with(arg_keys[3], (IN, CH), IN ** -0.5, 0.09375, ((0, 8),), (0, 1, 8, 2.0))
    bias_a = scatter_about(arg_keys[4], (CH,), 0.5, 3.0, ((0, 8),), jnp.float32)
    bias_b = scatter_about(arg_keys[5], (CH,), 0.5, 3.0, ((0, 8),), jnp.float32)
    stitch = jnp.clip(0.1 + 0.9 * jax.random.uniform(arg_keys[6], (2, 2, CH), jnp.float32) ** levels(arg_keys[6], (2, 2, CH), ((2, 8),), -0.2, 0.2), 0.1, 1.0)
    crop_count = place_ends(jax.random.randint(arg_keys[7], (ROWS,), 1, 5), jax.random.fold_in(arg_keys[7], 1), 1, 4).astype(jnp.int32)
    row_mask = draw_row_mask(jax.random.fold_in(arg_keys[11], 71), 0)
    outgrad_a = scatter_about(arg_keys[9], (ROWS, CH), 1.0, 6.0, ((0, 4), (1, 8)))
    outgrad_b = scatter_about(arg_keys[10], (ROWS, CH), 1.0, 6.0, ((0, 4), (1, 8)))
    return dict(pool_a=pool_a, pool_b=pool_b, weight_a=weight_a, weight_b=weight_b, bias_a=bias_a, bias_b=bias_b, stitch=stitch, crop_count=crop_count, row_mask=row_mask, outgrad_a=outgrad_a, outgrad_b=outgrad_b)


@jax.custom_vjp
def low(v):
    return lax.optimization_barrier(v.astype(jnp.bfloat16)).astype(jnp.float32)

@jax.custom_vjp
def low_back(v):
    return v

def low_keep(v):
    return (low(v), None)

def low_pass(kept, grad):
    return (grad,)

def back_keep(v):
    return (v, None)

def back_low(kept, grad):
    return (low(grad),)
low.defvjp(low_keep, low_pass)
low_back.defvjp(back_keep, back_low)

def forward(in_a, in_b, wgt_a, wgt_b, bias_one, bias_two, stitch_w, scale_rows):
    pre_a = low_back(jnp.dot(in_a, wgt_a, precision=lax.Precision.HIGHEST) + bias_one)
    pre_b = low_back(jnp.dot(in_b, wgt_b, precision=lax.Precision.HIGHEST) + bias_two)
    act_a = jax.nn.gelu(pre_a, approximate=False)
    act_b = jax.nn.gelu(pre_b, approximate=False)
    out_a = stitch_w[0, 0] * act_a + stitch_w[0, 1] * act_b
    out_b = stitch_w[1, 0] * act_a + stitch_w[1, 1] * act_b
    return (out_a * scale_rows[:, None], out_b * scale_rows[:, None])

def reference(pool_a, pool_b, weight_a, weight_b, bias_a, bias_b, stitch, crop_count, row_mask, outgrad_a, outgrad_b):
    row_scale = row_mask.astype(jnp.float32) / crop_count.astype(jnp.float32)
    blocks = ROWS // ROWS_DEV

    def split(value):
        return value.astype(jnp.float32).reshape((blocks, ROWS_DEV) + value.shape[1:])
    params = (weight_a.astype(jnp.float32), weight_b.astype(jnp.float32), bias_a, bias_b, stitch)

    def step(carry, items):
        in_a, in_b, scale_rows, gout_a, gout_b = items

        def apply(x_one, x_two, w_one, w_two, b_one, b_two, st_w):
            return forward(x_one, x_two, w_one, w_two, b_one, b_two, st_w, scale_rows)
        outputs, pull = jax.vjp(apply, in_a, in_b, *params)
        grads = pull((gout_a, gout_b))
        carry = tuple((total + part for total, part in zip(carry, grads[2:])))
        return (carry, (outputs[0], outputs[1], grads[0], grads[1]))
    start = tuple((jnp.zeros_like(param) for param in params))
    totals, stacked = lax.scan(step, start, (split(pool_a), split(pool_b), split(row_scale), split(outgrad_a), split(outgrad_b)))
    mixed_a = stacked[0].reshape(ROWS, CH).astype(jnp.bfloat16)
    mixed_b = stacked[1].reshape(ROWS, CH).astype(jnp.bfloat16)
    pool_grad_a = stacked[2].reshape(ROWS, IN).astype(jnp.bfloat16)
    pool_grad_b = stacked[3].reshape(ROWS, IN).astype(jnp.bfloat16)
    return (mixed_a, mixed_b, pool_grad_a, pool_grad_b, totals[0], totals[1], totals[2], totals[3], totals[4])
```

```python
import functools

import jax
import jax.numpy as jnp
from jax import lax
from jax.experimental import pallas as pl
from jax.experimental.pallas import tpu as pltpu
from jax.sharding import PartitionSpec as P

MESH = pl.DeviceIdType.MESH
F32 = jnp.float32
BF16 = jnp.bfloat16
LANE = 128
ROW_BLOCKS = 5
SUBS = 2
RIGHT, LEFT = 0, 1
FAR, NEAR, KEEP, OWN = 0, 1, 2, 3
INV_SQRT2 = 0.7071067811865476
INV_SQRT_2PI = 0.3989422804014327


def dot(lhs, rhs):
    return lax.dot_general(lhs, rhs, (((1,), (0,)), ((), ())), preferred_element_type=F32)


def dot_t(lhs, rhs):
    return lax.dot_general(lhs, rhs, (((1,), (1,)), ((), ())), preferred_element_type=F32)


def kernel(line, rows, width, chl, *refs):
    (
        pool_a, pool_b, weight_a, weight_b, par, scale, og_a, og_b,
        mixed_a, mixed_b, pg_a, pg_b, wg_a, wg_b, stats,
        pool_v, pool_t, wf, wb, part, xr, rbuf, gath, acc, wsend, wrecv, wout,
        og_v, mix_v, pg_v, sacc, sred, srecv,
        pool_s, wf_s, wb_s, xs_send, xs_recv, z_send, z_recv, g_send, g_recv,
        w_send, w_recv, wout_s, og_s, mix_s, pg_s, st_send, st_recv, credit, wcredit,
    ) = refs
    L = line
    NB, NS = ROW_BLOCKS, SUBS
    RB = rows // NB
    SB = RB // NS
    NCH = chl // LANE
    U = NCH * NB
    HALF = L // 2
    SENDING = U + 2
    TICKS = (U + 2 + NB) * L
    pools, weights = (pool_a, pool_b), (weight_a, weight_b)
    ogs, mixeds = (og_a, og_b), (mixed_a, mixed_b)
    pgs, wgs = (pg_a, pg_b), (wg_a, wg_b)

    f = lax.axis_index("feat")
    r = lax.axis_index("rows")
    p = lax.div(f, 2)
    c = lax.rem(f, 2)
    sib = f + 1 - 2 * c
    xp = r + 1 - 2 * lax.rem(r, 2)
    yp = lax.rem(r + 2, 4)
    dp = 3 - r
    has_left, has_right = p > 0, p < L - 1
    pos = (p, L - 1 - p)
    nxt = (f + 2, f - 2)

    def remote(src, dst, send, recv, **dev):
        return pltpu.make_async_remote_copy(
            src_ref=src, dst_ref=dst, send_sem=send, recv_sem=recv, device_id=dev, device_id_type=MESH
        )

    def signal(sem, **dev):
        pl.semaphore_signal(sem, inc=1, device_id=dev, device_id_type=MESH)

    def lanes(index):
        return pl.ds(pl.multiple_of(index * LANE, LANE), LANE)

    def block_rows(i):
        return pl.ds(pl.multiple_of(i * RB, RB), RB)

    def sub_rows(b):
        return pl.ds(b * SB, SB)

    def pool_load(u, t):
        slot = lax.rem(u, 2)
        return pltpu.make_async_copy(
            pools[t].at[block_rows(lax.rem(u, NB)), :], pool_v.at[slot, t], pool_s.at[slot, t]
        )

    def wf_loads(tick):
        j = lax.div(tick, L * NB)
        s = lax.rem(tick, L)
        slot = lax.rem(tick, 2)
        core = jnp.where(s < HALF, 1 - c, c)
        first = 2 * lax.rem(s, HALF)
        out = []
        for t in range(2):
            for k in range(2):
                owner = 2 * (first + k) + core
                out.append(
                    pltpu.make_async_copy(
                        weights[t].at[:, lanes(owner * NCH + j)],
                        wf.at[slot, t, :, k * LANE : (k + 1) * LANE],
                        wf_s.at[slot, t, k],
                    )
                )
        return out

    def wb_loads(j, t):
        out = []
        for q in range(L):
            for k in range(2):
                out.append(
                    pltpu.make_async_copy(
                        weights[t].at[:, lanes((2 * q + k) * NCH + j)],
                        wb.at[t, q, :, k * LANE : (k + 1) * LANE],
                        wb_s.at[t, q, k],
                    )
                )
        return out

    def og_load(u, t):
        slot = lax.rem(u, 2)
        return pltpu.make_async_copy(
            ogs[t].at[block_rows(lax.rem(u, NB)), lanes(lax.div(u, NB))], og_v.at[slot, t], og_s.at[slot, t]
        )

    def mix_store(u, b, t):
        i, j = lax.rem(u, NB), lax.div(u, NB)
        dst = pl.ds(pl.multiple_of(i * RB + b * SB, SB), SB)
        return pltpu.make_async_copy(mix_v.at[b, t], mixeds[t].at[dst, lanes(j)], mix_s.at[b, t])

    def part_copy(u, tile, per3):
        return remote(
            part.at[lax.rem(u, 2), 0, pl.ds(2 * tile, 2)],
            xr.at[lax.rem(u, 4), pl.ds(2 * tile, 2)],
            xs_send.at[tile],
            xs_recv.at[tile, per3],
            feat=sib,
        )

    def gath_block(u, o, b):
        i, j = lax.rem(u, NB), lax.div(u, NB)
        return gath.at[lax.rem(j, 2), o, c, pl.ds(pl.multiple_of(i * RB + b * SB, SB), SB), :]

    def gath_copy(u, o, d, b, s, per3):
        block = gath_block(u, o, b)
        return remote(block, block, z_send.at[d, b, s], z_recv.at[d, b, s, per3], feat=nxt[d])

    def share_copy(u, o, d, b, s, per3):
        block = gath_block(u, o, b)
        return remote(block, block, g_send.at[d, b, s], g_recv.at[d, b, s, per3], feat=sib)

    def share_wait(u, o, d, b, s, per3):
        i, j = lax.rem(u, NB), lax.div(u, NB)
        block = gath.at[lax.rem(j, 2), o, 1 - c, pl.ds(pl.multiple_of(i * RB + b * SB, SB), SB), :]
        remote(block, block, g_send.at[d, b, s], g_recv.at[d, b, s, per3], feat=sib).wait_recv()

    def sum_copy(u, d, b, s, per3):
        u3 = lax.rem(u, 3)
        return remote(
            rbuf.at[u3, d, s - 1, sub_rows(b), :],
            rbuf.at[u3, d, s, sub_rows(b), :],
            z_send.at[d, b, s],
            z_recv.at[d, b, s, per3],
            feat=nxt[d],
        )

    def sum_wait(u, d, b, s, per3):
        u3 = lax.rem(u, 3)
        block = rbuf.at[u3, d, s, sub_rows(b), :]
        remote(block, block, z_send.at[d, b, s], z_recv.at[d, b, s, per3], feat=nxt[d]).wait_recv()

    def own_sum(u, o, b):
        mine = part[lax.rem(u, 2), 1, o, sub_rows(b), :].astype(F32)
        return mine + xr[lax.rem(u, 4), o, sub_rows(b), :].astype(F32)

    def fold(v):
        return jnp.sum(v.reshape(SB // 8, 8, LANE), axis=0)

    def finalize(u, b, per):
        i, j = lax.rem(u, NB), lax.div(u, NB)
        last3 = lax.rem(per - 1, 3)

        @pl.when(has_left)
        def _():
            sum_wait(u, RIGHT, b, L - 1, last3)

        @pl.when(has_right)
        def _():
            sum_wait(u, LEFT, b, L - 1, last3)

        if b == 0:
            og_load(u, 0).wait()
            og_load(u, 1).wait()

        @pl.when(u >= 1)
        def _():
            mix_store(u, b, 0).wait()
            mix_store(u, b, 1).wait()

        u3 = lax.rem(u, 3)
        total = own_sum(u, p, b)
        total = total + rbuf[u3, RIGHT, L - 1, sub_rows(b), :].astype(F32)
        total = total + rbuf[u3, LEFT, L - 1, sub_rows(b), :].astype(F32)
        ch = lanes(j)
        s00, s01, s10, s11 = (par[k : k + 1, ch] for k in range(4))
        here = pl.ds(pl.multiple_of(i * RB + b * SB, SB), SB)
        row = scale[here, :]
        gy_a = row * og_v[lax.rem(u, 2), 0, sub_rows(b), :].astype(F32)
        gy_b = row * og_v[lax.rem(u, 2), 1, sub_rows(b), :].astype(F32)

        def gelu(v):
            cdf = 0.5 * (1.0 + lax.erf(v * INV_SQRT2))
            return v * cdf, cdf + v * (INV_SQRT_2PI * jnp.exp(-0.5 * v * v))

        act_a, slope_a = gelu(total[:, :LANE] + par[4:5, ch])
        act_b, slope_b = gelu(total[:, LANE:] + par[5:6, ch])
        mix_v[b, 0] = (row * (s00 * act_a + s01 * act_b)).astype(BF16)
        mix_v[b, 1] = (row * (s10 * act_a + s11 * act_b)).astype(BF16)
        mix_store(u, b, 0).start()
        mix_store(u, b, 1).start()
        gpre_a = ((s00 * gy_a + s10 * gy_b) * slope_a).astype(BF16)
        gpre_b = ((s01 * gy_a + s11 * gy_b) * slope_b).astype(BF16)
        gath[lax.rem(j, 2), p, c, here, :LANE] = gpre_a
        gath[lax.rem(j, 2), p, c, here, LANE:] = gpre_b
        sacc[j, 0] += fold(gy_a * act_a)
        sacc[j, 1] += fold(gy_a * act_b)
        sacc[j, 2] += fold(gy_b * act_a)
        sacc[j, 3] += fold(gy_b * act_b)
        sacc[j, 4] += fold(gpre_a.astype(F32))
        sacc[j, 5] += fold(gpre_b.astype(F32))

    def first_partner(t):
        return jnp.where(t == 0, xp, yp)

    def second_partner(t):
        return jnp.where(t == 0, yp, xp)

    def w_copy(t, kind):
        dst = KEEP if kind == KEEP else kind
        return remote(
            wsend.at[t, kind],
            wrecv.at[t, dst],
            w_send.at[t, kind],
            w_recv.at[t, dst],
            rows=second_partner(t) if kind == KEEP else first_partner(t),
        )

    per_row = 2 * L // 4

    def wout_stores(j, t):
        return [
            pltpu.make_async_copy(
                wout.at[t, :, k * LANE : (k + 1) * LANE], wgs[t].at[:, lanes(k * NCH + j)], wout_s.at[t, k]
            )
            for k in range(per_row)
        ]

    def pg_store(t, i, slot):
        return pltpu.make_async_copy(pg_v.at[slot], pgs[t].at[block_rows(i), :], pg_s.at[slot])

    for t in range(2):
        pool_load(0, t).start()
    for copy in wf_loads(0):
        copy.start()

    bar = pltpu.get_barrier_semaphore()

    @pl.when(has_left)
    def _():
        signal(bar, feat=f - 2)

    @pl.when(has_right)
    def _():
        signal(bar, feat=f + 2)

    signal(bar, feat=sib)
    signal(bar, rows=xp)
    signal(bar, rows=yp)
    signal(bar, rows=dp)
    sacc[...] = jnp.zeros_like(sacc)

    @pl.when(jnp.logical_not(has_left))
    def _():
        for k in range(3):
            rbuf[k, RIGHT, L - 1] = jnp.zeros((RB, 2 * LANE), BF16)

    @pl.when(jnp.logical_not(has_right))
    def _():
        for k in range(3):
            rbuf[k, LEFT, L - 1] = jnp.zeros((RB, 2 * LANE), BF16)

    pl.semaphore_wait(bar, 4 + has_left.astype(jnp.int32) + has_right.astype(jnp.int32))

    def tick(T, carry):
        per, s = lax.div(T, L), lax.rem(T, L)
        per3 = lax.rem(per, 3)
        u = per - 2
        ur = per - 1
        uf = per
        gathers = (u >= 0) & (u < U)
        gathered = (u >= 1) & (u <= U)
        sums = (ur >= 0) & (ur < U)
        summed = (ur >= 1) & (ur <= U)

        @pl.when((s == 0) & (per >= 2) & (per < SENDING))
        def _():
            @pl.when(has_left)
            def _():
                pl.semaphore_wait(credit.at[0], 1)

            @pl.when(has_right)
            def _():
                pl.semaphore_wait(credit.at[1], 1)

            pl.semaphore_wait(credit.at[2], 1)

        @pl.when((s == 1) & sums)
        def _():
            for k in range(HALF):
                part_copy(ur, k, lax.rem(per - 1, 3)).wait_recv()

        for b in range(NS):

            @pl.when((s == 0) & gathers)
            def _():
                finalize(u, b, per)

            for d in (RIGHT, LEFT):
                gather_here = pos[d] >= s
                o = p - s if d == RIGHT else p + s
                dest = p + (L - s) if d == RIGHT else p - (L - s)
                shares = (s >= 1) if d == LEFT else (s >= 0)

                @pl.when(gathered & gather_here)
                def _():
                    @pl.when(pos[d] < L - 1)
                    def _():
                        gath_copy(u, o, d, b, s, per3).wait_send()

                    @pl.when(shares)
                    def _():
                        share_copy(u, o, d, b, s, per3).wait_send()

                @pl.when(gathers & gather_here)
                def _():
                    @pl.when(s >= 1)
                    def _():
                        gath_copy(u, o, d, b, s - 1, per3).wait_recv()

                    @pl.when(pos[d] < L - 1)
                    def _():
                        gath_copy(u, o, d, b, s, per3).start()

                    @pl.when(shares)
                    def _():
                        share_copy(u, o, d, b, s, per3).start()

                @pl.when(summed & jnp.logical_not(gather_here))
                def _():
                    sum_copy(ur, d, b, s, per3).wait_send()

                @pl.when(sums & jnp.logical_not(gather_here))
                def _():
                    u3 = lax.rem(ur, 3)

                    @pl.when(pos[d] >= 1)
                    def _():
                        sum_wait(ur, d, b, s - 1, per3)
                        both = own_sum(ur, dest, b) + rbuf[u3, d, s - 1, sub_rows(b), :].astype(F32)
                        rbuf[u3, d, s - 1, sub_rows(b), :] = both.astype(BF16)

                    @pl.when(pos[d] < 1)
                    def _():
                        rbuf[u3, d, s - 1, sub_rows(b), :] = own_sum(ur, dest, b).astype(BF16)

                    sum_copy(ur, d, b, s, per3).start()

        before = T - 1 + L
        per_m, s_m = lax.div(before, L) - 1, lax.rem(before, L)
        u_m = per_m - 2

        @pl.when((u_m >= 0) & (u_m < U))
        def _():
            for b in range(NS):
                for d in (RIGHT, LEFT):
                    o = p - s_m if d == RIGHT else p + s_m
                    shares = (s_m >= 1) if d == LEFT else (s_m >= 0)

                    @pl.when((pos[d] >= s_m) & shares)
                    def _():
                        share_wait(u_m, o, d, b, s_m, lax.rem(per_m, 3))

        @pl.when((s == 1) & (ur >= 0) & (ur < U))
        def _():
            og_load(ur, 0).start()
            og_load(ur, 1).start()

        @pl.when((uf >= 1) & (uf <= U) & (s < HALF))
        def _():
            part_copy(uf, s, per3).wait_send()

        @pl.when(uf < U)
        def _():
            u2 = lax.rem(uf, 2)

            @pl.when(s == 0)
            def _():
                for t in range(2):
                    pool_load(uf, t).wait()

                @pl.when(uf + 1 < U)
                def _():
                    for t in range(2):
                        pool_load(uf + 1, t).start()

            for copy in wf_loads(T):
                copy.wait()

            @pl.when(T + 1 < U * L)
            def _():
                for copy in wf_loads(T + 1):
                    copy.start()

            which = lax.div(s, HALF)
            first = 2 * lax.rem(s, HALF)
            for t in range(2):
                res = dot(pool_v[u2, t], wf[lax.rem(T, 2), t]).astype(BF16)
                part[u2, which, first, :, t * LANE : (t + 1) * LANE] = res[:, :LANE]
                part[u2, which, first + 1, :, t * LANE : (t + 1) * LANE] = res[:, LANE:]

            @pl.when(s < HALF)
            def _():
                part_copy(uf, s, per3).start()

            @pl.when((uf < NB) & (s == L - 1))
            def _():
                for t in range(2):
                    pool_t[t, :, block_rows(uf)] = pool_v[u2, t].T

        since = jnp.maximum(T - 2 * L, 0)
        jb = lax.div(since, NB * L) - 1
        tau = lax.rem(since, NB * L)
        jb2 = lax.rem(jb, 2)

        @pl.when(jb >= 0)
        def _():
            @pl.when((tau == 0) & (jb >= 1))
            def _():
                pl.semaphore_wait(wcredit.at[0], 1)

            @pl.when((tau == 1) & (jb >= 1))
            def _():
                pl.semaphore_wait(wcredit.at[1], 1)

            for t in range(2):

                @pl.when(tau == 2 + t)
                def _():
                    for copy in wb_loads(jb, t):
                        copy.start()

            @pl.when(tau < 8)
            def _():
                t = lax.rem(tau, 2)
                kind = lax.div(tau, 2)
                one, two = first_partner(t), second_partner(t)
                owner = jnp.where(kind == FAR, dp, jnp.where(kind == NEAR, one, jnp.where(kind == KEEP, two, r)))
                cols = []
                for k in range(per_row):
                    fo = owner * per_row + k
                    cols.append(gath[jb2, lax.div(fo, 2), lax.rem(fo, 2), :, lanes(t)])
                cols = jnp.concatenate(cols, axis=1)
                step = 384 if width % 384 == 0 else LANE
                for m in range(0, width, step):
                    wsend[t, kind, m : m + step, :] = dot(pool_t[t, m : m + step, :], cols).astype(BF16)
                for way in (FAR, NEAR):

                    @pl.when(kind == way)
                    def _():
                        w_copy(t, way).start()

            for t in range(2):

                @pl.when(tau == 9 + t)
                def _():
                    w_copy(t, FAR).wait_recv()
                    both = wsend[t, KEEP].astype(F32) + wrecv[t, FAR].astype(F32)
                    wsend[t, KEEP] = both.astype(BF16)
                    w_copy(t, KEEP).start()

                @pl.when(tau == 15 + t)
                def _():
                    w_copy(t, NEAR).wait_recv()
                    w_copy(t, KEEP).wait_recv()
                    for kind in (FAR, NEAR, KEEP):
                        w_copy(t, kind).wait_send()

                    @pl.when(jb >= 1)
                    def _():
                        for copy in wout_stores(jb, t):
                            copy.wait()

                    both = wsend[t, OWN].astype(F32) + wrecv[t, NEAR].astype(F32)
                    wout[t] = both + wrecv[t, KEEP].astype(F32)
                    for copy in wout_stores(jb, t):
                        copy.start()

            @pl.when((tau == 17) & (jb < NCH - 1))
            def _():
                signal(wcredit.at[0], rows=xp)
                signal(wcredit.at[1], rows=yp)

            @pl.when((tau >= 8) & (tau < 8 + 2 * NB))
            def _():
                piece = tau - 8
                t = lax.div(piece, NB)
                i = lax.rem(piece, NB)
                for tt in range(2):

                    @pl.when(piece == tt * NB)
                    def _():
                        for copy in wb_loads(jb, tt):
                            copy.wait()

                total = None
                for q in range(L):
                    cols = [gath[jb2, q, k, block_rows(i), lanes(t)] for k in range(2)]
                    term = dot_t(jnp.concatenate(cols, axis=1), wb[t, q])
                    total = term if total is None else total + term

                @pl.when(jb == 0)
                def _():
                    acc[t, block_rows(i), :] = total

                @pl.when((jb > 0) & (jb < NCH - 1))
                def _():
                    acc[t, block_rows(i), :] += total

                @pl.when(jb == NCH - 1)
                def _():
                    slot = lax.rem(piece, 2)

                    @pl.when(piece >= 2)
                    def _():
                        pg_store(0, 0, slot).wait()

                    pg_v[slot] = (acc[t, block_rows(i), :] + total).astype(BF16)
                    for tt in range(2):

                        @pl.when(t == tt)
                        def _():
                            pg_store(tt, i, slot).start()

        @pl.when((s == L - 1) & (per < SENDING - 2))
        def _():
            @pl.when(has_left)
            def _():
                signal(credit.at[1], feat=f - 2)

            @pl.when(has_right)
            def _():
                signal(credit.at[0], feat=f + 2)

            signal(credit.at[2], feat=sib)

        @pl.when(T == (U + 1) * L + 1)
        def _():
            for j in range(NCH):
                for k in range(6):
                    sred[j, k : k + 1, :] = jnp.sum(sacc[j, k], axis=0, keepdims=True)
                sred[j, 6:8, :] = jnp.zeros((2, LANE), F32)
            for k, peer in enumerate((xp, yp, dp)):
                remote(sred.at[peer], srecv.at[k], st_send.at[k], st_recv.at[k], rows=peer).start()

        return carry

    lax.fori_loop(0, TICKS, tick, 0)

    for k, peer in enumerate((xp, yp, dp)):
        copy = remote(sred.at[peer], srecv.at[k], st_send.at[k], st_recv.at[k], rows=peer)
        copy.wait_send()
        copy.wait_recv()
    stats[...] = sred[r] + srecv[0] + srecv[1] + srecv[2]
    for t in range(2):
        for b in range(NS):
            mix_store(U - 1, b, t).wait()
        for copy in wout_stores(NCH - 1, t):
            copy.wait()
        pg_store(0, 0, t).wait()


def fused(line, pool_a, pool_b, weight_a, weight_b, bias_a, bias_b, stitch, row_scale, outgrad_a, outgrad_b):
    rows, width = pool_a.shape
    chl = bias_a.shape[0]
    NB, NS, L = ROW_BLOCKS, SUBS, line
    RB = rows // NB
    SB = RB // NS
    NCH = chl // LANE
    per_row = 2 * L // 4
    par = jnp.concatenate([stitch.reshape(4, chl), bias_a[None], bias_b[None], jnp.zeros((2, chl), F32)], axis=0)
    hbm = pl.BlockSpec(memory_space=pl.ANY)
    vmem = pl.BlockSpec(memory_space=pltpu.VMEM)
    dma = pltpu.SemaphoreType.DMA
    out_shape = (
        jax.ShapeDtypeStruct((rows, chl), BF16),
        jax.ShapeDtypeStruct((rows, chl), BF16),
        jax.ShapeDtypeStruct((rows, width), BF16),
        jax.ShapeDtypeStruct((rows, width), BF16),
        jax.ShapeDtypeStruct((width, per_row * chl), F32),
        jax.ShapeDtypeStruct((width, per_row * chl), F32),
        jax.ShapeDtypeStruct((8, LANE), F32),
    )
    scratch = [
        pltpu.VMEM((2, 2, RB, width), BF16),
        pltpu.VMEM((2, width, rows), BF16),
        pltpu.VMEM((2, 2, width, 2 * LANE), BF16),
        pltpu.VMEM((2, L, width, 2 * LANE), BF16),
        pltpu.VMEM((2, 2, L, RB, 2 * LANE), BF16),
        pltpu.VMEM((4, L, RB, 2 * LANE), BF16),
        pltpu.VMEM((3, 2, L, RB, 2 * LANE), BF16),
        pltpu.VMEM((2, L, 2, rows, 2 * LANE), BF16),
        pltpu.VMEM((2, rows, width), F32),
        pltpu.VMEM((2, 4, width, per_row * LANE), BF16),
        pltpu.VMEM((2, 3, width, per_row * LANE), BF16),
        pltpu.VMEM((2, width, per_row * LANE), F32),
        pltpu.VMEM((2, 2, RB, LANE), BF16),
        pltpu.VMEM((NS, 2, SB, LANE), BF16),
        pltpu.VMEM((2, RB, width), BF16),
        pltpu.VMEM((NCH, 6, 8, LANE), F32),
        pltpu.VMEM((NCH, 8, LANE), F32),
        pltpu.VMEM((3, 8, LANE), F32),
        dma((2, 2)),
        dma((2, 2, 2)),
        dma((2, L, 2)),
        dma((L // 2,)),
        dma((L // 2, 3)),
        dma((2, NS, L)),
        dma((2, NS, L, 3)),
        dma((2, NS, L)),
        dma((2, NS, L, 3)),
        dma((2, 3)),
        dma((2, 3)),
        dma((2, per_row)),
        dma((2, 2)),
        dma((NS, 2)),
        dma((2,)),
        dma((3,)),
        dma((3,)),
        pltpu.SemaphoreType.REGULAR((3,)),
        pltpu.SemaphoreType.REGULAR((2,)),
    ]
    mixed_a, mixed_b, pg_a, pg_b, wg_a, wg_b, stats = pl.pallas_call(
        functools.partial(kernel, line, rows, width, chl),
        out_shape=out_shape,
        in_specs=[hbm, hbm, hbm, hbm, vmem, vmem, hbm, hbm],
        out_specs=(hbm, hbm, hbm, hbm, hbm, hbm, vmem),
        scratch_shapes=scratch,
        compiler_params=pltpu.CompilerParams(
            collective_id=0, has_side_effects=True, vmem_limit_bytes=VMEM_LIMIT
        ),
    )(pool_a, pool_b, weight_a, weight_b, par, row_scale[:, None], outgrad_a, outgrad_b)
    return mixed_a, mixed_b, pg_a, pg_b, wg_a, wg_b, stats[4], stats[5], stats[:4].reshape(2, 2, LANE)


VMEM_LIMIT = 62 * 1024 * 1024


def plain(pool_a, pool_b, weight_a, weight_b, bias_a, bias_b, stitch, row_scale, outgrad_a, outgrad_b):
    row = row_scale[:, None]

    def pre(pool, weight, bias):
        partial = dot(pool, weight).astype(BF16)
        return lax.psum_scatter(partial, "feat", scatter_dimension=1, tiled=True).astype(F32) + bias

    def gelu(v):
        cdf = 0.5 * (1.0 + lax.erf(v * INV_SQRT2))
        return v * cdf, cdf + v * (INV_SQRT_2PI * jnp.exp(-0.5 * v * v))

    act_a, slope_a = gelu(pre(pool_a, weight_a, bias_a))
    act_b, slope_b = gelu(pre(pool_b, weight_b, bias_b))
    (s00, s01), (s10, s11) = stitch[0], stitch[1]
    mixed_a = (row * (s00 * act_a + s01 * act_b)).astype(BF16)
    mixed_b = (row * (s10 * act_a + s11 * act_b)).astype(BF16)
    gy_a = row * outgrad_a.astype(F32)
    gy_b = row * outgrad_b.astype(F32)
    gpre_a = ((s00 * gy_a + s10 * gy_b) * slope_a).astype(BF16)
    gpre_b = ((s01 * gy_a + s11 * gy_b) * slope_b).astype(BF16)
    sums = jnp.stack(
        [
            jnp.sum(v, axis=0)
            for v in (
                gy_a * act_a,
                gy_a * act_b,
                gy_b * act_a,
                gy_b * act_b,
                gpre_a.astype(F32),
                gpre_b.astype(F32),
            )
        ]
    )
    sums = lax.psum_scatter(sums, "rows", scatter_dimension=1, tiled=True)

    def back(pool, weight, gpre):
        whole = lax.all_gather(gpre, "feat", axis=1, tiled=True)
        pool_grad = dot_t(whole, weight).astype(BF16)
        wgrad = lax.dot_general(pool, whole, (((0,), (0,)), ((), ())), preferred_element_type=F32)
        wgrad = lax.psum_scatter(wgrad.astype(BF16), "rows", scatter_dimension=1, tiled=True)
        return pool_grad, wgrad.astype(F32)

    pg_a, wg_a = back(pool_a, weight_a, gpre_a)
    pg_b, wg_b = back(pool_b, weight_b, gpre_b)
    return mixed_a, mixed_b, pg_a, pg_b, wg_a, wg_b, sums[4], sums[5], sums[:4].reshape(2, 2, -1)


def shards(
    pool_a, pool_b, weight_a, weight_b, bias_a, bias_b, stitch, crop_count, row_mask, outgrad_a, outgrad_b
):
    row_scale = row_mask.astype(F32) / crop_count.astype(F32)
    rows, width = pool_a.shape
    chl = bias_a.shape[0]
    n_rows, n_feat = lax.axis_size("rows"), lax.axis_size("feat")
    fits = (
        n_rows == 4
        and n_feat == 8
        and chl == n_rows * LANE
        and width % LANE == 0
        and rows % (ROW_BLOCKS * LANE) == 0
    )
    run = functools.partial(fused, n_feat // 2) if fits else plain
    return run(pool_a, pool_b, weight_a, weight_b, bias_a, bias_b, stitch, row_scale, outgrad_a, outgrad_b)


def solution(mesh):
    return jax.shard_map(
        shards,
        mesh=mesh,
        in_specs=(
            P("rows", "feat"),
            P("rows", "feat"),
            P("feat", None),
            P("feat", None),
            P("feat"),
            P("feat"),
            P(None, None, "feat"),
            P("rows"),
            P("rows"),
            P("rows", "feat"),
            P("rows", "feat"),
        ),
        out_specs=(
            P("rows", "feat"),
            P("rows", "feat"),
            P("rows", "feat"),
            P("rows", "feat"),
            P("feat", "rows"),
            P("feat", "rows"),
            P(("feat", "rows")),
            P(("feat", "rows")),
            P(None, None, ("feat", "rows")),
        ),
        check_vma=False,
    )
```

```python
import functools

import jax
import jax.numpy as jnp
from jax import lax
from jax.experimental import pallas as pl
from jax.experimental.pallas import tpu as pltpu
from jax.sharding import PartitionSpec as P

MESH = pl.DeviceIdType.MESH
F32 = jnp.float32
BF16 = jnp.bfloat16
LANE = 128
ROW_BLOCKS = 2
SUBS = 5
PIECES = 4
RIGHT, LEFT = 0, 1
FAR, NEAR, KEEP, OWN = 0, 1, 2, 3
SIB, MINE = 0, 1
INV_SQRT2 = 0.7071067811865476
INV_SQRT_2PI = 0.3989422804014327


def dot(lhs, rhs):
    return lax.dot_general(lhs, rhs, (((1,), (0,)), ((), ())), preferred_element_type=F32)


def dot_t(lhs, rhs):
    return lax.dot_general(lhs, rhs, (((1,), (1,)), ((), ())), preferred_element_type=F32)


def kernel(rows, width, chl, *refs):
    (
        pool_a, pool_b, weight_a, weight_b, par, scale, og_a, og_b,
        mixed_a, mixed_b, pg_a, pg_b, wg_a, wg_b, stats,
        pool_v, pool_t, wf, wb, part_sib, part_own, xr, rbuf, gath, acc, wsend, wrecv, wout,
        og_v, mix_v, pg_v, sacc, sred, srecv,
        pool_s, wf_s, wb_s, xs_send, xs_recv, z_send, z_recv, g_send, g_recv,
        w_send, w_recv, wout_s, og_s, mix_s, pg_s, st_send, st_recv, credit, wcredit,
    ) = refs
    L = 4
    NB, NS = ROW_BLOCKS, SUBS
    RB = rows // NB
    SB = RB // NS
    PB = rows // PIECES
    NCH = chl // LANE
    U = NCH * NB
    SENDING = U + 2
    TICKS = (U + 2 + NB) * L
    pools, weights = (pool_a, pool_b), (weight_a, weight_b)
    ogs, mixeds = (og_a, og_b), (mixed_a, mixed_b)
    pgs, wgs = (pg_a, pg_b), (wg_a, wg_b)

    f = lax.axis_index("feat")
    r = lax.axis_index("rows")
    p = lax.div(f, 2)
    c = lax.rem(f, 2)
    sib = f + 1 - 2 * c
    xp = r + 1 - 2 * lax.rem(r, 2)
    yp = lax.rem(r + 2, 4)
    dp = 3 - r
    has_left, has_right = p > 0, p < L - 1
    pos = (p, L - 1 - p)
    nxt = (f + 2, f - 2)

    def remote(src, dst, send, recv, **dev):
        return pltpu.make_async_remote_copy(
            src_ref=src, dst_ref=dst, send_sem=send, recv_sem=recv, device_id=dev, device_id_type=MESH
        )

    def signal(sem, **dev):
        pl.semaphore_signal(sem, inc=1, device_id=dev, device_id_type=MESH)

    def lanes(index):
        return pl.ds(pl.multiple_of(index * LANE, LANE), LANE)

    def block_rows(i):
        return pl.ds(pl.multiple_of(i * RB, RB), RB)

    def sub_rows(b):
        return pl.ds(b * SB, SB)

    def here_rows(u, b):
        return pl.ds(pl.multiple_of(lax.rem(u, NB) * RB + b * SB, SB), SB)

    def pool_load(tick, t):
        slot = lax.rem(tick, 2)
        rows_of = block_rows(lax.rem(lax.div(tick, L), NB))
        return pltpu.make_async_copy(pools[t].at[rows_of, :], pool_v.at[slot], pool_s.at[slot])

    def wf_loads(tick, t):
        j = lax.div(tick, L * NB)
        slot = lax.rem(tick, 2)
        core = jnp.where(lax.rem(tick, L) < 2, 1 - c, c)
        return [
            pltpu.make_async_copy(
                weights[t].at[:, lanes((2 * q + core) * NCH + j)],
                wf.at[slot, :, q * LANE : (q + 1) * LANE],
                wf_s.at[slot, q],
            )
            for q in range(L)
        ]

    def tower_of(index, start):
        for t in range(2):

            @pl.when(lax.rem(index, 2) == t)
            def _():
                start(t)

    def wb_loads(j, t):
        out = []
        for q in range(L):
            for k in range(2):
                out.append(
                    pltpu.make_async_copy(
                        weights[t].at[:, lanes((2 * q + k) * NCH + j)],
                        wb.at[q, :, k * LANE : (k + 1) * LANE],
                        wb_s.at[q, k],
                    )
                )
        return out

    def start_all(copies):
        for copy in copies:
            copy.start()

    def wait_all(copies):
        for copy in copies:
            copy.wait()

    def og_load(u, t):
        slot = lax.rem(u, 2)
        return pltpu.make_async_copy(
            ogs[t].at[block_rows(lax.rem(u, NB)), lanes(lax.div(u, NB))], og_v.at[slot, t], og_s.at[slot, t]
        )

    def mix_store(u, b, t):
        return pltpu.make_async_copy(
            mix_v.at[b, t], mixeds[t].at[here_rows(u, b), lanes(lax.div(u, NB))], mix_s.at[b, t]
        )

    def part_copy(u, t, par2):
        return remote(part_sib.at[t], xr.at[lax.rem(u, 3), t], xs_send.at[t], xs_recv.at[t, par2], feat=sib)

    def share_copy(u, o, core, d, b, s, par2):
        block = gath.at[lax.rem(lax.div(u, NB), 2), o, core, here_rows(u, b), :]
        return remote(block, block, g_send.at[d, b, s], g_recv.at[d, b, s, par2], feat=sib)

    def gath_copy(u, o, d, b, s, par2):
        block = gath.at[lax.rem(lax.div(u, NB), 2), o, c, here_rows(u, b), :]
        return remote(block, block, z_send.at[d, b, s], z_recv.at[d, b, s, par2], feat=nxt[d])

    def sum_copy(u, d, b, s, par2):
        u2 = lax.rem(u, 2)
        return remote(
            rbuf.at[u2, d, s - 1, sub_rows(b), :],
            rbuf.at[u2, d, s, sub_rows(b), :],
            z_send.at[d, b, s],
            z_recv.at[d, b, s, par2],
            feat=nxt[d],
        )

    def sum_wait(u, d, b, s, par2):
        block = rbuf.at[lax.rem(u, 2), d, s, sub_rows(b), :]
        remote(block, block, z_send.at[d, b, s], z_recv.at[d, b, s, par2], feat=nxt[d]).wait_recv()

    def own_sum(u, t, o, b):
        mine = part_own[lax.rem(u, 2), t, o, sub_rows(b), :].astype(F32)
        return mine + xr[lax.rem(u, 3), t, o, sub_rows(b), :].astype(F32)

    def fold(v):
        return jnp.sum(v.reshape(SB // 8, 8, LANE), axis=0)

    def finalize(u, b, per):
        j = lax.div(u, NB)
        last2 = lax.rem(per - 1, 2)

        @pl.when(has_left)
        def _():
            sum_wait(u, RIGHT, b, L - 1, last2)

        @pl.when(has_right)
        def _():
            sum_wait(u, LEFT, b, L - 1, last2)

        if b == 0:
            wait_all([og_load(u, 0), og_load(u, 1)])

        @pl.when(u >= 1)
        def _():
            wait_all([mix_store(u, b, 0), mix_store(u, b, 1)])

        u2 = lax.rem(u, 2)
        ch = lanes(j)
        s00, s01, s10, s11 = (par[k : k + 1, ch] for k in range(4))
        here = here_rows(u, b)
        row = scale[here, :]
        gy_a = row * og_v[u2, 0, sub_rows(b), :].astype(F32)
        gy_b = row * og_v[u2, 1, sub_rows(b), :].astype(F32)

        def gelu(t):
            v = own_sum(u, t, p, b) + par[4 + t : 5 + t, ch]
            for d in (RIGHT, LEFT):
                v = v + rbuf[u2, d, L - 1, sub_rows(b), t * LANE : (t + 1) * LANE].astype(F32)
            cdf = 0.5 * (1.0 + lax.erf(v * INV_SQRT2))
            return v * cdf, cdf + v * (INV_SQRT_2PI * jnp.exp(-0.5 * v * v))

        act_a, slope_a = gelu(0)
        act_b, slope_b = gelu(1)
        mix_v[b, 0] = (row * (s00 * act_a + s01 * act_b)).astype(BF16)
        mix_v[b, 1] = (row * (s10 * act_a + s11 * act_b)).astype(BF16)
        start_all([mix_store(u, b, 0), mix_store(u, b, 1)])
        gpre_a = ((s00 * gy_a + s10 * gy_b) * slope_a).astype(BF16)
        gpre_b = ((s01 * gy_a + s11 * gy_b) * slope_b).astype(BF16)
        gath[lax.rem(j, 2), p, c, here, :LANE] = gpre_a
        gath[lax.rem(j, 2), p, c, here, LANE:] = gpre_b
        sacc[j, 0] += fold(gy_a * act_a)
        sacc[j, 1] += fold(gy_a * act_b)
        sacc[j, 2] += fold(gy_b * act_a)
        sacc[j, 3] += fold(gy_b * act_b)
        sacc[j, 4] += fold(gpre_a.astype(F32))
        sacc[j, 5] += fold(gpre_b.astype(F32))

    first_partner, second_partner = (xp, yp), (yp, xp)

    def w_copy(t, kind):
        return remote(
            wsend.at[t, kind],
            wrecv.at[t, kind],
            w_send.at[t, kind],
            w_recv.at[t, kind],
            rows=second_partner[t] if kind == KEEP else first_partner[t],
        )

    def wout_stores(j, t):
        return [
            pltpu.make_async_copy(
                wout.at[t, :, k * LANE : (k + 1) * LANE], wgs[t].at[:, lanes(k * NCH + j)], wout_s.at[t, k]
            )
            for k in range(2)
        ]

    def pg_store(t, i, slot):
        dst = pl.ds(pl.multiple_of(i * PB, PB), PB)
        return pltpu.make_async_copy(pg_v.at[slot], pgs[t].at[dst, :], pg_s.at[slot])

    pool_load(0, 0).start()
    start_all(wf_loads(0, 0))

    bar = pltpu.get_barrier_semaphore()

    @pl.when(has_left)
    def _():
        signal(bar, feat=f - 2)

    @pl.when(has_right)
    def _():
        signal(bar, feat=f + 2)

    signal(bar, feat=sib)
    signal(bar, rows=xp)
    signal(bar, rows=yp)
    signal(bar, rows=dp)
    sacc[...] = jnp.zeros_like(sacc)

    @pl.when(jnp.logical_not(has_left))
    def _():
        for k in range(2):
            rbuf[k, RIGHT, L - 1] = jnp.zeros((RB, 2 * LANE), BF16)

    @pl.when(jnp.logical_not(has_right))
    def _():
        for k in range(2):
            rbuf[k, LEFT, L - 1] = jnp.zeros((RB, 2 * LANE), BF16)

    pl.semaphore_wait(bar, 4 + has_left.astype(jnp.int32) + has_right.astype(jnp.int32))

    def tick(T, carry):
        per, s = lax.div(T, L), lax.rem(T, L)
        par2 = lax.rem(per, 2)
        u = per - 2
        ur = per - 1
        uf = per
        gathers = (u >= 0) & (u < U)
        sums = (ur >= 0) & (ur < U)

        @pl.when((s == 0) & (per >= 1) & (per < SENDING))
        def _():
            @pl.when(has_left)
            def _():
                pl.semaphore_wait(credit.at[0], 1)

            @pl.when(has_right)
            def _():
                pl.semaphore_wait(credit.at[1], 1)

            pl.semaphore_wait(credit.at[2], 1)

        @pl.when((s == 1) & sums)
        def _():
            for t in range(2):
                part_copy(ur, t, lax.rem(per - 1, 2)).wait_recv()
            start_all([og_load(ur, 0), og_load(ur, 1)])

        for b in range(NS):

            @pl.when((s == 0) & gathers)
            def _():
                finalize(u, b, per)

            for d in (RIGHT, LEFT):
                gather_here = pos[d] >= s
                o = p - s if d == RIGHT else p + s
                dest = p + (L - s) if d == RIGHT else p - (L - s)
                shares = (s >= 1) if d == LEFT else (s >= 0)

                @pl.when(gathers & gather_here)
                def _():
                    @pl.when(s >= 1)
                    def _():
                        gath_copy(u, o, d, b, s - 1, par2).wait_recv()

                    @pl.when(pos[d] < L - 1)
                    def _():
                        gath_copy(u, o, d, b, s, par2).start()

                    @pl.when(shares)
                    def _():
                        share_copy(u, o, c, d, b, s, par2).start()

                @pl.when(sums & jnp.logical_not(gather_here))
                def _():
                    u2 = lax.rem(ur, 2)

                    @pl.when(pos[d] >= 1)
                    def _():
                        sum_wait(ur, d, b, s - 1, par2)
                        for t in range(2):
                            half = slice(t * LANE, (t + 1) * LANE)
                            both = own_sum(ur, t, dest, b) + rbuf[u2, d, s - 1, sub_rows(b), half].astype(F32)
                            rbuf[u2, d, s - 1, sub_rows(b), half] = both.astype(BF16)

                    @pl.when(pos[d] < 1)
                    def _():
                        for t in range(2):
                            half = slice(t * LANE, (t + 1) * LANE)
                            rbuf[u2, d, s - 1, sub_rows(b), half] = own_sum(ur, t, dest, b).astype(BF16)

                    sum_copy(ur, d, b, s, par2).start()

        @pl.when(uf < U)
        def _():
            pool_load(T, 0).wait()
            wait_all(wf_loads(T, 0))

            @pl.when(T + 1 < U * L)
            def _():
                def load(t):
                    pool_load(T + 1, t).start()
                    start_all(wf_loads(T + 1, t))

                tower_of(T + 1, load)

            t = lax.rem(s, 2)
            res = dot(pool_v[lax.rem(T, 2)], wf[lax.rem(T, 2)]).astype(BF16)

            @pl.when(s < 2)
            def _():
                for q in range(L):
                    part_sib[t, q] = res[:, q * LANE : (q + 1) * LANE]
                part_copy(uf, t, par2).start()

            @pl.when(s >= 2)
            def _():
                for q in range(L):
                    part_own[lax.rem(uf, 2), t, q] = res[:, q * LANE : (q + 1) * LANE]

            @pl.when((uf < NB) & (s >= 2))
            def _():
                pool_t[t, :, block_rows(uf)] = pool_v[lax.rem(T, 2)].T

        since = jnp.maximum(T - 2 * L, 0)
        jb = lax.div(since, NB * L) - 1
        tau = lax.rem(since, NB * L)
        jb2 = lax.rem(jb, 2)

        before = T - 1 + L
        per_m, s_m = lax.div(before, L) - 1, lax.rem(before, L)
        par_m = lax.rem(per_m + 2, 2)
        u_m, ur_m = per_m - 2, per_m - 1
        gathers_m = (u_m >= 0) & (u_m < U)
        sums_m = (ur_m >= 0) & (ur_m < U)
        for b in range(NS):
            for d in (RIGHT, LEFT):
                o = p - s_m if d == RIGHT else p + s_m
                shares = (s_m >= 1) if d == LEFT else (s_m >= 0)

                @pl.when(gathers_m & (pos[d] >= s_m) & shares)
                def _():
                    share_copy(u_m, o, 1 - c, d, b, s_m, par_m).wait_recv()

        @pl.when(jb >= 0)
        def _():
            @pl.when((tau == 0) & (jb >= 1))
            def _():
                for k in range(2):
                    pl.semaphore_wait(wcredit.at[0, k], 1)

            @pl.when((tau == 1) & (jb >= 1))
            def _():
                for k in range(2):
                    pl.semaphore_wait(wcredit.at[1, k], 1)

            @pl.when(tau == 3)
            def _():
                start_all(wb_loads(jb, 0))

            @pl.when(tau < 4)
            def _():
                for t in range(2):
                    one, two = first_partner[t], second_partner[t]
                    owner = jnp.where(
                        tau == FAR, dp, jnp.where(tau == NEAR, one, jnp.where(tau == KEEP, two, r))
                    )
                    cols = [gath[jb2, owner, k, :, t * LANE : (t + 1) * LANE] for k in range(2)]
                    cols = jnp.concatenate(cols, axis=1)
                    wsend[t, tau] = dot(pool_t[t], cols).astype(BF16)
                    for way in (FAR, NEAR):

                        @pl.when(tau == way)
                        def _():
                            w_copy(t, way).start()

            @pl.when(tau == 4)
            def _():
                for t in range(2):
                    w_copy(t, FAR).wait_recv()
                    both = wsend[t, KEEP].astype(F32) + wrecv[t, FAR].astype(F32)
                    wsend[t, KEEP] = both.astype(BF16)
                    w_copy(t, KEEP).start()

                @pl.when(jb < NCH - 1)
                def _():
                    signal(wcredit.at[0, 0], rows=xp)
                    signal(wcredit.at[0, 1], rows=yp)

            @pl.when(tau >= 4)
            def _():
                t = lax.rem(tau, 2)
                wait_all(wb_loads(jb, 0))
                for k in range(2):
                    i = 2 * lax.div(tau - 4, 2) + k
                    mine = pl.ds(pl.multiple_of(i * PB, PB), PB)
                    total = None
                    for q in range(L):
                        cols = [gath[jb2, q, core, mine, lanes(t)] for core in range(2)]
                        term = dot_t(jnp.concatenate(cols, axis=1), wb[q])
                        total = term if total is None else total + term

                    @pl.when(jb == 0)
                    def _():
                        acc[t, mine, :] = total

                    @pl.when((jb > 0) & (jb < NCH - 1))
                    def _():
                        acc[t, mine, :] += total

                    @pl.when(jb == NCH - 1)
                    def _():
                        @pl.when(tau >= 5)
                        def _():
                            pg_store(0, 0, k).wait()

                        pg_v[k] = (acc[t, mine, :] + total).astype(BF16)

                        def store(tt):
                            pg_store(tt, i, k).start()

                        tower_of(tau, store)

                @pl.when(tau < 7)
                def _():
                    tower_of(tau + 1, lambda tt: start_all(wb_loads(jb, tt)))

            @pl.when(tau == 7)
            def _():
                for t in range(2):
                    w_copy(t, NEAR).wait_recv()
                    w_copy(t, KEEP).wait_recv()
                    for kind in (FAR, NEAR, KEEP):
                        w_copy(t, kind).wait_send()

                    @pl.when(jb >= 1)
                    def _():
                        wait_all(wout_stores(jb, t))

                    both = wsend[t, OWN].astype(F32) + wrecv[t, NEAR].astype(F32)
                    wout[t] = both + wrecv[t, KEEP].astype(F32)
                    start_all(wout_stores(jb, t))

                @pl.when(jb < NCH - 1)
                def _():
                    signal(wcredit.at[1, 0], rows=xp)
                    signal(wcredit.at[1, 1], rows=yp)

        @pl.when((per_m >= 0) & (per_m < U) & (s_m < 2))
        def _():
            part_copy(per_m, lax.rem(s_m, 2), par_m).wait_send()

        for b in range(NS):
            for d in (RIGHT, LEFT):
                shares = (s_m >= 1) if d == LEFT else (s_m >= 0)

                @pl.when(gathers_m & (pos[d] >= s_m))
                def _():
                    @pl.when(pos[d] < L - 1)
                    def _():
                        gath_copy(u_m, p, d, b, s_m, par_m).wait_send()

                    @pl.when(shares)
                    def _():
                        share_copy(u_m, p, c, d, b, s_m, par_m).wait_send()

                @pl.when(sums_m & (pos[d] < s_m))
                def _():
                    sum_copy(ur_m, d, b, s_m, par_m).wait_send()

        @pl.when((s == 1) & (per < SENDING - 1))
        def _():
            @pl.when(has_left)
            def _():
                signal(credit.at[1], feat=f - 2)

            @pl.when(has_right)
            def _():
                signal(credit.at[0], feat=f + 2)

            signal(credit.at[2], feat=sib)

        @pl.when(T == (U + 1) * L + 1)
        def _():
            for j in range(NCH):
                for k in range(6):
                    sred[j, k : k + 1, :] = jnp.sum(sacc[j, k], axis=0, keepdims=True)
                sred[j, 6:8, :] = jnp.zeros((2, LANE), F32)
            for k, peer in enumerate((xp, yp, dp)):
                remote(sred.at[peer], srecv.at[k], st_send.at[k], st_recv.at[k], rows=peer).start()

        return carry

    lax.fori_loop(0, TICKS, tick, 0)

    for k, peer in enumerate((xp, yp, dp)):
        copy = remote(sred.at[peer], srecv.at[k], st_send.at[k], st_recv.at[k], rows=peer)
        copy.wait_send()
        copy.wait_recv()
    stats[...] = sred[r] + srecv[0] + srecv[1] + srecv[2]
    for t in range(2):
        for b in range(NS):
            mix_store(U - 1, b, t).wait()
        wait_all(wout_stores(NCH - 1, t))
        pg_store(0, 0, t).wait()


def fused(pool_a, pool_b, weight_a, weight_b, bias_a, bias_b, stitch, row_scale, outgrad_a, outgrad_b):
    rows, width = pool_a.shape
    chl = bias_a.shape[0]
    NB, NS, L = ROW_BLOCKS, SUBS, 4
    RB = rows // NB
    SB = RB // NS
    NCH = chl // LANE
    par = jnp.concatenate([stitch.reshape(4, chl), bias_a[None], bias_b[None], jnp.zeros((2, chl), F32)], axis=0)
    hbm = pl.BlockSpec(memory_space=pl.ANY)
    vmem = pl.BlockSpec(memory_space=pltpu.VMEM)
    dma = pltpu.SemaphoreType.DMA
    out_shape = (
        jax.ShapeDtypeStruct((rows, chl), BF16),
        jax.ShapeDtypeStruct((rows, chl), BF16),
        jax.ShapeDtypeStruct((rows, width), BF16),
        jax.ShapeDtypeStruct((rows, width), BF16),
        jax.ShapeDtypeStruct((width, 2 * chl), F32),
        jax.ShapeDtypeStruct((width, 2 * chl), F32),
        jax.ShapeDtypeStruct((8, LANE), F32),
    )
    scratch = [
        pltpu.VMEM((2, RB, width), BF16),
        pltpu.VMEM((2, width, rows), BF16),
        pltpu.VMEM((2, width, L * LANE), BF16),
        pltpu.VMEM((L, width, 2 * LANE), BF16),
        pltpu.VMEM((2, L, RB, LANE), BF16),
        pltpu.VMEM((2, 2, L, RB, LANE), BF16),
        pltpu.VMEM((3, 2, L, RB, LANE), BF16),
        pltpu.VMEM((2, 2, L, RB, 2 * LANE), BF16),
        pltpu.VMEM((2, L, 2, rows, 2 * LANE), BF16),
        pltpu.VMEM((2, rows, width), F32),
        pltpu.VMEM((2, 4, width, 2 * LANE), BF16),
        pltpu.VMEM((2, 3, width, 2 * LANE), BF16),
        pltpu.VMEM((2, width, 2 * LANE), F32),
        pltpu.VMEM((2, 2, RB, LANE), BF16),
        pltpu.VMEM((NS, 2, SB, LANE), BF16),
        pltpu.VMEM((2, rows // PIECES, width), BF16),
        pltpu.VMEM((NCH, 6, 8, LANE), F32),
        pltpu.VMEM((NCH, 8, LANE), F32),
        pltpu.VMEM((3, 8, LANE), F32),
        dma((2,)),
        dma((2, L)),
        dma((L, 2)),
        dma((2,)),
        dma((2, 2)),
        dma((2, NS, L)),
        dma((2, NS, L, 2)),
        dma((2, NS, L)),
        dma((2, NS, L, 2)),
        dma((2, 3)),
        dma((2, 3)),
        dma((2, 2)),
        dma((2, 2)),
        dma((NS, 2)),
        dma((2,)),
        dma((3,)),
        dma((3,)),
        pltpu.SemaphoreType.REGULAR((3,)),
        pltpu.SemaphoreType.REGULAR((2, 2)),
    ]
    mixed_a, mixed_b, pg_a, pg_b, wg_a, wg_b, stats = pl.pallas_call(
        functools.partial(kernel, rows, width, chl),
        out_shape=out_shape,
        in_specs=[hbm, hbm, hbm, hbm, vmem, vmem, hbm, hbm],
        out_specs=(hbm, hbm, hbm, hbm, hbm, hbm, vmem),
        scratch_shapes=scratch,
        compiler_params=pltpu.CompilerParams(
            collective_id=0, has_side_effects=True, vmem_limit_bytes=VMEM_LIMIT
        ),
    )(pool_a, pool_b, weight_a, weight_b, par, row_scale[:, None], outgrad_a, outgrad_b)
    return mixed_a, mixed_b, pg_a, pg_b, wg_a, wg_b, stats[4], stats[5], stats[:4].reshape(2, 2, LANE)


VMEM_LIMIT = 63 * 1024 * 1024


def plain(pool_a, pool_b, weight_a, weight_b, bias_a, bias_b, stitch, row_scale, outgrad_a, outgrad_b):
    row = row_scale[:, None]

    def pre(pool, weight, bias):
        partial = dot(pool, weight).astype(BF16)
        return lax.psum_scatter(partial, "feat", scatter_dimension=1, tiled=True).astype(F32) + bias

    def gelu(v):
        cdf = 0.5 * (1.0 + lax.erf(v * INV_SQRT2))
        return v * cdf, cdf + v * (INV_SQRT_2PI * jnp.exp(-0.5 * v * v))

    act_a, slope_a = gelu(pre(pool_a, weight_a, bias_a))
    act_b, slope_b = gelu(pre(pool_b, weight_b, bias_b))
    (s00, s01), (s10, s11) = stitch[0], stitch[1]
    mixed_a = (row * (s00 * act_a + s01 * act_b)).astype(BF16)
    mixed_b = (row * (s10 * act_a + s11 * act_b)).astype(BF16)
    gy_a = row * outgrad_a.astype(F32)
    gy_b = row * outgrad_b.astype(F32)
    gpre_a = ((s00 * gy_a + s10 * gy_b) * slope_a).astype(BF16)
    gpre_b = ((s01 * gy_a + s11 * gy_b) * slope_b).astype(BF16)
    sums = jnp.stack(
        [
            jnp.sum(v, axis=0)
            for v in (
                gy_a * act_a,
                gy_a * act_b,
                gy_b * act_a,
                gy_b * act_b,
                gpre_a.astype(F32),
                gpre_b.astype(F32),
            )
        ]
    )
    sums = lax.psum_scatter(sums, "rows", scatter_dimension=1, tiled=True)

    def back(pool, weight, gpre):
        whole = lax.all_gather(gpre, "feat", axis=1, tiled=True)
        pool_grad = dot_t(whole, weight).astype(BF16)
        wgrad = lax.dot_general(pool, whole, (((0,), (0,)), ((), ())), preferred_element_type=F32)
        wgrad = lax.psum_scatter(wgrad.astype(BF16), "rows", scatter_dimension=1, tiled=True)
        return pool_grad, wgrad.astype(F32)

    pg_a, wg_a = back(pool_a, weight_a, gpre_a)
    pg_b, wg_b = back(pool_b, weight_b, gpre_b)
    return mixed_a, mixed_b, pg_a, pg_b, wg_a, wg_b, sums[4], sums[5], sums[:4].reshape(2, 2, -1)


def shards(
    pool_a, pool_b, weight_a, weight_b, bias_a, bias_b, stitch, crop_count, row_mask, outgrad_a, outgrad_b
):
    row_scale = row_mask.astype(F32) / crop_count.astype(F32)
    rows, width = pool_a.shape
    chl = bias_a.shape[0]
    n_rows, n_feat = lax.axis_size("rows"), lax.axis_size("feat")
    fits = (
        n_rows == 4
        and n_feat == 8
        and chl == n_rows * LANE
        and width % LANE == 0
        and rows % (ROW_BLOCKS * SUBS * LANE) == 0
    )
    run = fused if fits else plain
    return run(pool_a, pool_b, weight_a, weight_b, bias_a, bias_b, stitch, row_scale, outgrad_a, outgrad_b)


def solution(mesh):
    return jax.shard_map(
        shards,
        mesh=mesh,
        in_specs=(
            P("rows", "feat"),
            P("rows", "feat"),
            P("feat", None),
            P("feat", None),
            P("feat"),
            P("feat"),
            P(None, None, "feat"),
            P("rows"),
            P("rows"),
            P("rows", "feat"),
            P("rows", "feat"),
        ),
        out_specs=(
            P("rows", "feat"),
            P("rows", "feat"),
            P("rows", "feat"),
            P("rows", "feat"),
            P("feat", "rows"),
            P("feat", "rows"),
            P(("feat", "rows")),
            P(("feat", "rows")),
            P(None, None, ("feat", "rows")),
        ),
        check_vma=False,
    )
```

```python
import functools

import jax
import jax.numpy as jnp
from jax import lax
from jax.experimental import pallas as pl
from jax.experimental.pallas import tpu as pltpu
from jax.sharding import PartitionSpec as P

MESH = pl.DeviceIdType.MESH
F32 = jnp.float32
BF16 = jnp.bfloat16
LANE = 128
HALF = 64
SUBS = 5
PIECES = 4
RIGHT, LEFT = 0, 1
FAR, NEAR, KEEP, OWN = 0, 1, 2, 3
INV_SQRT2 = 0.7071067811865476
INV_SQRT_2PI = 0.3989422804014327


def dot(lhs, rhs):
    return lax.dot_general(lhs, rhs, (((1,), (0,)), ((), ())), preferred_element_type=F32)


def dot_t(lhs, rhs):
    return lax.dot_general(lhs, rhs, (((1,), (1,)), ((), ())), preferred_element_type=F32)


def swap(v):
    return pltpu.roll(v, HALF, 1)


def upper(rows):
    return lax.broadcasted_iota(jnp.int32, (rows, LANE), 1) >= HALF


def halves(one, two, half):
    if half == 0:
        return jnp.where(upper(one.shape[0]), swap(two), one)
    return jnp.where(upper(one.shape[0]), two, swap(one))


def kernel(rows, width, chl, *refs):
    (
        pool_a, pool_b, weight_a, weight_b, bias_a, bias_b, stitch, mask, count, og_a, og_b,
        mixed_a, mixed_b, pg_a, pg_b, wg_a, wg_b, stats,
        pool_v, pool_t, wf, wb, part_sib, part_own, xr, rbuf, gath, acc, wsend, wkeep, wrecv, wout,
        og_v, scale, par, mix_0, mix_v, sacc, sred, srecv,
        pool_s, wf_s, wb_s, xs_send, xs_recv, z_send, z_recv, g_send, g_recv,
        w_send, w_recv, wout_s, og_s, mix_s, pg_s, st_send, st_recv, credit, wcredit,
    ) = refs
    L = 4
    NS = SUBS
    SB = rows // NS
    HB = rows // 2
    PB = rows // PIECES
    NCH = chl // LANE
    U = 2 * NCH
    SENDING = U + 3
    TICKS = (U + 5) * L
    pools, weights = (pool_a, pool_b), (weight_a, weight_b)
    ogs, mixeds = (og_a, og_b), (mixed_a, mixed_b)
    pgs, wgs = (pg_a, pg_b), (wg_a, wg_b)

    f = lax.axis_index("feat")
    r = lax.axis_index("rows")
    p = lax.div(f, 2)
    c = lax.rem(f, 2)
    sib = f + 1 - 2 * c
    xp = r + 1 - 2 * lax.rem(r, 2)
    yp = lax.rem(r + 2, 4)
    dp = 3 - r
    has_left, has_right = p > 0, p < L - 1
    pos = (p, L - 1 - p)
    has_up = (has_left, has_right)
    nxt = (f + 2, f - 2)

    def remote(src, dst, send, recv, **dev):
        return pltpu.make_async_remote_copy(
            src_ref=src, dst_ref=dst, send_sem=send, recv_sem=recv, device_id=dev, device_id_type=MESH
        )

    def signal(sem, **dev):
        pl.semaphore_signal(sem, inc=1, device_id=dev, device_id_type=MESH)

    def start_all(copies):
        for copy in copies:
            copy.start()

    def wait_all(copies):
        for copy in copies:
            copy.wait()

    def lanes(index):
        return pl.ds(pl.multiple_of(index * LANE, LANE), LANE)

    def some_rows(i, n):
        return pl.ds(pl.multiple_of(i * n, n), n)

    def sub_rows(b):
        return pl.ds(b * SB, SB)

    def tower_of(index, run):
        for t in range(2):

            @pl.when(lax.rem(index, 2) == t)
            def _():
                run(t)

    def pool_load(tick, t):
        slot = lax.rem(tick, 2)
        half = lax.div(lax.rem(tick, L), 2)
        return pltpu.make_async_copy(pools[t].at[some_rows(half, HB), :], pool_v.at[slot], pool_s.at[slot])

    def wf_loads(tick, t):
        j = lax.div(tick, 2 * L)
        slot = lax.rem(tick, 2)
        core = jnp.where(lax.rem(lax.div(tick, L), 2) == 0, c, 1 - c)
        return [
            pltpu.make_async_copy(
                weights[t].at[:, lanes((2 * q + core) * NCH + j)],
                wf.at[slot, :, q * LANE : (q + 1) * LANE],
                wf_s.at[slot, q],
            )
            for q in range(L)
        ]

    def wb_loads(j, t):
        out = []
        for q in range(L):
            for k in range(2):
                out.append(
                    pltpu.make_async_copy(
                        weights[t].at[:, lanes((2 * q + k) * NCH + j)],
                        wb.at[q, :, k * LANE : (k + 1) * LANE],
                        wb_s.at[q, k],
                    )
                )
        return out

    def og_loads(j):
        return [pltpu.make_async_copy(ogs[t].at[:, lanes(j)], og_v.at[t], og_s.at[t]) for t in range(2)]

    def mix_stores(j, b):
        return [
            pltpu.make_async_copy(mix_v.at[b % 2, t], mixeds[t].at[sub_rows(b), lanes(j)], mix_s.at[b % 2, t])
            for t in range(2)
        ]

    def part_copy(j, s, slot):
        t, half = lax.rem(s, 2), lax.div(s, 2)
        return remote(
            part_sib.at[slot],
            xr.at[lax.rem(j, 2), t, :, some_rows(half, HB), :],
            xs_send.at[s],
            xs_recv.at[s],
            feat=sib,
        )

    def share_copy(u, o, core, d, b, s, par2):
        block = gath.at[lax.rem(u, 4), o, core, sub_rows(b), :]
        return remote(block, block, g_send.at[d, b, s], g_recv.at[d, b, s, par2], feat=sib)

    def gath_copy(u, o, d, b, s, par2):
        block = gath.at[lax.rem(u, 4), o, c, sub_rows(b), :]
        return remote(block, block, z_send.at[d, b, s], z_recv.at[d, b, s, par2], feat=nxt[d])

    def sum_block(u, d, b, s):
        return rbuf.at[lax.rem(u, 2), d, lax.rem(s, 3), sub_rows(b), :]

    def sum_copy(u, d, b, s, par2):
        return remote(
            sum_block(u, d, b, s - 1),
            sum_block(u, d, b, s),
            z_send.at[d, b, s],
            z_recv.at[d, b, s, par2],
            feat=nxt[d],
        )

    def sum_wait(u, d, b, s, par2):
        block = sum_block(u, d, b, s)
        remote(block, block, z_send.at[d, b, s], z_recv.at[d, b, s, par2], feat=nxt[d]).wait_recv()

    def packed(one, two, h):
        return jnp.where(upper(one.shape[0]) == (h == 1), one, swap(two))

    def own_sum(u, o, b):
        j, h = lax.div(u, 2), lax.rem(u, 2)
        j2 = lax.rem(j, 2)

        def tower(t):
            return part_own[j2, t, o, sub_rows(b), :].astype(F32) + xr[j2, t, o, sub_rows(b), :].astype(F32)

        return packed(tower(h), tower(1 - h), h)

    def fold(v):
        return jnp.sum(v.reshape(SB // 8, 8, LANE), axis=0)

    def finalize(u, b, per):
        j, h = lax.div(u, 2), lax.rem(u, 2)
        last2 = lax.rem(per - 1, 2)
        for d in (RIGHT, LEFT):

            @pl.when(has_up[d])
            def _():
                sum_wait(u, d, b, L - 1, last2)

        if b == 0:

            @pl.when(h == 0)
            def _():
                wait_all(og_loads(j))

        v = own_sum(u, p, b) + par[u, 3:4, :]
        for d in (RIGHT, LEFT):
            v = v + jnp.where(has_up[d], rbuf[lax.rem(u, 2), d, 0, sub_rows(b), :].astype(F32), 0.0)
        same, cross, back = (par[u, k : k + 1, :] for k in range(3))
        row = jnp.concatenate(
            [jnp.broadcast_to(scale[k : k + 1, :], (LANE, LANE)).T for k in range(b * SB // LANE, (b + 1) * SB // LANE)],
            axis=0,
        )
        gy = row * packed(og_v[h, sub_rows(b), :].astype(F32), og_v[1 - h, sub_rows(b), :].astype(F32), h)
        cdf = 0.5 * (1.0 + lax.erf(v * INV_SQRT2))
        act = v * cdf
        slope = cdf + v * (INV_SQRT_2PI * jnp.exp(-0.5 * v * v))
        act_x = swap(act)
        mixed = row * (same * act + cross * act_x)
        gpre = ((same * gy + back * swap(gy)) * slope).astype(BF16)
        gath[lax.rem(u, 4), p, c, sub_rows(b), :] = gpre
        sacc[u, 0] += fold(gy * act)
        sacc[u, 1] += fold(gy * act_x)
        sacc[u, 2] += fold(gpre.astype(F32))

        @pl.when(h == 0)
        def _():
            mix_0[sub_rows(b), :] = mixed.astype(BF16)

        @pl.when(h == 1)
        def _():
            if b > 1:
                wait_all(mix_stores(j, b))
            else:

                @pl.when(j >= 1)
                def _():
                    wait_all(mix_stores(j, b))

            first, second = mix_0[sub_rows(b), :], mixed.astype(BF16)
            for t in range(2):
                mix_v[b % 2, t] = halves(first, second, t)
            start_all(mix_stores(j, b))

    first_partner, second_partner = (xp, yp), (yp, xp)

    def w_copy(u, t, kind):
        u2 = lax.rem(u, 2)
        return remote(
            wkeep.at[u2, t, 0] if kind == KEEP else wsend.at[t, kind],
            wrecv.at[u2, t, kind],
            w_send.at[t, kind],
            w_recv.at[u2, t, kind],
            rows=second_partner[t] if kind == KEEP else first_partner[t],
        )

    def wout_stores(j, t):
        return [
            pltpu.make_async_copy(wout.at[t, k], wgs[t].at[:, lanes(k * NCH + j)], wout_s.at[t, k])
            for k in range(2)
        ]

    def pg_place(i):
        return pool_v.at[lax.div(i, 2), some_rows(lax.rem(i, 2), PB), :]

    def pg_store(t, i):
        return pltpu.make_async_copy(pg_place(i), pgs[t].at[some_rows(i, PB), :], pg_s.at[i])

    def row_products(u, t, one, two):
        cols = []
        for owner in (one, two):
            pair = [gath[lax.rem(u, 4), owner, core] for core in range(2)]
            cols.append(halves(pair[0], pair[1], t))
        return dot(pool_t[t], jnp.concatenate(cols, axis=1)).astype(BF16)

    def pool_products(j, t, i):
        mine = some_rows(i, PB)
        total = None
        for q in range(L):
            cols = []
            for core in range(2):
                pair = [gath[lax.rem(2 * j + h, 4), q, core, mine, :] for h in range(2)]
                cols.append(halves(pair[0], pair[1], t))
            term = dot_t(jnp.concatenate(cols, axis=1), wb[q])
            total = term if total is None else total + term

        @pl.when(j == 0)
        def _():
            acc[t, mine, :] = total

        @pl.when((j > 0) & (j < NCH - 1))
        def _():
            acc[t, mine, :] += total

        @pl.when(j == NCH - 1)
        def _():
            if t > 0:
                pg_store(t, i).wait()
            pg_place(i)[...] = (acc[t, mine, :] + total).astype(BF16)
            pg_store(t, i).start()

    pool_load(0, 0).start()
    start_all(wf_loads(0, 0))

    bar = pltpu.get_barrier_semaphore()

    @pl.when(has_left)
    def _():
        signal(bar, feat=f - 2)

    @pl.when(has_right)
    def _():
        signal(bar, feat=f + 2)

    signal(bar, feat=sib)
    signal(bar, rows=xp)
    signal(bar, rows=yp)
    signal(bar, rows=dp)
    sacc[...] = jnp.zeros_like(sacc)
    for k in range(rows // LANE):
        here = slice(k * LANE, (k + 1) * LANE)
        scale[k : k + 1, :] = mask[:, here].astype(F32) / count[:, here].astype(F32)
    for u in range(U):
        ch = slice(u // 2 * LANE, (u // 2 + 1) * LANE)
        s00, s01, s10, s11 = (stitch[k : k + 1, ch] for k in range(4))
        rows_of = (s00, s11), (s01, s10), (s10, s01), (bias_a[:, ch], bias_b[:, ch])
        for k, (one, two) in enumerate(rows_of):
            par[u, k : k + 1, :] = halves(one, two, u % 2)

    pl.semaphore_wait(bar, 4 + has_left.astype(jnp.int32) + has_right.astype(jnp.int32))

    def tick(T, carry):
        per, s = lax.div(T, L), lax.rem(T, L)
        par2 = lax.rem(per, 2)
        u = per - 3
        ur = per - 2
        gathers = (u >= 0) & (u < U)
        sums = (ur >= 0) & (ur < U)

        @pl.when((s == 0) & (per >= 1) & (per < SENDING))
        def _():
            @pl.when(has_left)
            def _():
                pl.semaphore_wait(credit.at[0], 1)

            @pl.when(has_right)
            def _():
                pl.semaphore_wait(credit.at[1], 1)

            pl.semaphore_wait(credit.at[2], 1)

        @pl.when((s == 1) & sums & (par2 == 0))
        def _():
            for k in range(L):
                part_copy(lax.div(ur, 2), k, 0).wait_recv()
            start_all(og_loads(lax.div(ur, 2)))

        before = T - 1 + L
        per_m, s_m = lax.div(before, L) - 1, lax.rem(before, L)
        par_m = lax.rem(per_m + 2, 2)
        u_m, ur_m = per_m - 3, per_m - 2
        gathers_m = (u_m >= 0) & (u_m < U)
        sums_m = (ur_m >= 0) & (ur_m < U)
        ub = per - 4
        uz = per - 5
        jp = lax.div(jnp.maximum(per - 5, 0), 2)

        def flows(b):
            @pl.when((s == 0) & gathers)
            def _():
                finalize(u, b, per)

            for d in (RIGHT, LEFT):
                gather_here = pos[d] >= s
                o = p - s if d == RIGHT else p + s
                dest = p + (L - s) if d == RIGHT else p - (L - s)
                shares = (s >= 1) if d == LEFT else (s >= 0)

                @pl.when(gathers & gather_here)
                def _():
                    @pl.when(s >= 1)
                    def _():
                        gath_copy(u, o, d, b, s - 1, par2).wait_recv()

                    @pl.when(pos[d] < L - 1)
                    def _():
                        gath_copy(u, o, d, b, s, par2).start()

                    @pl.when(shares)
                    def _():
                        share_copy(u, o, c, d, b, s, par2).start()

                @pl.when(sums & jnp.logical_not(gather_here))
                def _():
                    block = sum_block(ur, d, b, s - 1)

                    @pl.when(pos[d] >= 1)
                    def _():
                        sum_wait(ur, d, b, s - 1, par2)
                        block[...] = (own_sum(ur, dest, b) + block[...].astype(F32)).astype(BF16)

                    @pl.when(pos[d] < 1)
                    def _():
                        block[...] = own_sum(ur, dest, b).astype(BF16)

                    sum_copy(ur, d, b, s, par2).start()

        def share_waits():
            for b in range(NS):
                for d in (RIGHT, LEFT):
                    o = p - s_m if d == RIGHT else p + s_m
                    shares = (s_m >= 1) if d == LEFT else (s_m >= 0)

                    @pl.when(gathers_m & (pos[d] >= s_m) & shares)
                    def _():
                        share_copy(u_m, o, 1 - c, d, b, s_m, par_m).wait_recv()

        def partial_products():
            @pl.when(per < U)
            def _():
                slot = lax.rem(T, 2)
                pool_load(T, 0).wait()
                wait_all(wf_loads(T, 0))

                @pl.when(T + 1 < U * L)
                def _():
                    def load(t):
                        pool_load(T + 1, t).start()
                        start_all(wf_loads(T + 1, t))

                    tower_of(T + 1, load)

                j = lax.div(per, 2)
                t, half = lax.rem(s, 2), lax.div(s, 2)
                res = dot(pool_v[slot], wf[slot]).astype(BF16)

                @pl.when(par2 == 0)
                def _():
                    for q in range(L):
                        part_own[lax.rem(j, 2), t, q, some_rows(half, HB), :] = res[:, q * LANE : (q + 1) * LANE]

                @pl.when(par2 == 1)
                def _():
                    for q in range(L):
                        part_sib[slot, q] = res[:, q * LANE : (q + 1) * LANE]
                    part_copy(j, s, slot).start()

                @pl.when(per == 0)
                def _():
                    pool_t[t, :, some_rows(half, HB)] = pool_v[slot].T

        def weight_products(t):
            @pl.when((s == 0) & (ub >= 0) & (ub < U))
            def _():
                if t == 0:

                    @pl.when(ub >= 2)
                    def _():
                        pl.semaphore_wait(wcredit.at[0], 1)
                        pl.semaphore_wait(wcredit.at[1], 1)

                res = row_products(ub, t, dp, first_partner[t])
                for kind in (FAR, NEAR):
                    wsend[t, kind] = res[:, kind * LANE : (kind + 1) * LANE]
                    w_copy(ub, t, kind).start()

            @pl.when((s == 1) & (ub >= 0) & (ub < U))
            def _():
                res = row_products(ub, t, second_partner[t], r)
                for k in range(2):
                    wkeep[lax.rem(ub, 2), t, k] = res[:, k * LANE : (k + 1) * LANE]

        def pool_piece(k):
            @pl.when((per >= 5) & (par2 == 1) & (s >= 2))
            def _():
                if k == 0:

                    @pl.when(s == 2)
                    def _():
                        wait_all(wb_loads(jp, 0))

                pool_products(jp, 0, 2 * (s - 2) + k)
                if k == 1:

                    @pl.when(s == 3)
                    def _():
                        start_all(wb_loads(jp, 1))

            @pl.when((per >= 6) & (par2 == 0) & ((s == 1) | (s == 2)))
            def _():
                if k == 0:

                    @pl.when(s == 1)
                    def _():
                        wait_all(wb_loads(jp, 1))

                pool_products(jp, 1, 2 * (s - 1) + k)

        def finish_weights():
            @pl.when((s == 2) & (uz >= 0) & (uz < U))
            def _():
                j, h, u2 = lax.div(uz, 2), lax.rem(uz, 2), lax.rem(uz, 2)
                for t in range(2):
                    w_copy(uz, t, NEAR).wait_recv()
                    w_copy(uz, t, KEEP).wait_recv()
                    w_copy(uz, t, KEEP).wait_send()
                    both = wkeep[u2, t, 1].astype(F32) + wrecv[u2, t, NEAR].astype(F32)
                    both = both + wrecv[u2, t, KEEP].astype(F32)

                    @pl.when(h == 0)
                    def _():
                        @pl.when(j >= 1)
                        def _():
                            wait_all(wout_stores(j, t))

                        wout[t, 0] = both

                    @pl.when(h == 1)
                    def _():
                        first = wout[t, 0]
                        for k in range(2):
                            wout[t, k] = halves(first, both, k)
                        start_all(wout_stores(j, t))

                @pl.when(uz < U - 2)
                def _():
                    signal(wcredit.at[0], rows=xp)
                    signal(wcredit.at[1], rows=yp)

            @pl.when((s == 3) & (ub >= 0) & (ub < U))
            def _():
                u2 = lax.rem(ub, 2)
                for t in range(2):
                    w_copy(ub, t, FAR).wait_recv()
                    both = wkeep[u2, t, 0].astype(F32) + wrecv[u2, t, FAR].astype(F32)
                    wkeep[u2, t, 0] = both.astype(BF16)
                    w_copy(ub, t, KEEP).start()

        @pl.when((s == 0) & (uz >= 0) & (uz < U))
        def _():
            for t in range(2):
                for kind in (FAR, NEAR):
                    w_copy(uz, t, kind).wait_send()

        @pl.when((s == 0) & (per >= 5) & (par2 == 1))
        def _():
            start_all(wb_loads(jp, 0))

        flows(0)
        share_waits()
        weight_products(0)
        flows(1)
        pool_piece(0)
        flows(2)
        weight_products(1)
        flows(3)
        pool_piece(1)
        flows(4)
        partial_products()
        finish_weights()

        @pl.when((per_m >= 1) & (per_m < U) & (par_m == 1))
        def _():
            part_copy(0, s_m, 0).wait_send()

        for b in range(NS):
            for d in (RIGHT, LEFT):
                shares = (s_m >= 1) if d == LEFT else (s_m >= 0)

                @pl.when(gathers_m & (pos[d] >= s_m))
                def _():
                    @pl.when(pos[d] < L - 1)
                    def _():
                        gath_copy(u_m, p, d, b, s_m, par_m).wait_send()

                    @pl.when(shares)
                    def _():
                        share_copy(u_m, p, c, d, b, s_m, par_m).wait_send()

                @pl.when(sums_m & (pos[d] < s_m))
                def _():
                    sum_copy(ur_m, d, b, s_m, par_m).wait_send()

        @pl.when((s == 2) & (per < SENDING - 1))
        def _():
            @pl.when(has_left)
            def _():
                signal(credit.at[1], feat=f - 2)

            @pl.when(has_right)
            def _():
                signal(credit.at[0], feat=f + 2)

            signal(credit.at[2], feat=sib)

        @pl.when(T == (U + 2) * L + 1)
        def _():
            for j in range(NCH):
                sums_of = [[jnp.sum(sacc[2 * j + h, k], axis=0, keepdims=True) for h in range(2)] for k in range(3)]
                (same, cross, bias) = sums_of
                rows_of = [halves(*same, 0), halves(*cross, 0), halves(*cross, 1), halves(*same, 1)]
                rows_of += [halves(*bias, 0), halves(*bias, 1), jnp.zeros((2, LANE), F32)]
                sred[j] = jnp.concatenate(rows_of, axis=0)
            for k, peer in enumerate((xp, yp, dp)):
                remote(sred.at[peer], srecv.at[k], st_send.at[k], st_recv.at[k], rows=peer).start()

        return carry

    lax.fori_loop(0, TICKS, tick, 0)

    for k, peer in enumerate((xp, yp, dp)):
        copy = remote(sred.at[peer], srecv.at[k], st_send.at[k], st_recv.at[k], rows=peer)
        copy.wait_send()
        copy.wait_recv()
    stats[...] = sred[r] + srecv[0] + srecv[1] + srecv[2]
    for b in range(2):
        wait_all(mix_stores(NCH - 1, b))
    for t in range(2):
        wait_all(wout_stores(NCH - 1, t))
    for i in range(PIECES):
        pg_store(1, i).wait()


def fused(
    pool_a, pool_b, weight_a, weight_b, bias_a, bias_b, stitch, crop_count, row_mask, outgrad_a, outgrad_b
):
    rows, width = pool_a.shape
    chl = bias_a.shape[0]
    NS, L = SUBS, 4
    SB, HB, PB = rows // NS, rows // 2, rows // PIECES
    NCH = chl // LANE
    hbm = pl.BlockSpec(memory_space=pl.ANY)
    vmem = pl.BlockSpec(memory_space=pltpu.VMEM)
    dma = pltpu.SemaphoreType.DMA
    out_shape = (
        jax.ShapeDtypeStruct((rows, chl), BF16),
        jax.ShapeDtypeStruct((rows, chl), BF16),
        jax.ShapeDtypeStruct((rows, width), BF16),
        jax.ShapeDtypeStruct((rows, width), BF16),
        jax.ShapeDtypeStruct((width, 2 * chl), F32),
        jax.ShapeDtypeStruct((width, 2 * chl), F32),
        jax.ShapeDtypeStruct((8, LANE), F32),
    )
    scratch = [
        pltpu.VMEM((2, HB, width), BF16),
        pltpu.VMEM((2, width, rows), BF16),
        pltpu.VMEM((2, width, L * LANE), BF16),
        pltpu.VMEM((L, width, 2 * LANE), BF16),
        pltpu.VMEM((2, L, HB, LANE), BF16),
        pltpu.VMEM((2, 2, L, rows, LANE), BF16),
        pltpu.VMEM((2, 2, L, rows, LANE), BF16),
        pltpu.VMEM((2, 2, 3, rows, LANE), BF16),
        pltpu.VMEM((4, L, 2, rows, LANE), BF16),
        pltpu.VMEM((2, rows, width), F32),
        pltpu.VMEM((2, 2, width, LANE), BF16),
        pltpu.VMEM((2, 2, 2, width, LANE), BF16),
        pltpu.VMEM((2, 2, 3, width, LANE), BF16),
        pltpu.VMEM((2, 2, width, LANE), F32),
        pltpu.VMEM((2, rows, LANE), BF16),
        pltpu.VMEM((rows // LANE, LANE), F32),
        pltpu.VMEM((2 * NCH, 8, LANE), F32),
        pltpu.VMEM((rows, LANE), BF16),
        pltpu.VMEM((2, 2, SB, LANE), BF16),
        pltpu.VMEM((2 * NCH, 3, 8, LANE), F32),
        pltpu.VMEM((NCH, 8, LANE), F32),
        pltpu.VMEM((3, 8, LANE), F32),
        dma((2,)),
        dma((2, L)),
        dma((L, 2)),
        dma((L,)),
        dma((L,)),
        dma((2, NS, L)),
        dma((2, NS, L, 2)),
        dma((2, NS, L)),
        dma((2, NS, L, 2)),
        dma((2, 3)),
        dma((2, 2, 3)),
        dma((2, 2)),
        dma((2,)),
        dma((2, 2)),
        dma((PIECES,)),
        dma((3,)),
        dma((3,)),
        pltpu.SemaphoreType.REGULAR((3,)),
        pltpu.SemaphoreType.REGULAR((2,)),
    ]
    mixed_a, mixed_b, pg_a, pg_b, wg_a, wg_b, stats = pl.pallas_call(
        functools.partial(kernel, rows, width, chl),
        out_shape=out_shape,
        in_specs=[hbm] * 4 + [vmem] * 5 + [hbm] * 2,
        out_specs=(hbm, hbm, hbm, hbm, hbm, hbm, vmem),
        scratch_shapes=scratch,
        compiler_params=pltpu.CompilerParams(
            collective_id=0, has_side_effects=True, vmem_limit_bytes=VMEM_LIMIT
        ),
    )(
        pool_a,
        pool_b,
        weight_a,
        weight_b,
        bias_a[None],
        bias_b[None],
        stitch.reshape(4, chl),
        row_mask[None],
        crop_count[None],
        outgrad_a,
        outgrad_b,
    )
    return mixed_a, mixed_b, pg_a, pg_b, wg_a, wg_b, stats[4], stats[5], stats[:4].reshape(2, 2, LANE)


VMEM_LIMIT = 63 * 1024 * 1024


def plain(
    pool_a, pool_b, weight_a, weight_b, bias_a, bias_b, stitch, crop_count, row_mask, outgrad_a, outgrad_b
):
    row = (row_mask.astype(F32) / crop_count.astype(F32))[:, None]

    def pre(pool, weight, bias):
        partial = dot(pool, weight).astype(BF16)
        return lax.psum_scatter(partial, "feat", scatter_dimension=1, tiled=True).astype(F32) + bias

    def gelu(v):
        cdf = 0.5 * (1.0 + lax.erf(v * INV_SQRT2))
        return v * cdf, cdf + v * (INV_SQRT_2PI * jnp.exp(-0.5 * v * v))

    act_a, slope_a = gelu(pre(pool_a, weight_a, bias_a))
    act_b, slope_b = gelu(pre(pool_b, weight_b, bias_b))
    (s00, s01), (s10, s11) = stitch[0], stitch[1]
    mixed_a = (row * (s00 * act_a + s01 * act_b)).astype(BF16)
    mixed_b = (row * (s10 * act_a + s11 * act_b)).astype(BF16)
    gy_a = row * outgrad_a.astype(F32)
    gy_b = row * outgrad_b.astype(F32)
    gpre_a = ((s00 * gy_a + s10 * gy_b) * slope_a).astype(BF16)
    gpre_b = ((s01 * gy_a + s11 * gy_b) * slope_b).astype(BF16)
    sums = jnp.stack(
        [
            jnp.sum(v, axis=0)
            for v in (
                gy_a * act_a,
                gy_a * act_b,
                gy_b * act_a,
                gy_b * act_b,
                gpre_a.astype(F32),
                gpre_b.astype(F32),
            )
        ]
    )
    sums = lax.psum_scatter(sums, "rows", scatter_dimension=1, tiled=True)

    def back(pool, weight, gpre):
        whole = lax.all_gather(gpre, "feat", axis=1, tiled=True)
        pool_grad = dot_t(whole, weight).astype(BF16)
        wgrad = lax.dot_general(pool, whole, (((0,), (0,)), ((), ())), preferred_element_type=F32)
        wgrad = lax.psum_scatter(wgrad.astype(BF16), "rows", scatter_dimension=1, tiled=True)
        return pool_grad, wgrad.astype(F32)

    pg_a, wg_a = back(pool_a, weight_a, gpre_a)
    pg_b, wg_b = back(pool_b, weight_b, gpre_b)
    return mixed_a, mixed_b, pg_a, pg_b, wg_a, wg_b, sums[4], sums[5], sums[:4].reshape(2, 2, -1)


def shards(
    pool_a, pool_b, weight_a, weight_b, bias_a, bias_b, stitch, crop_count, row_mask, outgrad_a, outgrad_b
):
    rows, width = pool_a.shape
    chl = bias_a.shape[0]
    n_rows, n_feat = lax.axis_size("rows"), lax.axis_size("feat")
    fits = (
        n_rows == 4
        and n_feat == 8
        and chl == n_rows * LANE
        and width % LANE == 0
        and rows % (2 * SUBS * LANE) == 0
    )
    run = fused if fits else plain
    return run(pool_a, pool_b, weight_a, weight_b, bias_a, bias_b, stitch, crop_count, row_mask, outgrad_a, outgrad_b)


def solution(mesh):
    return jax.shard_map(
        shards,
        mesh=mesh,
        in_specs=(
            P("rows", "feat"),
            P("rows", "feat"),
            P("feat", None),
            P("feat", None),
            P("feat"),
            P("feat"),
            P(None, None, "feat"),
            P("rows"),
            P("rows"),
            P("rows", "feat"),
            P("rows", "feat"),
        ),
        out_specs=(
            P("rows", "feat"),
            P("rows", "feat"),
            P("rows", "feat"),
            P("rows", "feat"),
            P("feat", "rows"),
            P("feat", "rows"),
            P(("feat", "rows")),
            P(("feat", "rows")),
            P(None, None, ("feat", "rows")),
        ),
        check_vma=False,
    )
```

```python
import functools

import jax
import jax.numpy as jnp
from jax import lax
from jax.experimental import pallas as pl
from jax.experimental.pallas import tpu as pltpu
from jax.sharding import PartitionSpec as P

MESH = pl.DeviceIdType.MESH
F32 = jnp.float32
BF16 = jnp.bfloat16
LANE = 128
HALF = 64
SUBS = 5
PIECES = 4
COPIES = 4
RIGHT, LEFT = 0, 1
FAR, NEAR, KEEP, OWN = 0, 1, 2, 3
INV_SQRT2 = 0.7071067811865476
INV_SQRT_2PI = 0.3989422804014327


def dot(lhs, rhs):
    return lax.dot_general(lhs, rhs, (((1,), (0,)), ((), ())), preferred_element_type=F32)


def dot_t(lhs, rhs):
    return lax.dot_general(lhs, rhs, (((1,), (1,)), ((), ())), preferred_element_type=F32)


def swap(v):
    return pltpu.roll(v, HALF, 1)


def upper(rows):
    return lax.broadcasted_iota(jnp.int32, (rows, LANE), 1) >= HALF


def halves(one, two, half):
    if half == 0:
        return jnp.where(upper(one.shape[0]), swap(two), one)
    return jnp.where(upper(one.shape[0]), two, swap(one))


def kernel(rows, width, chl, *refs):
    (
        pool_a, pool_b, weight_a, weight_b, bias_a, bias_b, stitch, mask, count, og_a, og_b,
        mixed_a, mixed_b, pg_a, pg_b, wg_a, wg_b, stats,
        pool_v, pool_t, wf, wb, part_sib, part_own, xr, rbuf, gath, acc, wsend, wkeep, wrecv, wout_0, wout,
        og_v, scale, par, mix_0, mix_v, sacc, sred, srecv,
        pool_s, wf_s, wb_s, xs_send, xs_recv, z_send, z_recv, g_send, g_recv,
        w_send, w_recv, wout_s, og_s, mix_s, pg_s, st_send, st_recv, credit, wcredit,
    ) = refs
    L = 4
    NS = SUBS
    SB = rows // NS
    HB = rows // 2
    PB = rows // PIECES
    NCH = chl // LANE
    U = 2 * NCH
    SENDING = U + 3
    TICKS = (U + 5) * L
    pools, weights = (pool_a, pool_b), (weight_a, weight_b)
    ogs, mixeds = (og_a, og_b), (mixed_a, mixed_b)
    pgs, wgs = (pg_a, pg_b), (wg_a, wg_b)

    f = lax.axis_index("feat")
    r = lax.axis_index("rows")
    p = lax.div(f, 2)
    c = lax.rem(f, 2)
    sib = f + 1 - 2 * c
    xp = r + 1 - 2 * lax.rem(r, 2)
    yp = lax.rem(r + 2, 4)
    dp = 3 - r
    has_left, has_right = p > 0, p < L - 1
    pos = (p, L - 1 - p)
    has_up = (has_left, has_right)
    nxt = (f + 2, f - 2)

    def remote(src, dst, send, recv, **dev):
        return pltpu.make_async_remote_copy(
            src_ref=src, dst_ref=dst, send_sem=send, recv_sem=recv, device_id=dev, device_id_type=MESH
        )

    def signal(sem, **dev):
        pl.semaphore_signal(sem, inc=1, device_id=dev, device_id_type=MESH)

    def start_all(copies):
        for copy in copies:
            copy.start()

    def wait_all(copies):
        for copy in copies:
            copy.wait()

    def lanes(index):
        return pl.ds(pl.multiple_of(index * LANE, LANE), LANE)

    def some_rows(i, n):
        return pl.ds(pl.multiple_of(i * n, n), n)

    def sub_rows(b):
        return pl.ds(b * SB, SB)

    def tower_of(index, run):
        for t in range(2):

            @pl.when(lax.rem(index, 2) == t)
            def _():
                run(t)

    def pool_load(tick, t):
        slot = lax.rem(tick, 2)
        half = lax.div(lax.rem(tick, L), 2)
        return pltpu.make_async_copy(pools[t].at[some_rows(half, HB), :], pool_v.at[slot], pool_s.at[slot])

    def wf_loads(tick, t):
        j = lax.div(tick, 2 * L)
        slot = lax.rem(tick, 2)
        core = jnp.where(lax.rem(lax.div(tick, L), 2) == 0, c, 1 - c)
        return [
            pltpu.make_async_copy(
                weights[t].at[:, lanes((2 * q + core) * NCH + j)],
                wf.at[slot, :, q * LANE : (q + 1) * LANE],
                wf_s.at[slot, q],
            )
            for q in range(L)
        ]

    def wb_loads(j, t):
        out = []
        for q in range(L):
            for k in range(2):
                out.append(
                    pltpu.make_async_copy(
                        weights[t].at[:, lanes((2 * q + k) * NCH + j)],
                        wb.at[q, :, k * LANE : (k + 1) * LANE],
                        wb_s.at[q, k],
                    )
                )
        return out

    def og_loads(j):
        return [pltpu.make_async_copy(ogs[t].at[:, lanes(j)], og_v.at[t], og_s.at[t]) for t in range(2)]

    def mix_stores(j, b):
        return [
            pltpu.make_async_copy(mix_v.at[b % 2, t], mixeds[t].at[sub_rows(b), lanes(j)], mix_s.at[b % 2, t])
            for t in range(2)
        ]

    def part_copy(j, s, slot):
        t, half = lax.rem(s, 2), lax.div(s, 2)
        return remote(
            part_sib.at[slot],
            xr.at[lax.rem(j, 2), t, :, some_rows(half, HB), :],
            xs_send.at[s],
            xs_recv.at[s],
            feat=sib,
        )

    def share_copy(u, o, core, d, b, s, par2):
        block = gath.at[lax.rem(u, 4), o, core, sub_rows(b), :]
        return remote(block, block, g_send.at[d, b, s], g_recv.at[d, b, s, par2], feat=sib)

    def gath_copy(u, o, d, b, s, par2):
        block = gath.at[lax.rem(u, 4), o, c, sub_rows(b), :]
        return remote(block, block, z_send.at[d, b, s], z_recv.at[d, b, s, par2], feat=nxt[d])

    def sum_block(u, d, b, s):
        return rbuf.at[lax.rem(u, 2), d, lax.rem(s, 3), sub_rows(b), :]

    def sum_copy(u, d, b, s, par2):
        return remote(
            sum_block(u, d, b, s - 1),
            sum_block(u, d, b, s),
            z_send.at[d, b, s],
            z_recv.at[d, b, s, par2],
            feat=nxt[d],
        )

    def sum_wait(u, d, b, s, par2):
        block = sum_block(u, d, b, s)
        remote(block, block, z_send.at[d, b, s], z_recv.at[d, b, s, par2], feat=nxt[d]).wait_recv()

    def packed(one, two, h):
        return jnp.where(upper(one.shape[0]) == (h == 1), one, swap(two))

    def own_sum(u, o, b):
        j, h = lax.div(u, 2), lax.rem(u, 2)
        j2 = lax.rem(j, 2)

        def tower(t):
            return part_own[j2, t, o, sub_rows(b), :].astype(F32) + xr[j2, t, o, sub_rows(b), :].astype(F32)

        return packed(tower(h), tower(1 - h), h)

    def fold(v):
        return jnp.sum(v.reshape(SB // 8, 8, LANE), axis=0)

    def finalize(u, b, per):
        j, h = lax.div(u, 2), lax.rem(u, 2)
        last2 = lax.rem(per - 1, 2)
        for d in (RIGHT, LEFT):

            @pl.when(has_up[d])
            def _():
                sum_wait(u, d, b, L - 1, last2)

        if b == 0:

            @pl.when(h == 0)
            def _():
                wait_all(og_loads(j))

        v = own_sum(u, p, b) + par[u, 3:4, :]
        for d in (RIGHT, LEFT):
            v = v + jnp.where(has_up[d], rbuf[lax.rem(u, 2), d, 0, sub_rows(b), :].astype(F32), 0.0)
        same, cross, back = (par[u, k : k + 1, :] for k in range(3))
        row = jnp.concatenate(
            [jnp.broadcast_to(scale[k : k + 1, :], (LANE, LANE)).T for k in range(b * SB // LANE, (b + 1) * SB // LANE)],
            axis=0,
        )
        gy = row * packed(og_v[h, sub_rows(b), :].astype(F32), og_v[1 - h, sub_rows(b), :].astype(F32), h)
        cdf = 0.5 * (1.0 + lax.erf(v * INV_SQRT2))
        act = v * cdf
        slope = cdf + v * (INV_SQRT_2PI * jnp.exp(-0.5 * v * v))
        act_x = swap(act)
        mixed = row * (same * act + cross * act_x)
        gpre = ((same * gy + back * swap(gy)) * slope).astype(BF16)
        gath[lax.rem(u, 4), p, c, sub_rows(b), :] = gpre
        sacc[u, 0] += fold(gy * act)
        sacc[u, 1] += fold(gy * act_x)
        sacc[u, 2] += fold(gpre.astype(F32))

        @pl.when(h == 0)
        def _():
            mix_0[sub_rows(b), :] = mixed.astype(BF16)

        @pl.when(h == 1)
        def _():
            if b > 1:
                wait_all(mix_stores(j, b))
            else:

                @pl.when(j >= 1)
                def _():
                    wait_all(mix_stores(j, b))

            first, second = mix_0[sub_rows(b), :], mixed.astype(BF16)
            for t in range(2):
                mix_v[b % 2, t] = halves(first, second, t)
            start_all(mix_stores(j, b))

    first_partner, second_partner = (xp, yp), (yp, xp)

    def w_copy(u, t, kind):
        u2 = lax.rem(u, 2)
        return remote(
            wkeep.at[u2, t, 0] if kind == KEEP else wsend.at[t, kind],
            wrecv.at[u2, t, kind],
            w_send.at[t, kind],
            w_recv.at[u2, t, kind],
            rows=second_partner[t] if kind == KEEP else first_partner[t],
        )

    def wout_stores(j, t):
        return [
            pltpu.make_async_copy(wout.at[t, k], wgs[t].at[:, lanes(k * NCH + j)], wout_s.at[t, k])
            for k in range(2)
        ]

    def pg_place(i):
        return pool_v.at[lax.div(i, 2), some_rows(lax.rem(i, 2), PB), :]

    def pg_store(t, i):
        return pltpu.make_async_copy(pg_place(i), pgs[t].at[some_rows(i, PB), :], pg_s.at[i])

    def row_products(u, t, one, two):
        cols = []
        for owner in (one, two):
            pair = [gath[lax.rem(u, 4), owner, core] for core in range(2)]
            cols.append(halves(pair[0], pair[1], t))
        return dot(pool_t[t], jnp.concatenate(cols, axis=1)).astype(BF16)

    def pool_products(j, t, i):
        mine = some_rows(i, PB)
        total = None
        for q in range(L):
            cols = []
            for core in range(2):
                pair = [gath[lax.rem(2 * j + h, 4), q, core, mine, :] for h in range(2)]
                cols.append(halves(pair[0], pair[1], t))
            term = dot_t(jnp.concatenate(cols, axis=1), wb[q])
            total = term if total is None else total + term

        @pl.when(j == 0)
        def _():
            acc[t, mine, :] = total

        @pl.when((j > 0) & (j < NCH - 1))
        def _():
            acc[t, mine, :] += total

        @pl.when(j == NCH - 1)
        def _():
            if t > 0:
                pg_store(t, i).wait()
            pg_place(i)[...] = (acc[t, mine, :] + total).astype(BF16)
            pg_store(t, i).start()

    def first_weights(t, other):
        core = 1 - c if other else c
        out = []
        for q in range(L):
            src = weights[t].at[:, lanes((2 * q + core) * NCH)]
            if other:
                tile, k = 2 * t + q // 2, q % 2
                dst, sem = wb.at[tile, :, k * LANE : (k + 1) * LANE], wb_s.at[tile, k]
            else:
                dst, sem = wf.at[t, :, q * LANE : (q + 1) * LANE], wf_s.at[t, q]
            out.append(pltpu.make_async_copy(src, dst, sem))
        return out

    def first_rows(t, half):
        return pltpu.make_async_copy(pools[t].at[half * HB : (half + 1) * HB, :], pool_v.at[t], pool_s.at[t])

    for t in range(2):
        first_rows(t, 0).start()
        start_all(first_weights(t, False))
    for t in range(2):
        start_all(first_weights(t, True))

    bar = pltpu.get_barrier_semaphore()

    @pl.when(has_left)
    def _():
        signal(bar, feat=f - 2)

    @pl.when(has_right)
    def _():
        signal(bar, feat=f + 2)

    signal(bar, feat=sib)
    signal(bar, rows=xp)
    signal(bar, rows=yp)
    signal(bar, rows=dp)
    sacc[...] = jnp.zeros_like(sacc)
    scale[...] = mask[...].astype(F32) / count[...].astype(F32)
    for u in range(U):
        ch = slice(u // 2 * LANE, (u // 2 + 1) * LANE)
        s00, s01, s10, s11 = (stitch[k // 2, k % 2 : k % 2 + 1, ch] for k in range(4))
        rows_of = (s00, s11), (s01, s10), (s10, s01), (bias_a[:, ch], bias_b[:, ch])
        for k, (one, two) in enumerate(rows_of):
            par[u, k : k + 1, :] = halves(one, two, u % 2)

    for half in range(2):
        here = slice(half * HB, (half + 1) * HB)
        for t in range(2):
            first_rows(t, half).wait()
            if half == 0:
                wait_all(first_weights(t, False))
            res = dot(pool_v[t], wf[t]).astype(BF16)
            for q in range(L):
                part_own[0, t, q, here, :] = res[:, q * LANE : (q + 1) * LANE]
        if half == 0:
            pl.semaphore_wait(bar, 4 + has_left.astype(jnp.int32) + has_right.astype(jnp.int32))
        for t in range(2):
            if half == 0:
                wait_all(first_weights(t, True))
            else:
                part_copy(0, t, t).wait_send()
            for k in range(2):
                res = dot(pool_v[t], wb[2 * t + k]).astype(BF16)
                for q in range(2):
                    part_sib[t, 2 * k + q] = res[:, q * LANE : (q + 1) * LANE]
            part_copy(0, 2 * half + t, t).start()
            if half == 0:
                first_rows(t, 1).start()
            elif t == 0:
                pool_load(2 * L, 0).start()
                start_all(wf_loads(2 * L, 0))
    part_copy(0, 2, 0).wait_send()

    def tick(T, carry):
        per, s = lax.div(T, L), lax.rem(T, L)
        par2 = lax.rem(per, 2)
        u = per - 3
        ur = per - 2
        gathers = (u >= 0) & (u < U)
        sums = (ur >= 0) & (ur < U)

        @pl.when((s == 0) & (per >= 3) & (per < SENDING))
        def _():
            @pl.when(has_left)
            def _():
                pl.semaphore_wait(credit.at[0], 1)

            @pl.when(has_right)
            def _():
                pl.semaphore_wait(credit.at[1], 1)

            pl.semaphore_wait(credit.at[2], 1)

        @pl.when((s == 1) & sums & (par2 == 0))
        def _():
            for k in range(L):
                part_copy(lax.div(ur, 2), k, 0).wait_recv()
            start_all(og_loads(lax.div(ur, 2)))

        before = T - 1 + L
        per_m, s_m = lax.div(before, L) - 1, lax.rem(before, L)
        par_m = lax.rem(per_m + 2, 2)
        u_m, ur_m = per_m - 3, per_m - 2
        gathers_m = (u_m >= 0) & (u_m < U)
        sums_m = (ur_m >= 0) & (ur_m < U)
        ub = per - 4
        uz = per - 5
        jp = lax.div(jnp.maximum(per - 5, 0), 2)

        def flows(b):
            @pl.when((s == 0) & gathers)
            def _():
                finalize(u, b, per)

            for d in (RIGHT, LEFT):
                gather_here = pos[d] >= s
                o = p - s if d == RIGHT else p + s
                dest = p + (L - s) if d == RIGHT else p - (L - s)
                shares = (s >= 1) if d == LEFT else (s >= 0)

                @pl.when(gathers & gather_here)
                def _():
                    @pl.when(s >= 1)
                    def _():
                        gath_copy(u, o, d, b, s - 1, par2).wait_recv()

                    @pl.when(pos[d] < L - 1)
                    def _():
                        gath_copy(u, o, d, b, s, par2).start()

                    @pl.when(shares)
                    def _():
                        share_copy(u, o, c, d, b, s, par2).start()

                @pl.when(sums & jnp.logical_not(gather_here))
                def _():
                    block = sum_block(ur, d, b, s - 1)

                    @pl.when(pos[d] >= 1)
                    def _():
                        sum_wait(ur, d, b, s - 1, par2)
                        block[...] = (own_sum(ur, dest, b) + block[...].astype(F32)).astype(BF16)

                    @pl.when(pos[d] < 1)
                    def _():
                        block[...] = own_sum(ur, dest, b).astype(BF16)

                    sum_copy(ur, d, b, s, par2).start()

        def share_waits():
            for b in range(NS):
                for d in (RIGHT, LEFT):
                    o = p - s_m if d == RIGHT else p + s_m
                    shares = (s_m >= 1) if d == LEFT else (s_m >= 0)

                    @pl.when(gathers_m & (pos[d] >= s_m) & shares)
                    def _():
                        share_copy(u_m, o, 1 - c, d, b, s_m, par_m).wait_recv()

        def partial_products():
            @pl.when(per < U)
            def _():
                slot = lax.rem(T, 2)
                pool_load(T, 0).wait()
                wait_all(wf_loads(T, 0))

                @pl.when(T + 1 < U * L)
                def _():
                    def load(t):
                        pool_load(T + 1, t).start()
                        start_all(wf_loads(T + 1, t))

                    tower_of(T + 1, load)

                j = lax.div(per, 2)
                t, half = lax.rem(s, 2), lax.div(s, 2)
                res = dot(pool_v[slot], wf[slot]).astype(BF16)

                @pl.when(par2 == 0)
                def _():
                    for q in range(L):
                        part_own[lax.rem(j, 2), t, q, some_rows(half, HB), :] = res[:, q * LANE : (q + 1) * LANE]

                @pl.when(par2 == 1)
                def _():
                    for q in range(L):
                        part_sib[slot, q] = res[:, q * LANE : (q + 1) * LANE]
                    part_copy(j, s, slot).start()

                @pl.when(per == 2)
                def _():
                    pool_t[t, :, some_rows(half, HB)] = pool_v[slot].T

        def weight_products(t):
            @pl.when((s == 0) & (ub >= 0) & (ub < U))
            def _():
                if t == 0:

                    @pl.when(ub >= 2)
                    def _():
                        pl.semaphore_wait(wcredit.at[0], 1)
                        pl.semaphore_wait(wcredit.at[1], 1)

                res = row_products(ub, t, dp, first_partner[t])
                for kind in (FAR, NEAR):
                    wsend[t, kind] = res[:, kind * LANE : (kind + 1) * LANE]
                w_copy(ub, t, FAR).start()

            @pl.when((s == 1) & (ub >= 0) & (ub < U))
            def _():
                res = row_products(ub, t, second_partner[t], r)
                for k in range(2):
                    wkeep[lax.rem(ub, 2), t, k] = res[:, k * LANE : (k + 1) * LANE]

        def pool_piece(k):
            @pl.when((per >= 5) & (par2 == 1) & (s >= 2))
            def _():
                if k == 0:

                    @pl.when(s == 2)
                    def _():
                        wait_all(wb_loads(jp, 0))

                pool_products(jp, 0, 2 * (s - 2) + k)
                if k == 1:

                    @pl.when(s == 3)
                    def _():
                        start_all(wb_loads(jp, 1))

            @pl.when((per >= 6) & (par2 == 0) & ((s == 1) | (s == 2)))
            def _():
                if k == 0:

                    @pl.when(s == 1)
                    def _():
                        wait_all(wb_loads(jp, 1))

                pool_products(jp, 1, 2 * (s - 1) + k)

        def send_near():
            @pl.when((s == 2) & (ub >= 0) & (ub < U))
            def _():
                for t in range(2):
                    w_copy(ub, t, NEAR).start()

        def finish_weights():
            @pl.when((s == 2) & (uz >= 0) & (uz < U))
            def _():
                j, h, u2 = lax.div(uz, 2), lax.rem(uz, 2), lax.rem(uz, 2)
                for t in range(2):
                    w_copy(uz, t, NEAR).wait_recv()
                    w_copy(uz, t, KEEP).wait_recv()
                    w_copy(uz, t, KEEP).wait_send()
                    both = wkeep[u2, t, 1].astype(F32) + wrecv[u2, t, NEAR].astype(F32)
                    both = both + wrecv[u2, t, KEEP].astype(F32)

                    @pl.when(h == 0)
                    def _():
                        @pl.when(j >= 1)
                        def _():
                            wait_all(wout_stores(j, t))

                        wout_0[t] = both

                    @pl.when(h == 1)
                    def _():
                        for k in range(2):
                            wout[t, k] = halves(wout_0[t], both, k).astype(BF16)
                        start_all(wout_stores(j, t))

                @pl.when(uz < U - 2)
                def _():
                    signal(wcredit.at[0], rows=xp)
                    signal(wcredit.at[1], rows=yp)

            @pl.when((s == 3) & (ub >= 0) & (ub < U))
            def _():
                u2 = lax.rem(ub, 2)
                for t in range(2):
                    w_copy(ub, t, FAR).wait_recv()
                    both = wkeep[u2, t, 0].astype(F32) + wrecv[u2, t, FAR].astype(F32)
                    wkeep[u2, t, 0] = both.astype(BF16)
                    w_copy(ub, t, KEEP).start()

        @pl.when((s == 0) & (uz >= 0) & (uz < U))
        def _():
            for t in range(2):
                for kind in (FAR, NEAR):
                    w_copy(uz, t, kind).wait_send()

        @pl.when((s == 0) & (per >= 5) & (par2 == 1))
        def _():
            start_all(wb_loads(jp, 0))

        flows(0)
        share_waits()
        weight_products(0)
        flows(1)
        pool_piece(0)
        flows(2)
        send_near()
        weight_products(1)
        flows(3)
        pool_piece(1)
        flows(4)
        partial_products()
        finish_weights()

        @pl.when((per_m >= 1) & (per_m < U) & (par_m == 1))
        def _():
            part_copy(0, s_m, 0).wait_send()

        for b in range(NS):
            for d in (RIGHT, LEFT):
                shares = (s_m >= 1) if d == LEFT else (s_m >= 0)

                @pl.when(gathers_m & (pos[d] >= s_m))
                def _():
                    @pl.when(pos[d] < L - 1)
                    def _():
                        gath_copy(u_m, p, d, b, s_m, par_m).wait_send()

                    @pl.when(shares)
                    def _():
                        share_copy(u_m, p, c, d, b, s_m, par_m).wait_send()

                @pl.when(sums_m & (pos[d] < s_m))
                def _():
                    sum_copy(ur_m, d, b, s_m, par_m).wait_send()

        @pl.when((s == 2) & (per < SENDING - 1))
        def _():
            @pl.when(has_left)
            def _():
                signal(credit.at[1], feat=f - 2)

            @pl.when(has_right)
            def _():
                signal(credit.at[0], feat=f + 2)

            signal(credit.at[2], feat=sib)

        @pl.when(T == (U + 2) * L + 1)
        def _():
            for j in range(NCH):
                sums_of = [[jnp.sum(sacc[2 * j + h, k], axis=0, keepdims=True) for h in range(2)] for k in range(3)]
                (same, cross, bias) = sums_of
                rows_of = [halves(*same, 0), halves(*cross, 0), halves(*cross, 1), halves(*same, 1)]
                rows_of += [halves(*bias, 0), halves(*bias, 1), jnp.zeros((2, LANE), F32)]
                sred[j] = jnp.concatenate(rows_of, axis=0)
            for k, peer in enumerate((xp, yp, dp)):
                remote(sred.at[peer], srecv.at[k], st_send.at[k], st_recv.at[k], rows=peer).start()

        return carry

    lax.fori_loop(2 * L, TICKS, tick, 0)

    for k, peer in enumerate((xp, yp, dp)):
        copy = remote(sred.at[peer], srecv.at[k], st_send.at[k], st_recv.at[k], rows=peer)
        copy.wait_send()
        copy.wait_recv()
    stats[...] = sred[r] + srecv[0] + srecv[1] + srecv[2]
    for b in range(2):
        wait_all(mix_stores(NCH - 1, b))
    for t in range(2):
        wait_all(wout_stores(NCH - 1, t))
    for i in range(PIECES):
        pg_store(1, i).wait()


def hand_over(*refs):
    sources, stats, results = refs[:6], refs[6], refs[7:13]
    bias_a, bias_b, stitch = refs[13:16]
    low, held, (load_s, store_s) = refs[16:18], refs[18:24], refs[24:]
    loads, stores, widen = [], [], []
    for k in (4, 0, 2, 5, 1, 3):
        n = results[k].shape[0] // COPIES
        for i in range(COPIES):
            some = pl.ds(i * n, n)
            via = low[k - 4] if k >= 4 else held[k]
            loads.append(pltpu.make_async_copy(sources[k].at[some, :], via.at[some, :], load_s.at[k, i]))
            stores.append(pltpu.make_async_copy(held[k].at[some, :], results[k].at[some, :], store_s.at[k, i]))
            widen.append((via, held[k], some) if k >= 4 else None)
    for copy in loads:
        copy.start()
    bias_a[...] = stats[4:5, :]
    bias_b[...] = stats[5:6, :]
    stitch[0] = stats[0:2, :]
    stitch[1] = stats[2:4, :]
    for load, store, wide in zip(loads, stores, widen, strict=True):
        load.wait()
        if wide is not None:
            src, dst, some = wide
            dst[some, :] = src[some, :].astype(F32)
        store.start()
    for copy in stores:
        copy.wait()


def fused(
    pool_a, pool_b, weight_a, weight_b, bias_a, bias_b, stitch, crop_count, row_mask, outgrad_a, outgrad_b
):
    rows, width = pool_a.shape
    chl = bias_a.shape[0]
    NS, L = SUBS, 4
    SB, HB, PB = rows // NS, rows // 2, rows // PIECES
    NCH = chl // LANE
    hbm = pl.BlockSpec(memory_space=pl.ANY)
    vmem = pl.BlockSpec(memory_space=pltpu.VMEM)
    dma = pltpu.SemaphoreType.DMA
    out_shape = (
        jax.ShapeDtypeStruct((rows, chl), BF16),
        jax.ShapeDtypeStruct((rows, chl), BF16),
        jax.ShapeDtypeStruct((rows, width), BF16),
        jax.ShapeDtypeStruct((rows, width), BF16),
        jax.ShapeDtypeStruct((width, 2 * chl), BF16),
        jax.ShapeDtypeStruct((width, 2 * chl), BF16),
        jax.ShapeDtypeStruct((8, LANE), F32),
    )
    results = out_shape[:4] + (jax.ShapeDtypeStruct((width, 2 * chl), F32),) * 2
    scratch = [
        pltpu.VMEM((2, HB, width), BF16),
        pltpu.VMEM((2, width, rows), BF16),
        pltpu.VMEM((2, width, L * LANE), BF16),
        pltpu.VMEM((L, width, 2 * LANE), BF16),
        pltpu.VMEM((2, L, HB, LANE), BF16),
        pltpu.VMEM((2, 2, L, rows, LANE), BF16),
        pltpu.VMEM((2, 2, L, rows, LANE), BF16),
        pltpu.VMEM((2, 2, 3, rows, LANE), BF16),
        pltpu.VMEM((4, L, 2, rows, LANE), BF16),
        pltpu.VMEM((2, rows, width), F32),
        pltpu.VMEM((2, 2, width, LANE), BF16),
        pltpu.VMEM((2, 2, 2, width, LANE), BF16),
        pltpu.VMEM((2, 2, 3, width, LANE), BF16),
        pltpu.VMEM((2, width, LANE), F32),
        pltpu.VMEM((2, 2, width, LANE), BF16),
        pltpu.VMEM((2, rows, LANE), BF16),
        pltpu.VMEM((rows // LANE, LANE), F32),
        pltpu.VMEM((2 * NCH, 8, LANE), F32),
        pltpu.VMEM((rows, LANE), BF16),
        pltpu.VMEM((2, 2, SB, LANE), BF16),
        pltpu.VMEM((2 * NCH, 3, 8, LANE), F32),
        pltpu.VMEM((NCH, 8, LANE), F32),
        pltpu.VMEM((3, 8, LANE), F32),
        dma((2,)),
        dma((2, L)),
        dma((L, 2)),
        dma((L,)),
        dma((L,)),
        dma((2, NS, L)),
        dma((2, NS, L, 2)),
        dma((2, NS, L)),
        dma((2, NS, L, 2)),
        dma((2, 3)),
        dma((2, 2, 3)),
        dma((2, 2)),
        dma((2,)),
        dma((2, 2)),
        dma((PIECES,)),
        dma((3,)),
        dma((3,)),
        pltpu.SemaphoreType.REGULAR((3,)),
        pltpu.SemaphoreType.REGULAR((2,)),
    ]
    mixed_a, mixed_b, pg_a, pg_b, wg_a, wg_b, stats = pl.pallas_call(
        functools.partial(kernel, rows, width, chl),
        out_shape=out_shape,
        in_specs=[hbm] * 4 + [vmem] * 5 + [hbm] * 2,
        out_specs=(hbm, hbm, hbm, hbm, hbm, hbm, vmem),
        scratch_shapes=scratch,
        compiler_params=pltpu.CompilerParams(
            collective_id=0, has_side_effects=True, vmem_limit_bytes=VMEM_LIMIT
        ),
    )(
        pool_a,
        pool_b,
        weight_a,
        weight_b,
        bias_a[None],
        bias_b[None],
        stitch,
        row_mask.reshape(rows // LANE, LANE),
        crop_count.reshape(rows // LANE, LANE),
        outgrad_a,
        outgrad_b,
    )
    outs = pl.pallas_call(
        hand_over,
        out_shape=results
        + (
            jax.ShapeDtypeStruct((1, LANE), F32),
            jax.ShapeDtypeStruct((1, LANE), F32),
            jax.ShapeDtypeStruct((2, 2, LANE), F32),
        ),
        in_specs=[hbm] * 6 + [vmem],
        out_specs=(hbm,) * 6 + (vmem,) * 3,
        scratch_shapes=[pltpu.VMEM(out.shape, out.dtype) for out in out_shape[4:6] + results] + [dma((6, COPIES))] * 2,
        compiler_params=pltpu.CompilerParams(vmem_limit_bytes=VMEM_LIMIT),
    )(mixed_a, mixed_b, pg_a, pg_b, wg_a, wg_b, stats)
    return (*outs[:6], outs[6][0], outs[7][0], outs[8])


VMEM_LIMIT = 63 * 1024 * 1024


def plain(
    pool_a, pool_b, weight_a, weight_b, bias_a, bias_b, stitch, crop_count, row_mask, outgrad_a, outgrad_b
):
    row = (row_mask.astype(F32) / crop_count.astype(F32))[:, None]

    def pre(pool, weight, bias):
        partial = dot(pool, weight).astype(BF16)
        return lax.psum_scatter(partial, "feat", scatter_dimension=1, tiled=True).astype(F32) + bias

    def gelu(v):
        cdf = 0.5 * (1.0 + lax.erf(v * INV_SQRT2))
        return v * cdf, cdf + v * (INV_SQRT_2PI * jnp.exp(-0.5 * v * v))

    act_a, slope_a = gelu(pre(pool_a, weight_a, bias_a))
    act_b, slope_b = gelu(pre(pool_b, weight_b, bias_b))
    (s00, s01), (s10, s11) = stitch[0], stitch[1]
    mixed_a = (row * (s00 * act_a + s01 * act_b)).astype(BF16)
    mixed_b = (row * (s10 * act_a + s11 * act_b)).astype(BF16)
    gy_a = row * outgrad_a.astype(F32)
    gy_b = row * outgrad_b.astype(F32)
    gpre_a = ((s00 * gy_a + s10 * gy_b) * slope_a).astype(BF16)
    gpre_b = ((s01 * gy_a + s11 * gy_b) * slope_b).astype(BF16)
    sums = jnp.stack(
        [
            jnp.sum(v, axis=0)
            for v in (
                gy_a * act_a,
                gy_a * act_b,
                gy_b * act_a,
                gy_b * act_b,
                gpre_a.astype(F32),
                gpre_b.astype(F32),
            )
        ]
    )
    sums = lax.psum_scatter(sums, "rows", scatter_dimension=1, tiled=True)

    def back(pool, weight, gpre):
        whole = lax.all_gather(gpre, "feat", axis=1, tiled=True)
        pool_grad = dot_t(whole, weight).astype(BF16)
        wgrad = lax.dot_general(pool, whole, (((0,), (0,)), ((), ())), preferred_element_type=F32)
        wgrad = lax.psum_scatter(wgrad.astype(BF16), "rows", scatter_dimension=1, tiled=True)
        return pool_grad, wgrad.astype(F32)

    pg_a, wg_a = back(pool_a, weight_a, gpre_a)
    pg_b, wg_b = back(pool_b, weight_b, gpre_b)
    return mixed_a, mixed_b, pg_a, pg_b, wg_a, wg_b, sums[4], sums[5], sums[:4].reshape(2, 2, -1)


def shards(
    pool_a, pool_b, weight_a, weight_b, bias_a, bias_b, stitch, crop_count, row_mask, outgrad_a, outgrad_b
):
    rows, width = pool_a.shape
    chl = bias_a.shape[0]
    n_rows, n_feat = lax.axis_size("rows"), lax.axis_size("feat")
    fits = (
        n_rows == 4
        and n_feat == 8
        and chl == n_rows * LANE
        and width % LANE == 0
        and rows % (2 * SUBS * LANE) == 0
    )
    run = fused if fits else plain
    return run(pool_a, pool_b, weight_a, weight_b, bias_a, bias_b, stitch, crop_count, row_mask, outgrad_a, outgrad_b)


def solution(mesh):
    return jax.shard_map(
        shards,
        mesh=mesh,
        in_specs=(
            P("rows", "feat"),
            P("rows", "feat"),
            P("feat", None),
            P("feat", None),
            P("feat"),
            P("feat"),
            P(None, None, "feat"),
            P("rows"),
            P("rows"),
            P("rows", "feat"),
            P("rows", "feat"),
        ),
        out_specs=(
            P("rows", "feat"),
            P("rows", "feat"),
            P("rows", "feat"),
            P("rows", "feat"),
            P("feat", "rows"),
            P("feat", "rows"),
            P(("feat", "rows")),
            P(("feat", "rows")),
            P(None, None, ("feat", "rows")),
        ),
        check_vma=False,
    )
```

```python
import functools

import jax
import jax.numpy as jnp
from jax import lax
from jax.experimental import pallas as pl
from jax.experimental.pallas import tpu as pltpu
from jax.sharding import PartitionSpec as P

MESH = pl.DeviceIdType.MESH
F32 = jnp.float32
BF16 = jnp.bfloat16
LANE = 128
HALF = 64
SUBS = 5
PIECES = 4
COPIES = 4
RIGHT, LEFT = 0, 1
FAR, NEAR, KEEP, OWN = 0, 1, 2, 3
INV_SQRT2 = 0.7071067811865476
INV_SQRT_2PI = 0.3989422804014327


def dot(lhs, rhs):
    return lax.dot_general(lhs, rhs, (((1,), (0,)), ((), ())), preferred_element_type=F32)


def dot_t(lhs, rhs):
    return lax.dot_general(lhs, rhs, (((1,), (1,)), ((), ())), preferred_element_type=F32)


def swap(v):
    return pltpu.roll(v, HALF, 1)


def upper(rows):
    return lax.broadcasted_iota(jnp.int32, (rows, LANE), 1) >= HALF


def halves(one, two, half):
    if half == 0:
        return jnp.where(upper(one.shape[0]), swap(two), one)
    return jnp.where(upper(one.shape[0]), two, swap(one))


def kernel(rows, width, chl, *refs):
    (
        pool_a, pool_b, weight_a, weight_b, bias_a, bias_b, stitch, mask, count, og_a, og_b,
        mixed_a, mixed_b, pg_a, pg_b, wg_a, wg_b, stats,
        pool_0, pool_1, pool_t, wf, wb, part_0, part_1, part_own, xr, rbuf, gath, acc, wsend, wkeep, wrecv, wout_0, wout,
        og_v, scale, par, mix_0, mix_v, sacc, sred, srecv,
        pool_s, wf_s, wb_s, xs_send, xs_recv, x0_send, x0_recv, z_send, z_recv, g_send, g_recv,
        w_send, w_recv, wout_s, og_s, mix_s, pg_s, st_send, st_recv, credit, wcredit,
    ) = refs
    L = 4
    NS = SUBS
    SB = rows // NS
    BIG, SMALL = rows * 3 // 10, rows // 5
    PB = rows // PIECES
    NCH = chl // LANE
    U = 2 * NCH
    SENDING = U + 3
    TICKS = (U + 5) * L
    pools, weights = (pool_a, pool_b), (weight_a, weight_b)
    ogs, mixeds = (og_a, og_b), (mixed_a, mixed_b)
    pgs, wgs = (pg_a, pg_b), (wg_a, wg_b)

    f = lax.axis_index("feat")
    r = lax.axis_index("rows")
    p = lax.div(f, 2)
    c = lax.rem(f, 2)
    sib = f + 1 - 2 * c
    xp = r + 1 - 2 * lax.rem(r, 2)
    yp = lax.rem(r + 2, 4)
    dp = 3 - r
    has_left, has_right = p > 0, p < L - 1
    pos = (p, L - 1 - p)
    has_up = (has_left, has_right)
    nxt = (f + 2, f - 2)

    def remote(src, dst, send, recv, **dev):
        return pltpu.make_async_remote_copy(
            src_ref=src, dst_ref=dst, send_sem=send, recv_sem=recv, device_id=dev, device_id_type=MESH
        )

    def signal(sem, **dev):
        pl.semaphore_signal(sem, inc=1, device_id=dev, device_id_type=MESH)

    def start_all(copies):
        for copy in copies:
            copy.start()

    def wait_all(copies):
        for copy in copies:
            copy.wait()

    def lanes(index):
        return pl.ds(pl.multiple_of(index * LANE, LANE), LANE)

    def some_rows(i, n):
        return pl.ds(pl.multiple_of(i * n, n), n)

    def sub_rows(b):
        return pl.ds(b * SB, SB)

    def tower_of(index, run):
        for t in range(2):

            @pl.when(lax.rem(index, 2) == t)
            def _():
                run(t)

    sizes, pool_v, part_v = (BIG, SMALL), (pool_0, pool_1), (part_0, part_1)

    def piece_rows(s, k):
        return pl.ds(pl.multiple_of(lax.div(s, 2) * (BIG + SMALL) + k * BIG, LANE), sizes[k])

    def pool_loads(s, k):
        return [
            pltpu.make_async_copy(pools[t].at[piece_rows(s, k), :], pool_v[k].at[t], pool_s.at[k, t])
            for t in range(2)
        ]

    def wf_loads(per):
        j = lax.div(per, 2)
        core = jnp.where(lax.rem(per, 2) == 0, c, 1 - c)
        return [
            pltpu.make_async_copy(
                weights[t].at[:, lanes((2 * q + core) * NCH + j)],
                wf.at[t, :, q * LANE : (q + 1) * LANE],
                wf_s.at[t, q],
            )
            for t in range(2)
            for q in range(L)
        ]

    def wb_loads(j, t):
        out = []
        for q in range(L):
            for k in range(2):
                out.append(
                    pltpu.make_async_copy(
                        weights[t].at[:, lanes((2 * q + k) * NCH + j)],
                        wb.at[q, :, k * LANE : (k + 1) * LANE],
                        wb_s.at[q, k],
                    )
                )
        return out

    def og_loads(j):
        return [pltpu.make_async_copy(ogs[t].at[:, lanes(j)], og_v.at[t], og_s.at[t]) for t in range(2)]

    def mix_stores(j, b):
        return [
            pltpu.make_async_copy(mix_v.at[b % 2, t], mixeds[t].at[sub_rows(b), lanes(j)], mix_s.at[b % 2, t])
            for t in range(2)
        ]

    def part_copy(j, s, k):
        return remote(
            part_v[k],
            xr.at[lax.rem(j, 2), :, :, piece_rows(s, k), :],
            xs_send.at[s],
            xs_recv.at[s],
            feat=sib,
        )

    def first_copy(h, s, k):
        return remote(
            part_v[k].at[lax.div(s, 2)],
            xr.at[0, h, :, piece_rows(s, k), :],
            x0_send.at[h, s],
            x0_recv.at[h, s],
            feat=sib,
        )

    def share_copy(u, o, core, d, b, s, par2):
        block = gath.at[lax.rem(u, 4), o, core, sub_rows(b), :]
        return remote(block, block, g_send.at[d, b, s], g_recv.at[d, b, s, par2], feat=sib)

    def gath_copy(u, o, d, b, s, par2):
        block = gath.at[lax.rem(u, 4), o, c, sub_rows(b), :]
        return remote(block, block, z_send.at[d, b, s], z_recv.at[d, b, s, par2], feat=nxt[d])

    def sum_block(u, d, b, s):
        return rbuf.at[lax.rem(u, 2), d, lax.rem(s, 3), sub_rows(b), :]

    def sum_copy(u, d, b, s, par2):
        return remote(
            sum_block(u, d, b, s - 1),
            sum_block(u, d, b, s),
            z_send.at[d, b, s],
            z_recv.at[d, b, s, par2],
            feat=nxt[d],
        )

    def sum_wait(u, d, b, s, par2):
        block = sum_block(u, d, b, s)
        remote(block, block, z_send.at[d, b, s], z_recv.at[d, b, s, par2], feat=nxt[d]).wait_recv()

    def packed(one, two, h):
        return jnp.where(upper(one.shape[0]) == (h == 1), one, swap(two))

    def own_sum(u, o, b):
        h, j2 = lax.rem(u, 2), lax.rem(lax.div(u, 2), 2)
        return part_own[j2, h, o, sub_rows(b), :].astype(F32) + xr[j2, h, o, sub_rows(b), :].astype(F32)

    def fold(v):
        return jnp.sum(v.reshape(SB // 8, 8, LANE), axis=0)

    def finalize(u, b, per):
        j, h = lax.div(u, 2), lax.rem(u, 2)
        last2 = lax.rem(per - 1, 2)
        for d in (RIGHT, LEFT):

            @pl.when(has_up[d])
            def _():
                sum_wait(u, d, b, L - 1, last2)

        if b == 0:

            @pl.when(h == 0)
            def _():
                wait_all(og_loads(j))

        v = own_sum(u, p, b) + par[u, 3:4, :]
        for d in (RIGHT, LEFT):
            v = v + jnp.where(has_up[d], rbuf[lax.rem(u, 2), d, 0, sub_rows(b), :].astype(F32), 0.0)
        same, cross, back = (par[u, k : k + 1, :] for k in range(3))
        row = jnp.concatenate(
            [jnp.broadcast_to(scale[k : k + 1, :], (LANE, LANE)).T for k in range(b * SB // LANE, (b + 1) * SB // LANE)],
            axis=0,
        )
        gy = row * packed(og_v[h, sub_rows(b), :].astype(F32), og_v[1 - h, sub_rows(b), :].astype(F32), h)
        cdf = 0.5 * (1.0 + lax.erf(v * INV_SQRT2))
        act = v * cdf
        slope = cdf + v * (INV_SQRT_2PI * jnp.exp(-0.5 * v * v))
        act_x = swap(act)
        mixed = row * (same * act + cross * act_x)
        gpre = ((same * gy + back * swap(gy)) * slope).astype(BF16)
        gath[lax.rem(u, 4), p, c, sub_rows(b), :] = gpre
        sacc[u, 0] += fold(gy * act)
        sacc[u, 1] += fold(gy * act_x)
        sacc[u, 2] += fold(gpre.astype(F32))

        @pl.when(h == 0)
        def _():
            mix_0[sub_rows(b), :] = mixed.astype(BF16)

        @pl.when(h == 1)
        def _():
            if b > 1:
                wait_all(mix_stores(j, b))
            else:

                @pl.when(j >= 1)
                def _():
                    wait_all(mix_stores(j, b))

            first, second = mix_0[sub_rows(b), :], mixed.astype(BF16)
            for t in range(2):
                mix_v[b % 2, t] = halves(first, second, t)
            start_all(mix_stores(j, b))

    first_partner, second_partner = (xp, yp), (yp, xp)

    def w_copy(u, t, kind):
        u2 = lax.rem(u, 2)
        return remote(
            wkeep.at[u2, t, 0] if kind == KEEP else wsend.at[t, kind],
            wrecv.at[u2, t, kind],
            w_send.at[t, kind],
            w_recv.at[u2, t, kind],
            rows=second_partner[t] if kind == KEEP else first_partner[t],
        )

    def wout_stores(j, t):
        return [
            pltpu.make_async_copy(wout.at[t, k], wgs[t].at[:, lanes(k * NCH + j)], wout_s.at[t, k])
            for k in range(2)
        ]

    def pg_store(t, i):
        place = pool_0.at[lax.rem(i, 2), pl.ds(0, PB), :]
        return pltpu.make_async_copy(place, pgs[t].at[some_rows(i, PB), :], pg_s.at[lax.rem(i, 2)])

    def row_products(u, t, one, two):
        cols = []
        for owner in (one, two):
            pair = [gath[lax.rem(u, 4), owner, core] for core in range(2)]
            cols.append(halves(pair[0], pair[1], t))
        return dot(pool_t[t], jnp.concatenate(cols, axis=1)).astype(BF16)

    def pool_products(j, t, i):
        mine = some_rows(i, PB)
        total = None
        for q in range(L):
            cols = []
            for core in range(2):
                pair = [gath[lax.rem(2 * j + h, 4), q, core, mine, :] for h in range(2)]
                cols.append(halves(pair[0], pair[1], t))
            term = dot_t(jnp.concatenate(cols, axis=1), wb[q])
            total = term if total is None else total + term

        @pl.when(j == 0)
        def _():
            acc[t, mine, :] = total

        @pl.when((j > 0) & (j < NCH - 1))
        def _():
            acc[t, mine, :] += total

        @pl.when(j == NCH - 1)
        def _():
            if t > 0:
                pg_store(t, i).wait()
            else:

                @pl.when(i >= 2)
                def _():
                    pg_store(t, i).wait()

            pool_0[lax.rem(i, 2), pl.ds(0, PB), :] = (acc[t, mine, :] + total).astype(BF16)
            pg_store(t, i).start()

    def first_weights():
        out = wf_loads(0)
        for t in range(2):
            for q in range(L):
                tile, k = 2 * t + q // 2, q % 2
                out.append(
                    pltpu.make_async_copy(
                        weights[t].at[:, lanes((2 * q + 1 - c) * NCH)],
                        wb.at[tile, :, k * LANE : (k + 1) * LANE],
                        wb_s.at[tile, k],
                    )
                )
        return out

    start_all(first_weights())
    start_all(pool_loads(0, 0))
    start_all(pool_loads(1, 1))

    bar = pltpu.get_barrier_semaphore()

    @pl.when(has_left)
    def _():
        signal(bar, feat=f - 2)

    @pl.when(has_right)
    def _():
        signal(bar, feat=f + 2)

    signal(bar, feat=sib)
    signal(bar, rows=xp)
    signal(bar, rows=yp)
    signal(bar, rows=dp)
    sacc[...] = jnp.zeros_like(sacc)
    scale[...] = mask[...].astype(F32) / count[...].astype(F32)
    for u in range(U):
        ch = slice(u // 2 * LANE, (u // 2 + 1) * LANE)
        s00, s01, s10, s11 = (stitch[k // 2, k % 2 : k % 2 + 1, ch] for k in range(4))
        rows_of = (s00, s11), (s01, s10), (s10, s01), (bias_a[:, ch], bias_b[:, ch])
        for k, (one, two) in enumerate(rows_of):
            par[u, k : k + 1, :] = halves(one, two, u % 2)

    def first_tiles(h):
        for t in range(2):
            for q in range(L):
                mine = wf[t, :, q * LANE : (q + 1) * LANE]
                other = wb[2 * t + q // 2, :, q % 2 * LANE : (q % 2 + 1) * LANE]
                gath[3 - h, q, t, :width, :] = halves(mine, other, h)

    def first_products(h, s, k, slot):
        res = []
        for t in range(2):
            cols = jnp.concatenate([gath[3 - h, q, t, :width, :] for q in range(L)], axis=1)
            res.append(dot(pool_v[k][t], cols).astype(BF16))
        for q in range(L):
            both = [v[:, q * LANE : (q + 1) * LANE] for v in res]
            part_own[0, h, q, piece_rows(s, k), :] = halves(*both, 0)
            part_v[k][slot, q] = halves(*both, 1)

    wait_all(first_weights())
    first_tiles(0)
    for s in range(L):
        k = s % 2
        wait_all(pool_loads(s, k))
        first_products(0, s, k, s // 2)
        if s < 3:
            start_all(pool_loads((s + 2) % L, k))
        if s == 0:
            pl.semaphore_wait(bar, 4 + has_left.astype(jnp.int32) + has_right.astype(jnp.int32))
        first_copy(0, s, k).start()
    first_tiles(1)
    start_all(wf_loads(2))
    for s in range(L):
        first_copy(0, s, s % 2).wait_recv()
    for d in (RIGHT, LEFT):
        @pl.when(pos[d] == 0)
        def _():
            for b in range(NS):
                sum_block(0, d, b, 0)[...] = own_sum(0, p + (L - 1) * (1 - 2 * d), b).astype(BF16)
                sum_copy(0, d, b, 1, 0).start()

    def tick(T, carry):
        per, s = lax.div(T, L), lax.rem(T, L)
        par2 = lax.rem(per, 2)
        u = per - 3
        ur = per - 2
        gathers = (u >= 0) & (u < U)
        sums = (ur >= 0) & (ur < U)

        @pl.when((s == 0) & (per >= 3) & (per < SENDING))
        def _():
            @pl.when(has_left)
            def _():
                pl.semaphore_wait(credit.at[0], 1)

            @pl.when(has_right)
            def _():
                pl.semaphore_wait(credit.at[1], 1)

            pl.semaphore_wait(credit.at[2], 1)

        @pl.when((s == 1) & sums & (par2 == 0))
        def _():
            @pl.when(ur > 0)
            def _():
                for k in range(L):
                    part_copy(lax.div(ur, 2), k, k % 2).wait_recv()

            start_all(og_loads(lax.div(ur, 2)))

        @pl.when(T == 3 * L + 1)
        def _():
            for k in range(L):
                first_copy(1, k, k % 2).wait_recv()

        before = T - 1 + L
        per_m, s_m = lax.div(before, L) - 1, lax.rem(before, L)
        par_m = lax.rem(per_m + 2, 2)
        u_m, ur_m = per_m - 3, per_m - 2
        gathers_m = (u_m >= 0) & (u_m < U)
        sums_m = (ur_m >= 0) & (ur_m < U)
        ub = per - 4
        uz = per - 5
        jp = lax.div(jnp.maximum(per - 5, 0), 2)

        def flows(b):
            @pl.when((s == 0) & gathers)
            def _():
                finalize(u, b, per)

            for d in (RIGHT, LEFT):
                gather_here = pos[d] >= s
                o = p - s if d == RIGHT else p + s
                dest = p + (L - s) if d == RIGHT else p - (L - s)
                shares = (s >= 1) if d == LEFT else (s >= 0)

                @pl.when(gathers & gather_here)
                def _():
                    @pl.when(s >= 1)
                    def _():
                        gath_copy(u, o, d, b, s - 1, par2).wait_recv()

                    @pl.when(pos[d] < L - 1)
                    def _():
                        gath_copy(u, o, d, b, s, par2).start()

                    @pl.when(shares)
                    def _():
                        share_copy(u, o, c, d, b, s, par2).start()

                begun = (ur == 0) & (s == 1)

                @pl.when(sums & jnp.logical_not(gather_here | begun))
                def _():
                    block = sum_block(ur, d, b, s - 1)

                    @pl.when(pos[d] >= 1)
                    def _():
                        sum_wait(ur, d, b, s - 1, par2)
                        block[...] = (own_sum(ur, dest, b) + block[...].astype(F32)).astype(BF16)

                    @pl.when(pos[d] < 1)
                    def _():
                        block[...] = own_sum(ur, dest, b).astype(BF16)

                    sum_copy(ur, d, b, s, par2).start()

        def share_waits():
            for b in range(NS):
                for d in (RIGHT, LEFT):
                    o = p - s_m if d == RIGHT else p + s_m
                    shares = (s_m >= 1) if d == LEFT else (s_m >= 0)

                    @pl.when(gathers_m & (pos[d] >= s_m) & shares)
                    def _():
                        share_copy(u_m, o, 1 - c, d, b, s_m, par_m).wait_recv()

        def partial_products():
            @pl.when(per < U)
            def _():
                @pl.when(s == 0)
                def _():
                    wait_all(wf_loads(per))

                j = lax.div(per, 2)
                for k in range(2):

                    @pl.when(lax.rem(s, 2) == k)
                    def _():
                        wait_all(pool_loads(s, k))

                        @pl.when(per == 2)
                        def _():
                            first_copy(0, s, k).wait_send()
                            first_products(1, s, k, lax.div(s, 2))
                            first_copy(1, s, k).start()

                        @pl.when((per == 3) & (s < 2))
                        def _():
                            for i in range(2):
                                first_copy(1, s + 2 * i, k).wait_send()

                        @pl.when(T + 1 < U * L)
                        def _():
                            start_all(pool_loads(lax.rem(s + 1, L), 1 - k))

                        res = [dot(pool_v[k][t], wf[t]).astype(BF16) for t in range(2)]
                        for q in range(L):
                            both = [v[:, q * LANE : (q + 1) * LANE] for v in res]
                            for h in range(2):
                                block = halves(*both, h)

                                @pl.when(par2 == 0)
                                def _():
                                    part_own[lax.rem(j, 2), h, q, piece_rows(s, k), :] = block

                                @pl.when(par2 == 1)
                                def _():
                                    part_v[k][h, q] = block

                        @pl.when(par2 == 1)
                        def _():
                            part_copy(j, s, k).start()

                        @pl.when(per == 2)
                        def _():
                            for t in range(2):
                                pool_t[t, :, piece_rows(s, k)] = pool_v[k][t].T

                @pl.when((s == L - 1) & (per + 1 < U))
                def _():
                    start_all(wf_loads(per + 1))

        def weight_products(t):
            @pl.when((s == 0) & (ub >= 0) & (ub < U))
            def _():
                if t == 0:

                    @pl.when(ub >= 2)
                    def _():
                        pl.semaphore_wait(wcredit.at[0], 1)
                        pl.semaphore_wait(wcredit.at[1], 1)

                res = row_products(ub, t, dp, first_partner[t])
                for kind in (FAR, NEAR):
                    wsend[t, kind] = res[:, kind * LANE : (kind + 1) * LANE]
                w_copy(ub, t, FAR).start()

            @pl.when((s == 1) & (ub >= 0) & (ub < U))
            def _():
                res = row_products(ub, t, second_partner[t], r)
                for k in range(2):
                    wkeep[lax.rem(ub, 2), t, k] = res[:, k * LANE : (k + 1) * LANE]

        def pool_piece(k):
            @pl.when((per >= 5) & (par2 == 1) & (s >= 2))
            def _():
                if k == 0:

                    @pl.when(s == 2)
                    def _():
                        wait_all(wb_loads(jp, 0))

                pool_products(jp, 0, 2 * (s - 2) + k)
                if k == 1:

                    @pl.when(s == 3)
                    def _():
                        start_all(wb_loads(jp, 1))

            @pl.when((per >= 6) & (par2 == 0) & ((s == 1) | (s == 2)))
            def _():
                if k == 0:

                    @pl.when(s == 1)
                    def _():
                        wait_all(wb_loads(jp, 1))

                pool_products(jp, 1, 2 * (s - 1) + k)

        def send_near():
            @pl.when((s == 2) & (ub >= 0) & (ub < U))
            def _():
                for t in range(2):
                    w_copy(ub, t, NEAR).start()

        def finish_weights():
            @pl.when((s == 2) & (uz >= 0) & (uz < U))
            def _():
                j, h, u2 = lax.div(uz, 2), lax.rem(uz, 2), lax.rem(uz, 2)
                for t in range(2):
                    w_copy(uz, t, NEAR).wait_recv()
                    w_copy(uz, t, KEEP).wait_recv()
                    w_copy(uz, t, KEEP).wait_send()
                    both = wkeep[u2, t, 1].astype(F32) + wrecv[u2, t, NEAR].astype(F32)
                    both = both + wrecv[u2, t, KEEP].astype(F32)

                    @pl.when(h == 0)
                    def _():
                        @pl.when(j >= 1)
                        def _():
                            wait_all(wout_stores(j, t))

                        wout_0[t] = both

                    @pl.when(h == 1)
                    def _():
                        for k in range(2):
                            wout[t, k] = halves(wout_0[t], both, k).astype(BF16)
                        start_all(wout_stores(j, t))

                @pl.when(uz < U - 2)
                def _():
                    signal(wcredit.at[0], rows=xp)
                    signal(wcredit.at[1], rows=yp)

            @pl.when((s == 3) & (ub >= 0) & (ub < U))
            def _():
                u2 = lax.rem(ub, 2)
                for t in range(2):
                    w_copy(ub, t, FAR).wait_recv()
                    both = wkeep[u2, t, 0].astype(F32) + wrecv[u2, t, FAR].astype(F32)
                    wkeep[u2, t, 0] = both.astype(BF16)
                    w_copy(ub, t, KEEP).start()

        @pl.when((s == 0) & (uz >= 0) & (uz < U))
        def _():
            for t in range(2):
                for kind in (FAR, NEAR):
                    w_copy(uz, t, kind).wait_send()

        @pl.when((s == 0) & (per >= 5) & (par2 == 1))
        def _():
            start_all(wb_loads(jp, 0))

        flows(0)
        share_waits()
        weight_products(0)
        flows(1)
        pool_piece(0)
        flows(2)
        send_near()
        weight_products(1)
        flows(3)
        pool_piece(1)
        flows(4)
        partial_products()
        finish_weights()

        for k in range(2):

            @pl.when((per_m >= 3) & (per_m < U) & (par_m == 1) & (lax.rem(s_m, 2) == k))
            def _():
                part_copy(0, s_m, k).wait_send()

        for b in range(NS):
            for d in (RIGHT, LEFT):
                shares = (s_m >= 1) if d == LEFT else (s_m >= 0)

                @pl.when(gathers_m & (pos[d] >= s_m))
                def _():
                    @pl.when(pos[d] < L - 1)
                    def _():
                        gath_copy(u_m, p, d, b, s_m, par_m).wait_send()

                    @pl.when(shares)
                    def _():
                        share_copy(u_m, p, c, d, b, s_m, par_m).wait_send()

                @pl.when(sums_m & (pos[d] < s_m))
                def _():
                    sum_copy(ur_m, d, b, s_m, par_m).wait_send()

        @pl.when((s == 2) & (per < SENDING - 1))
        def _():
            @pl.when(has_left)
            def _():
                signal(credit.at[1], feat=f - 2)

            @pl.when(has_right)
            def _():
                signal(credit.at[0], feat=f + 2)

            signal(credit.at[2], feat=sib)

        @pl.when(T == (U + 2) * L + 1)
        def _():
            for j in range(NCH):
                sums_of = [[jnp.sum(sacc[2 * j + h, k], axis=0, keepdims=True) for h in range(2)] for k in range(3)]
                (same, cross, bias) = sums_of
                rows_of = [halves(*same, 0), halves(*cross, 0), halves(*cross, 1), halves(*same, 1)]
                rows_of += [halves(*bias, 0), halves(*bias, 1), jnp.zeros((2, LANE), F32)]
                sred[j] = jnp.concatenate(rows_of, axis=0)
            for k, peer in enumerate((xp, yp, dp)):
                remote(sred.at[peer], srecv.at[k], st_send.at[k], st_recv.at[k], rows=peer).start()

        return carry

    lax.fori_loop(2 * L, TICKS, tick, 0)

    for k, peer in enumerate((xp, yp, dp)):
        copy = remote(sred.at[peer], srecv.at[k], st_send.at[k], st_recv.at[k], rows=peer)
        copy.wait_send()
        copy.wait_recv()
    stats[...] = sred[r] + srecv[0] + srecv[1] + srecv[2]
    for b in range(2):
        wait_all(mix_stores(NCH - 1, b))
    for t in range(2):
        wait_all(wout_stores(NCH - 1, t))
    for i in range(2):
        pg_store(1, i).wait()


def hand_over(*refs):
    sources, stats, results = refs[:6], refs[6], refs[7:13]
    bias_a, bias_b, stitch = refs[13:16]
    low, held, (load_s, store_s) = refs[16:18], refs[18:24], refs[24:]
    loads, stores, widen = [], [], []
    for k in (4, 0, 2, 5, 1, 3):
        n = results[k].shape[0] // COPIES
        for i in range(COPIES):
            some = pl.ds(i * n, n)
            via = low[k - 4] if k >= 4 else held[k]
            loads.append(pltpu.make_async_copy(sources[k].at[some, :], via.at[some, :], load_s.at[k, i]))
            stores.append(pltpu.make_async_copy(held[k].at[some, :], results[k].at[some, :], store_s.at[k, i]))
            widen.append((via, held[k], some) if k >= 4 else None)
    for copy in loads:
        copy.start()
    bias_a[...] = stats[4:5, :]
    bias_b[...] = stats[5:6, :]
    stitch[0] = stats[0:2, :]
    stitch[1] = stats[2:4, :]
    for load, store, wide in zip(loads, stores, widen, strict=True):
        load.wait()
        if wide is not None:
            src, dst, some = wide
            dst[some, :] = src[some, :].astype(F32)
        store.start()
    for copy in stores:
        copy.wait()


def fused(
    pool_a, pool_b, weight_a, weight_b, bias_a, bias_b, stitch, crop_count, row_mask, outgrad_a, outgrad_b
):
    rows, width = pool_a.shape
    chl = bias_a.shape[0]
    NS, L = SUBS, 4
    BIG, SMALL = rows * 3 // 10, rows // 5
    NCH = chl // LANE
    hbm = pl.BlockSpec(memory_space=pl.ANY)
    vmem = pl.BlockSpec(memory_space=pltpu.VMEM)
    dma = pltpu.SemaphoreType.DMA
    out_shape = (
        jax.ShapeDtypeStruct((rows, chl), BF16),
        jax.ShapeDtypeStruct((rows, chl), BF16),
        jax.ShapeDtypeStruct((rows, width), BF16),
        jax.ShapeDtypeStruct((rows, width), BF16),
        jax.ShapeDtypeStruct((width, 2 * chl), BF16),
        jax.ShapeDtypeStruct((width, 2 * chl), BF16),
        jax.ShapeDtypeStruct((8, LANE), F32),
    )
    results = out_shape[:4] + (jax.ShapeDtypeStruct((width, 2 * chl), F32),) * 2
    scratch = [
        pltpu.VMEM((2, BIG, width), BF16),
        pltpu.VMEM((2, SMALL, width), BF16),
        pltpu.VMEM((2, width, rows), BF16),
        pltpu.VMEM((2, width, L * LANE), BF16),
        pltpu.VMEM((L, width, 2 * LANE), BF16),
        pltpu.VMEM((2, L, BIG, LANE), BF16),
        pltpu.VMEM((2, L, SMALL, LANE), BF16),
        pltpu.VMEM((2, 2, L, rows, LANE), BF16),
        pltpu.VMEM((2, 2, L, rows, LANE), BF16),
        pltpu.VMEM((2, 2, 3, rows, LANE), BF16),
        pltpu.VMEM((4, L, 2, rows, LANE), BF16),
        pltpu.VMEM((2, rows, width), F32),
        pltpu.VMEM((2, 2, width, LANE), BF16),
        pltpu.VMEM((2, 2, 2, width, LANE), BF16),
        pltpu.VMEM((2, 2, 3, width, LANE), BF16),
        pltpu.VMEM((2, width, LANE), F32),
        pltpu.VMEM((2, 2, width, LANE), BF16),
        pltpu.VMEM((2, rows, LANE), BF16),
        pltpu.VMEM((rows // LANE, LANE), F32),
        pltpu.VMEM((2 * NCH, 8, LANE), F32),
        pltpu.VMEM((rows, LANE), BF16),
        pltpu.VMEM((2, 2, rows // NS, LANE), BF16),
        pltpu.VMEM((2 * NCH, 3, 8, LANE), F32),
        pltpu.VMEM((NCH, 8, LANE), F32),
        pltpu.VMEM((3, 8, LANE), F32),
        dma((2, 2)),
        dma((2, L)),
        dma((L, 2)),
        dma((L,)),
        dma((L,)),
        dma((2, L)),
        dma((2, L)),
        dma((2, NS, L)),
        dma((2, NS, L, 2)),
        dma((2, NS, L)),
        dma((2, NS, L, 2)),
        dma((2, 3)),
        dma((2, 2, 3)),
        dma((2, 2)),
        dma((2,)),
        dma((2, 2)),
        dma((2,)),
        dma((3,)),
        dma((3,)),
        pltpu.SemaphoreType.REGULAR((3,)),
        pltpu.SemaphoreType.REGULAR((2,)),
    ]
    mixed_a, mixed_b, pg_a, pg_b, wg_a, wg_b, stats = pl.pallas_call(
        functools.partial(kernel, rows, width, chl),
        out_shape=out_shape,
        in_specs=[hbm] * 4 + [vmem] * 5 + [hbm] * 2,
        out_specs=(hbm, hbm, hbm, hbm, hbm, hbm, vmem),
        scratch_shapes=scratch,
        compiler_params=pltpu.CompilerParams(
            collective_id=0, has_side_effects=True, vmem_limit_bytes=VMEM_LIMIT
        ),
    )(
        pool_a,
        pool_b,
        weight_a,
        weight_b,
        bias_a[None],
        bias_b[None],
        stitch,
        row_mask.reshape(rows // LANE, LANE),
        crop_count.reshape(rows // LANE, LANE),
        outgrad_a,
        outgrad_b,
    )
    outs = pl.pallas_call(
        hand_over,
        out_shape=results
        + (
            jax.ShapeDtypeStruct((1, LANE), F32),
            jax.ShapeDtypeStruct((1, LANE), F32),
            jax.ShapeDtypeStruct((2, 2, LANE), F32),
        ),
        in_specs=[hbm] * 6 + [vmem],
        out_specs=(hbm,) * 6 + (vmem,) * 3,
        scratch_shapes=[pltpu.VMEM(out.shape, out.dtype) for out in out_shape[4:6] + results] + [dma((6, COPIES))] * 2,
        compiler_params=pltpu.CompilerParams(vmem_limit_bytes=VMEM_LIMIT),
    )(mixed_a, mixed_b, pg_a, pg_b, wg_a, wg_b, stats)
    return (*outs[:6], outs[6][0], outs[7][0], outs[8])


VMEM_LIMIT = 63 * 1024 * 1024


def plain(
    pool_a, pool_b, weight_a, weight_b, bias_a, bias_b, stitch, crop_count, row_mask, outgrad_a, outgrad_b
):
    row = (row_mask.astype(F32) / crop_count.astype(F32))[:, None]

    def pre(pool, weight, bias):
        partial = dot(pool, weight).astype(BF16)
        return lax.psum_scatter(partial, "feat", scatter_dimension=1, tiled=True).astype(F32) + bias

    def gelu(v):
        cdf = 0.5 * (1.0 + lax.erf(v * INV_SQRT2))
        return v * cdf, cdf + v * (INV_SQRT_2PI * jnp.exp(-0.5 * v * v))

    act_a, slope_a = gelu(pre(pool_a, weight_a, bias_a))
    act_b, slope_b = gelu(pre(pool_b, weight_b, bias_b))
    (s00, s01), (s10, s11) = stitch[0], stitch[1]
    mixed_a = (row * (s00 * act_a + s01 * act_b)).astype(BF16)
    mixed_b = (row * (s10 * act_a + s11 * act_b)).astype(BF16)
    gy_a = row * outgrad_a.astype(F32)
    gy_b = row * outgrad_b.astype(F32)
    gpre_a = ((s00 * gy_a + s10 * gy_b) * slope_a).astype(BF16)
    gpre_b = ((s01 * gy_a + s11 * gy_b) * slope_b).astype(BF16)
    sums = jnp.stack(
        [
            jnp.sum(v, axis=0)
            for v in (
                gy_a * act_a,
                gy_a * act_b,
                gy_b * act_a,
                gy_b * act_b,
                gpre_a.astype(F32),
                gpre_b.astype(F32),
            )
        ]
    )
    sums = lax.psum_scatter(sums, "rows", scatter_dimension=1, tiled=True)

    def back(pool, weight, gpre):
        whole = lax.all_gather(gpre, "feat", axis=1, tiled=True)
        pool_grad = dot_t(whole, weight).astype(BF16)
        wgrad = lax.dot_general(pool, whole, (((0,), (0,)), ((), ())), preferred_element_type=F32)
        wgrad = lax.psum_scatter(wgrad.astype(BF16), "rows", scatter_dimension=1, tiled=True)
        return pool_grad, wgrad.astype(F32)

    pg_a, wg_a = back(pool_a, weight_a, gpre_a)
    pg_b, wg_b = back(pool_b, weight_b, gpre_b)
    return mixed_a, mixed_b, pg_a, pg_b, wg_a, wg_b, sums[4], sums[5], sums[:4].reshape(2, 2, -1)


def shards(
    pool_a, pool_b, weight_a, weight_b, bias_a, bias_b, stitch, crop_count, row_mask, outgrad_a, outgrad_b
):
    rows, width = pool_a.shape
    chl = bias_a.shape[0]
    n_rows, n_feat = lax.axis_size("rows"), lax.axis_size("feat")
    fits = (
        n_rows == 4
        and n_feat == 8
        and chl == n_rows * LANE
        and width % LANE == 0
        and width <= rows
        and rows % (2 * SUBS * LANE) == 0
    )
    run = fused if fits else plain
    return run(pool_a, pool_b, weight_a, weight_b, bias_a, bias_b, stitch, crop_count, row_mask, outgrad_a, outgrad_b)


def solution(mesh):
    return jax.shard_map(
        shards,
        mesh=mesh,
        in_specs=(
            P("rows", "feat"),
            P("rows", "feat"),
            P("feat", None),
            P("feat", None),
            P("feat"),
            P("feat"),
            P(None, None, "feat"),
            P("rows"),
            P("rows"),
            P("rows", "feat"),
            P("rows", "feat"),
        ),
        out_specs=(
            P("rows", "feat"),
            P("rows", "feat"),
            P("rows", "feat"),
            P("rows", "feat"),
            P("feat", "rows"),
            P("feat", "rows"),
            P(("feat", "rows")),
            P(("feat", "rows")),
            P(None, None, ("feat", "rows")),
        ),
        check_vma=False,
    )
```

```python
import functools

import jax
import jax.numpy as jnp
from jax import lax
from jax.experimental import pallas as pl
from jax.experimental.pallas import tpu as pltpu
from jax.sharding import PartitionSpec as P

MESH = pl.DeviceIdType.MESH
F32 = jnp.float32
BF16 = jnp.bfloat16
LANE = 128
HALF = 64
SUBS = 5
PIECES = 4
COPIES = 4
RIGHT, LEFT = 0, 1
FAR, NEAR, KEEP, OWN = 0, 1, 2, 3
INV_SQRT2 = 0.7071067811865476
INV_SQRT_2PI = 0.3989422804014327


def dot(lhs, rhs):
    return lax.dot_general(lhs, rhs, (((1,), (0,)), ((), ())), preferred_element_type=F32)


def dot_t(lhs, rhs):
    return lax.dot_general(lhs, rhs, (((1,), (1,)), ((), ())), preferred_element_type=F32)


def swap(v):
    return pltpu.roll(v, HALF, 1)


def upper(rows):
    return lax.broadcasted_iota(jnp.int32, (rows, LANE), 1) >= HALF


def halves(one, two, half):
    if half == 0:
        return jnp.where(upper(one.shape[0]), swap(two), one)
    return jnp.where(upper(one.shape[0]), two, swap(one))


def kernel(rows, width, chl, *refs):
    (
        pool_a, pool_b, weight_a, weight_b, bias_a, bias_b, stitch, mask, count, og_a, og_b,
        mixed_a, mixed_b, acc, wg_a, wg_b, stats,
        pool_0, pool_1, pool_t, wf, wb, part_0, part_1, part_own, xr, rbuf, gath, wsend, wkeep, wrecv, wout_0, wout,
        og_v, scale, par, mix_0, mix_v, sacc, sred, srecv,
        pool_s, wf_s, wb_s, xs_send, xs_recv, x0_send, x0_recv, z_send, z_recv, g_send, g_recv,
        w_send, w_recv, wout_s, og_s, mix_s, st_send, st_recv, credit, wcredit,
    ) = refs
    L = 4
    NS = SUBS
    SB = rows // NS
    BIG, SMALL = rows * 3 // 10, rows // 5
    PB = rows // PIECES
    NCH = chl // LANE
    U = 2 * NCH
    SENDING = U + 3
    TICKS = (U + 5) * L
    pools, weights = (pool_a, pool_b), (weight_a, weight_b)
    ogs, mixeds = (og_a, og_b), (mixed_a, mixed_b)
    wgs = (wg_a, wg_b)

    f = lax.axis_index("feat")
    r = lax.axis_index("rows")
    p = lax.div(f, 2)
    c = lax.rem(f, 2)
    sib = f + 1 - 2 * c
    xp = r + 1 - 2 * lax.rem(r, 2)
    yp = lax.rem(r + 2, 4)
    dp = 3 - r
    has_left, has_right = p > 0, p < L - 1
    pos = (p, L - 1 - p)
    has_up = (has_left, has_right)
    nxt = (f + 2, f - 2)

    def remote(src, dst, send, recv, **dev):
        return pltpu.make_async_remote_copy(
            src_ref=src, dst_ref=dst, send_sem=send, recv_sem=recv, device_id=dev, device_id_type=MESH
        )

    def signal(sem, **dev):
        pl.semaphore_signal(sem, inc=1, device_id=dev, device_id_type=MESH)

    def start_all(copies):
        for copy in copies:
            copy.start()

    def wait_all(copies):
        for copy in copies:
            copy.wait()

    def lanes(index):
        return pl.ds(pl.multiple_of(index * LANE, LANE), LANE)

    def some_rows(i, n):
        return pl.ds(pl.multiple_of(i * n, n), n)

    def sub_rows(b):
        return pl.ds(b * SB, SB)

    def tower_of(index, run):
        for t in range(2):

            @pl.when(lax.rem(index, 2) == t)
            def _():
                run(t)

    sizes, pool_v, part_v = (BIG, SMALL), (pool_0, pool_1), (part_0, part_1)

    def piece_rows(s, k):
        return pl.ds(pl.multiple_of(lax.div(s, 2) * (BIG + SMALL) + k * BIG, LANE), sizes[k])

    def pool_loads(s, k):
        return [
            pltpu.make_async_copy(pools[t].at[piece_rows(s, k), :], pool_v[k].at[t], pool_s.at[k, t])
            for t in range(2)
        ]

    def wf_loads(per):
        j = lax.div(per, 2)
        core = jnp.where(lax.rem(per, 2) == 0, c, 1 - c)
        return [
            pltpu.make_async_copy(
                weights[t].at[:, lanes((2 * q + core) * NCH + j)],
                wf.at[t, :, q * LANE : (q + 1) * LANE],
                wf_s.at[t, q],
            )
            for t in range(2)
            for q in range(L)
        ]

    def wb_loads(j, t):
        out = []
        for q in range(L):
            for k in range(2):
                out.append(
                    pltpu.make_async_copy(
                        weights[t].at[:, lanes((2 * q + k) * NCH + j)],
                        wb.at[q, :, k * LANE : (k + 1) * LANE],
                        wb_s.at[q, k],
                    )
                )
        return out

    def og_loads(j):
        return [pltpu.make_async_copy(ogs[t].at[:, lanes(j)], og_v.at[t], og_s.at[t]) for t in range(2)]

    def mix_stores(j, b):
        return [
            pltpu.make_async_copy(mix_v.at[b % 2, t], mixeds[t].at[sub_rows(b), lanes(j)], mix_s.at[b % 2, t])
            for t in range(2)
        ]

    def part_copy(j, s, k):
        return remote(
            part_v[k],
            xr.at[lax.rem(j, 2), :, :, piece_rows(s, k), :],
            xs_send.at[s],
            xs_recv.at[s],
            feat=sib,
        )

    def first_copy(h, s, k):
        return remote(
            part_v[k].at[lax.div(s, 2)],
            xr.at[0, h, :, piece_rows(s, k), :],
            x0_send.at[h, s],
            x0_recv.at[h, s],
            feat=sib,
        )

    def share_copy(u, o, core, d, b, s, par2):
        block = gath.at[lax.rem(u, 4), o, core, sub_rows(b), :]
        return remote(block, block, g_send.at[d, b, s], g_recv.at[d, b, s, par2], feat=sib)

    def gath_copy(u, o, d, b, s, par2):
        block = gath.at[lax.rem(u, 4), o, c, sub_rows(b), :]
        return remote(block, block, z_send.at[d, b, s], z_recv.at[d, b, s, par2], feat=nxt[d])

    def sum_block(u, d, b, s):
        return rbuf.at[lax.rem(u, 2), d, lax.rem(s, 3), sub_rows(b), :]

    def sum_copy(u, d, b, s, par2):
        return remote(
            sum_block(u, d, b, s - 1),
            sum_block(u, d, b, s),
            z_send.at[d, b, s],
            z_recv.at[d, b, s, par2],
            feat=nxt[d],
        )

    def sum_wait(u, d, b, s, par2):
        block = sum_block(u, d, b, s)
        remote(block, block, z_send.at[d, b, s], z_recv.at[d, b, s, par2], feat=nxt[d]).wait_recv()

    def packed(one, two, h):
        return jnp.where(upper(one.shape[0]) == (h == 1), one, swap(two))

    def own_sum(u, o, b):
        h, j2 = lax.rem(u, 2), lax.rem(lax.div(u, 2), 2)
        return part_own[j2, h, o, sub_rows(b), :].astype(F32) + xr[j2, h, o, sub_rows(b), :].astype(F32)

    def fold(v):
        return jnp.sum(v.reshape(SB // 8, 8, LANE), axis=0)

    def finalize(u, b, per):
        j, h = lax.div(u, 2), lax.rem(u, 2)
        last2 = lax.rem(per - 1, 2)
        for d in (RIGHT, LEFT):

            @pl.when(has_up[d])
            def _():
                sum_wait(u, d, b, L - 1, last2)

        if b == 0:

            @pl.when(h == 0)
            def _():
                wait_all(og_loads(j))

        v = own_sum(u, p, b) + par[u, 3:4, :]
        for d in (RIGHT, LEFT):
            v = v + jnp.where(has_up[d], rbuf[lax.rem(u, 2), d, 0, sub_rows(b), :].astype(F32), 0.0)
        same, cross, back = (par[u, k : k + 1, :] for k in range(3))
        row = jnp.concatenate(
            [jnp.broadcast_to(scale[k : k + 1, :], (LANE, LANE)).T for k in range(b * SB // LANE, (b + 1) * SB // LANE)],
            axis=0,
        )
        gy = row * packed(og_v[h, sub_rows(b), :].astype(F32), og_v[1 - h, sub_rows(b), :].astype(F32), h)
        cdf = 0.5 * (1.0 + lax.erf(v * INV_SQRT2))
        act = v * cdf
        slope = cdf + v * (INV_SQRT_2PI * jnp.exp(-0.5 * v * v))
        act_x = swap(act)
        mixed = row * (same * act + cross * act_x)
        gpre = ((same * gy + back * swap(gy)) * slope).astype(BF16)
        gath[lax.rem(u, 4), p, c, sub_rows(b), :] = gpre
        sacc[u, 0] += fold(gy * act)
        sacc[u, 1] += fold(gy * act_x)
        sacc[u, 2] += fold(gpre.astype(F32))

        @pl.when(h == 0)
        def _():
            mix_0[sub_rows(b), :] = mixed.astype(BF16)

        @pl.when(h == 1)
        def _():
            if b > 1:
                wait_all(mix_stores(j, b))
            else:

                @pl.when(j >= 1)
                def _():
                    wait_all(mix_stores(j, b))

            first, second = mix_0[sub_rows(b), :], mixed.astype(BF16)
            for t in range(2):
                mix_v[b % 2, t] = halves(first, second, t)
            start_all(mix_stores(j, b))

    first_partner, second_partner = (xp, yp), (yp, xp)

    def w_copy(u, t, kind):
        u2 = lax.rem(u, 2)
        return remote(
            wkeep.at[u2, t, 0] if kind == KEEP else wsend.at[t, kind],
            wrecv.at[u2, t, kind],
            w_send.at[t, kind],
            w_recv.at[u2, t, kind],
            rows=second_partner[t] if kind == KEEP else first_partner[t],
        )

    def wout_stores(j, t):
        return [
            pltpu.make_async_copy(wout.at[t, k], wgs[t].at[:, lanes(k * NCH + j)], wout_s.at[t, k])
            for k in range(2)
        ]

    def row_products(u, t, one, two):
        cols = []
        for owner in (one, two):
            pair = [gath[lax.rem(u, 4), owner, core] for core in range(2)]
            cols.append(halves(pair[0], pair[1], t))
        return dot(pool_t[t], jnp.concatenate(cols, axis=1)).astype(BF16)

    def pool_products(j, t, i):
        mine = some_rows(i, PB)
        total = None
        for q in range(L):
            cols = []
            for core in range(2):
                pair = [gath[lax.rem(2 * j + h, 4), q, core, mine, :] for h in range(2)]
                cols.append(halves(pair[0], pair[1], t))
            term = dot_t(jnp.concatenate(cols, axis=1), wb[q])
            total = term if total is None else total + term

        @pl.when(j == 0)
        def _():
            acc[t, mine, :] = total

        @pl.when(j > 0)
        def _():
            acc[t, mine, :] += total

    def first_weights():
        out = wf_loads(0)
        for t in range(2):
            for q in range(L):
                tile, k = 2 * t + q // 2, q % 2
                out.append(
                    pltpu.make_async_copy(
                        weights[t].at[:, lanes((2 * q + 1 - c) * NCH)],
                        wb.at[tile, :, k * LANE : (k + 1) * LANE],
                        wb_s.at[tile, k],
                    )
                )
        return out

    start_all(first_weights())
    start_all(pool_loads(0, 0))
    start_all(pool_loads(1, 1))

    bar = pltpu.get_barrier_semaphore()

    @pl.when(has_left)
    def _():
        signal(bar, feat=f - 2)

    @pl.when(has_right)
    def _():
        signal(bar, feat=f + 2)

    signal(bar, feat=sib)
    signal(bar, rows=xp)
    signal(bar, rows=yp)
    signal(bar, rows=dp)
    sacc[...] = jnp.zeros_like(sacc)
    scale[...] = mask[...].astype(F32) / count[...].astype(F32)
    for u in range(U):
        ch = slice(u // 2 * LANE, (u // 2 + 1) * LANE)
        s00, s01, s10, s11 = (stitch[k // 2, k % 2 : k % 2 + 1, ch] for k in range(4))
        rows_of = (s00, s11), (s01, s10), (s10, s01), (bias_a[:, ch], bias_b[:, ch])
        for k, (one, two) in enumerate(rows_of):
            par[u, k : k + 1, :] = halves(one, two, u % 2)

    def first_tiles(h):
        for t in range(2):
            for q in range(L):
                mine = wf[t, :, q * LANE : (q + 1) * LANE]
                other = wb[2 * t + q // 2, :, q % 2 * LANE : (q % 2 + 1) * LANE]
                gath[3 - h, q, t, :width, :] = halves(mine, other, h)

    def first_products(h, s, k, slot):
        res = []
        for t in range(2):
            cols = jnp.concatenate([gath[3 - h, q, t, :width, :] for q in range(L)], axis=1)
            res.append(dot(pool_v[k][t], cols).astype(BF16))
        for q in range(L):
            both = [v[:, q * LANE : (q + 1) * LANE] for v in res]
            part_own[0, h, q, piece_rows(s, k), :] = halves(*both, 0)
            part_v[k][slot, q] = halves(*both, 1)

    wait_all(first_weights())
    first_tiles(0)
    for s in range(L):
        k = s % 2
        wait_all(pool_loads(s, k))
        first_products(0, s, k, s // 2)
        if s < 3:
            start_all(pool_loads((s + 2) % L, k))
        if s == 0:
            pl.semaphore_wait(bar, 4 + has_left.astype(jnp.int32) + has_right.astype(jnp.int32))
        first_copy(0, s, k).start()
    first_tiles(1)
    start_all(wf_loads(2))

    def begin_sums():
        for i in range(L):
            first_copy(0, i, i % 2).wait_recv()
        for d in (RIGHT, LEFT):

            @pl.when(pos[d] == 0)
            def _():
                for b in range(NS):
                    sum_block(0, d, b, 0)[...] = own_sum(0, p + (L - 1) * (1 - 2 * d), b).astype(BF16)
                    sum_copy(0, d, b, 1, 0).start()

    def tick(T, carry):
        per, s = lax.div(T, L), lax.rem(T, L)
        par2 = lax.rem(per, 2)
        u = per - 3
        ur = per - 2
        gathers = (u >= 0) & (u < U)
        sums = (ur >= 0) & (ur < U)

        @pl.when((s == 0) & (per >= 3) & (per < SENDING))
        def _():
            @pl.when(has_left)
            def _():
                pl.semaphore_wait(credit.at[0], 1)

            @pl.when(has_right)
            def _():
                pl.semaphore_wait(credit.at[1], 1)

            pl.semaphore_wait(credit.at[2], 1)

        @pl.when((s == 1) & sums & (par2 == 0))
        def _():
            @pl.when(ur > 0)
            def _():
                for k in range(L):
                    part_copy(lax.div(ur, 2), k, k % 2).wait_recv()

            start_all(og_loads(lax.div(ur, 2)))

        @pl.when(T == 3 * L + 1)
        def _():
            for k in range(L):
                first_copy(1, k, k % 2).wait_recv()

        before = T - 1 + L
        per_m, s_m = lax.div(before, L) - 1, lax.rem(before, L)
        par_m = lax.rem(per_m + 2, 2)
        u_m, ur_m = per_m - 3, per_m - 2
        gathers_m = (u_m >= 0) & (u_m < U)
        sums_m = (ur_m >= 0) & (ur_m < U)
        ub = per - 4
        uz = per - 5
        jp = lax.div(jnp.maximum(per - 5, 0), 2)

        def flows(b):
            @pl.when((s == 0) & gathers)
            def _():
                finalize(u, b, per)

            for d in (RIGHT, LEFT):
                gather_here = pos[d] >= s
                o = p - s if d == RIGHT else p + s
                dest = p + (L - s) if d == RIGHT else p - (L - s)
                shares = (s >= 1) if d == LEFT else (s >= 0)

                @pl.when(gathers & gather_here)
                def _():
                    @pl.when(s >= 1)
                    def _():
                        gath_copy(u, o, d, b, s - 1, par2).wait_recv()

                    @pl.when(pos[d] < L - 1)
                    def _():
                        gath_copy(u, o, d, b, s, par2).start()

                    @pl.when(shares)
                    def _():
                        share_copy(u, o, c, d, b, s, par2).start()

                begun = (ur == 0) & (s == 1)

                @pl.when(sums & jnp.logical_not(gather_here | begun))
                def _():
                    block = sum_block(ur, d, b, s - 1)

                    @pl.when(pos[d] >= 1)
                    def _():
                        sum_wait(ur, d, b, s - 1, par2)
                        block[...] = (own_sum(ur, dest, b) + block[...].astype(F32)).astype(BF16)

                    @pl.when(pos[d] < 1)
                    def _():
                        block[...] = own_sum(ur, dest, b).astype(BF16)

                    sum_copy(ur, d, b, s, par2).start()

        def share_waits():
            for b in range(NS):
                for d in (RIGHT, LEFT):
                    o = p - s_m if d == RIGHT else p + s_m
                    shares = (s_m >= 1) if d == LEFT else (s_m >= 0)

                    @pl.when(gathers_m & (pos[d] >= s_m) & shares)
                    def _():
                        share_copy(u_m, o, 1 - c, d, b, s_m, par_m).wait_recv()

        def partial_products():
            @pl.when(per < U)
            def _():
                j = lax.div(per, 2)
                for k in range(2):

                    @pl.when(lax.rem(s, 2) == k)
                    def _():
                        wait_all(pool_loads(s, k))

                        @pl.when(per == 2)
                        def _():
                            first_copy(0, s, k).wait_send()
                            first_products(1, s, k, lax.div(s, 2))
                            first_copy(1, s, k).start()
                            if k == 0:

                                @pl.when(s == 0)
                                def _():
                                    begin_sums()

                        if k == 0:

                            @pl.when(s == 0)
                            def _():
                                wait_all(wf_loads(per))

                        @pl.when((per == 3) & (s < 2))
                        def _():
                            for i in range(2):
                                first_copy(1, s + 2 * i, k).wait_send()

                        @pl.when(T + 1 < U * L)
                        def _():
                            start_all(pool_loads(lax.rem(s + 1, L), 1 - k))

                        res = [dot(pool_v[k][t], wf[t]).astype(BF16) for t in range(2)]
                        for q in range(L):
                            both = [v[:, q * LANE : (q + 1) * LANE] for v in res]
                            for h in range(2):
                                block = halves(*both, h)

                                @pl.when(par2 == 0)
                                def _():
                                    part_own[lax.rem(j, 2), h, q, piece_rows(s, k), :] = block

                                @pl.when(par2 == 1)
                                def _():
                                    part_v[k][h, q] = block

                        @pl.when(par2 == 1)
                        def _():
                            part_copy(j, s, k).start()

                        @pl.when(per == 3)
                        def _():
                            for t in range(2):
                                pool_t[t, :, piece_rows(s, k)] = pool_v[k][t].T

                @pl.when((s == L - 1) & (per + 1 < U))
                def _():
                    start_all(wf_loads(per + 1))

        def weight_products(t):
            @pl.when((s == 0) & (ub >= 0) & (ub < U))
            def _():
                if t == 0:

                    @pl.when(ub >= 2)
                    def _():
                        pl.semaphore_wait(wcredit.at[0], 1)
                        pl.semaphore_wait(wcredit.at[1], 1)

                res = row_products(ub, t, dp, first_partner[t])
                for kind in (FAR, NEAR):
                    wsend[t, kind] = res[:, kind * LANE : (kind + 1) * LANE]
                w_copy(ub, t, FAR).start()

            @pl.when((s == 1) & (ub >= 0) & (ub < U))
            def _():
                res = row_products(ub, t, second_partner[t], r)
                for k in range(2):
                    wkeep[lax.rem(ub, 2), t, k] = res[:, k * LANE : (k + 1) * LANE]

        def pool_piece(k):
            @pl.when((per >= 5) & (par2 == 1) & (s >= 2))
            def _():
                if k == 0:

                    @pl.when(s == 2)
                    def _():
                        wait_all(wb_loads(jp, 0))

                pool_products(jp, 0, 2 * (s - 2) + k)
                if k == 1:

                    @pl.when(s == 3)
                    def _():
                        start_all(wb_loads(jp, 1))

            @pl.when((per >= 6) & (par2 == 0) & ((s == 1) | (s == 2)))
            def _():
                if k == 0:

                    @pl.when(s == 1)
                    def _():
                        wait_all(wb_loads(jp, 1))

                pool_products(jp, 1, 2 * (s - 1) + k)

        def send_near():
            @pl.when((s == 2) & (ub >= 0) & (ub < U))
            def _():
                for t in range(2):
                    w_copy(ub, t, NEAR).start()

        def finish_weights():
            @pl.when((s == 2) & (uz >= 0) & (uz < U))
            def _():
                j, h, u2 = lax.div(uz, 2), lax.rem(uz, 2), lax.rem(uz, 2)
                for t in range(2):
                    w_copy(uz, t, NEAR).wait_recv()
                    w_copy(uz, t, KEEP).wait_recv()
                    w_copy(uz, t, KEEP).wait_send()
                    both = wkeep[u2, t, 1].astype(F32) + wrecv[u2, t, NEAR].astype(F32)
                    both = both + wrecv[u2, t, KEEP].astype(F32)

                    @pl.when(h == 0)
                    def _():
                        @pl.when(j >= 1)
                        def _():
                            wait_all(wout_stores(j, t))

                        wout_0[t] = both

                    @pl.when(h == 1)
                    def _():
                        for k in range(2):
                            wout[t, k] = halves(wout_0[t], both, k).astype(BF16)
                        start_all(wout_stores(j, t))

                @pl.when(uz < U - 2)
                def _():
                    signal(wcredit.at[0], rows=xp)
                    signal(wcredit.at[1], rows=yp)

            @pl.when((s == 3) & (ub >= 0) & (ub < U))
            def _():
                u2 = lax.rem(ub, 2)
                for t in range(2):
                    w_copy(ub, t, FAR).wait_recv()
                    both = wkeep[u2, t, 0].astype(F32) + wrecv[u2, t, FAR].astype(F32)
                    wkeep[u2, t, 0] = both.astype(BF16)
                    w_copy(ub, t, KEEP).start()

        @pl.when((s == 0) & (uz >= 0) & (uz < U))
        def _():
            for t in range(2):
                for kind in (FAR, NEAR):
                    w_copy(uz, t, kind).wait_send()

        @pl.when((s == 0) & (per >= 5) & (par2 == 1))
        def _():
            start_all(wb_loads(jp, 0))

        flows(0)
        share_waits()
        weight_products(0)
        flows(1)
        pool_piece(0)
        flows(2)
        send_near()
        weight_products(1)
        flows(3)
        pool_piece(1)
        flows(4)
        partial_products()
        finish_weights()

        for k in range(2):

            @pl.when((per_m >= 3) & (per_m < U) & (par_m == 1) & (lax.rem(s_m, 2) == k))
            def _():
                part_copy(0, s_m, k).wait_send()

        for b in range(NS):
            for d in (RIGHT, LEFT):
                shares = (s_m >= 1) if d == LEFT else (s_m >= 0)

                @pl.when(gathers_m & (pos[d] >= s_m))
                def _():
                    @pl.when(pos[d] < L - 1)
                    def _():
                        gath_copy(u_m, p, d, b, s_m, par_m).wait_send()

                    @pl.when(shares)
                    def _():
                        share_copy(u_m, p, c, d, b, s_m, par_m).wait_send()

                @pl.when(sums_m & (pos[d] < s_m))
                def _():
                    sum_copy(ur_m, d, b, s_m, par_m).wait_send()

        @pl.when((s == 2) & (per < SENDING - 1))
        def _():
            @pl.when(has_left)
            def _():
                signal(credit.at[1], feat=f - 2)

            @pl.when(has_right)
            def _():
                signal(credit.at[0], feat=f + 2)

            signal(credit.at[2], feat=sib)

        @pl.when(T == (U + 2) * L + 1)
        def _():
            for j in range(NCH):
                sums_of = [[jnp.sum(sacc[2 * j + h, k], axis=0, keepdims=True) for h in range(2)] for k in range(3)]
                (same, cross, bias) = sums_of
                rows_of = [halves(*same, 0), halves(*cross, 0), halves(*cross, 1), halves(*same, 1)]
                rows_of += [halves(*bias, 0), halves(*bias, 1), jnp.zeros((2, LANE), F32)]
                sred[j] = jnp.concatenate(rows_of, axis=0)
            for k, peer in enumerate((xp, yp, dp)):
                remote(sred.at[peer], srecv.at[k], st_send.at[k], st_recv.at[k], rows=peer).start()

        return carry

    lax.fori_loop(2 * L, TICKS, tick, 0)

    for k, peer in enumerate((xp, yp, dp)):
        copy = remote(sred.at[peer], srecv.at[k], st_send.at[k], st_recv.at[k], rows=peer)
        copy.wait_send()
        copy.wait_recv()
    stats[...] = sred[r] + srecv[0] + srecv[1] + srecv[2]
    for b in range(2):
        wait_all(mix_stores(NCH - 1, b))
    for t in range(2):
        wait_all(wout_stores(NCH - 1, t))


def hand_over(mixed_a, mixed_b, acc, wg_a, wg_b, stats, *refs):
    results, (bias_a, bias_b, stitch) = refs[:6], refs[6:9]
    low, held, (load_s, store_s) = refs[9:11], refs[11:17], refs[17:]
    sources = {0: mixed_a, 1: mixed_b, 4: wg_a, 5: wg_b}
    steps = []
    for k in (4, 0, 5, 1, 2, 3):
        n = results[k].shape[0] // COPIES
        for i in range(COPIES):
            some = pl.ds(i * n, n)
            load = None
            if k in sources:
                via = low[k - 4] if k >= 4 else held[k]
                load = pltpu.make_async_copy(sources[k].at[some, :], via.at[some, :], load_s.at[k, i])
            store = pltpu.make_async_copy(held[k].at[some, :], results[k].at[some, :], store_s.at[k, i])
            steps.append((k, some, load, store))
    for _, _, load, _ in steps:
        if load is not None:
            load.start()
    bias_a[...] = stats[4:5, :]
    bias_b[...] = stats[5:6, :]
    stitch[0] = stats[0:2, :]
    stitch[1] = stats[2:4, :]
    for k, some, load, store in sorted(steps, key=lambda step: (2, 3, 4, 0, 5, 1).index(step[0])):
        if load is not None:
            load.wait()
        if k >= 4:
            held[k][some, :] = low[k - 4][some, :].astype(F32)
        elif k >= 2:
            held[k][some, :] = acc[k - 2, some, :].astype(BF16)
        store.start()
    for _, _, _, store in steps:
        store.wait()


def fused(
    pool_a, pool_b, weight_a, weight_b, bias_a, bias_b, stitch, crop_count, row_mask, outgrad_a, outgrad_b
):
    rows, width = pool_a.shape
    chl = bias_a.shape[0]
    NS, L = SUBS, 4
    BIG, SMALL = rows * 3 // 10, rows // 5
    NCH = chl // LANE
    hbm = pl.BlockSpec(memory_space=pl.ANY)
    vmem = pl.BlockSpec(memory_space=pltpu.VMEM)
    dma = pltpu.SemaphoreType.DMA
    out_shape = (
        jax.ShapeDtypeStruct((rows, chl), BF16),
        jax.ShapeDtypeStruct((rows, chl), BF16),
        pltpu.VMEM((2, rows, width), F32),
        jax.ShapeDtypeStruct((width, 2 * chl), BF16),
        jax.ShapeDtypeStruct((width, 2 * chl), BF16),
        jax.ShapeDtypeStruct((8, LANE), F32),
    )
    results = (
        out_shape[:2]
        + (jax.ShapeDtypeStruct((rows, width), BF16),) * 2
        + (jax.ShapeDtypeStruct((width, 2 * chl), F32),) * 2
    )
    scratch = [
        pltpu.VMEM((2, BIG, width), BF16),
        pltpu.VMEM((2, SMALL, width), BF16),
        pltpu.VMEM((2, width, rows), BF16),
        pltpu.VMEM((2, width, L * LANE), BF16),
        pltpu.VMEM((L, width, 2 * LANE), BF16),
        pltpu.VMEM((2, L, BIG, LANE), BF16),
        pltpu.VMEM((2, L, SMALL, LANE), BF16),
        pltpu.VMEM((2, 2, L, rows, LANE), BF16),
        pltpu.VMEM((2, 2, L, rows, LANE), BF16),
        pltpu.VMEM((2, 2, 3, rows, LANE), BF16),
        pltpu.VMEM((4, L, 2, rows, LANE), BF16),
        pltpu.VMEM((2, 2, width, LANE), BF16),
        pltpu.VMEM((2, 2, 2, width, LANE), BF16),
        pltpu.VMEM((2, 2, 3, width, LANE), BF16),
        pltpu.VMEM((2, width, LANE), F32),
        pltpu.VMEM((2, 2, width, LANE), BF16),
        pltpu.VMEM((2, rows, LANE), BF16),
        pltpu.VMEM((rows // LANE, LANE), F32),
        pltpu.VMEM((2 * NCH, 8, LANE), F32),
        pltpu.VMEM((rows, LANE), BF16),
        pltpu.VMEM((2, 2, rows // NS, LANE), BF16),
        pltpu.VMEM((2 * NCH, 3, 8, LANE), F32),
        pltpu.VMEM((NCH, 8, LANE), F32),
        pltpu.VMEM((3, 8, LANE), F32),
        dma((2, 2)),
        dma((2, L)),
        dma((L, 2)),
        dma((L,)),
        dma((L,)),
        dma((2, L)),
        dma((2, L)),
        dma((2, NS, L)),
        dma((2, NS, L, 2)),
        dma((2, NS, L)),
        dma((2, NS, L, 2)),
        dma((2, 3)),
        dma((2, 2, 3)),
        dma((2, 2)),
        dma((2,)),
        dma((2, 2)),
        dma((3,)),
        dma((3,)),
        pltpu.SemaphoreType.REGULAR((3,)),
        pltpu.SemaphoreType.REGULAR((2,)),
    ]
    mixed_a, mixed_b, acc, wg_a, wg_b, stats = pl.pallas_call(
        functools.partial(kernel, rows, width, chl),
        out_shape=out_shape,
        in_specs=[hbm] * 4 + [vmem] * 5 + [hbm] * 2,
        out_specs=(hbm, hbm, vmem, hbm, hbm, vmem),
        scratch_shapes=scratch,
        compiler_params=pltpu.CompilerParams(
            collective_id=0, has_side_effects=True, vmem_limit_bytes=VMEM_LIMIT
        ),
    )(
        pool_a,
        pool_b,
        weight_a,
        weight_b,
        bias_a[None],
        bias_b[None],
        stitch,
        row_mask.reshape(rows // LANE, LANE),
        crop_count.reshape(rows // LANE, LANE),
        outgrad_a,
        outgrad_b,
    )
    held = [pltpu.with_memory_space_constraint(v, pltpu.HBM) for v in (mixed_a, mixed_b, acc, wg_a, wg_b)]
    held[2] = pltpu.with_memory_space_constraint(acc, pltpu.VMEM)
    held.append(stats)
    outs = pl.pallas_call(
        hand_over,
        out_shape=results
        + (
            jax.ShapeDtypeStruct((1, LANE), F32),
            jax.ShapeDtypeStruct((1, LANE), F32),
            jax.ShapeDtypeStruct((2, 2, LANE), F32),
        ),
        in_specs=[hbm, hbm, vmem, hbm, hbm, vmem],
        out_specs=(hbm,) * 6 + (vmem,) * 3,
        scratch_shapes=[pltpu.VMEM(out.shape, out.dtype) for out in out_shape[3:5] + results] + [dma((6, COPIES))] * 2,
        compiler_params=pltpu.CompilerParams(vmem_limit_bytes=VMEM_LIMIT),
    )(*held)
    return (*outs[:6], outs[6][0], outs[7][0], outs[8])


VMEM_LIMIT = 52 * 1024 * 1024


def plain(
    pool_a, pool_b, weight_a, weight_b, bias_a, bias_b, stitch, crop_count, row_mask, outgrad_a, outgrad_b
):
    row = (row_mask.astype(F32) / crop_count.astype(F32))[:, None]

    def pre(pool, weight, bias):
        partial = dot(pool, weight).astype(BF16)
        return lax.psum_scatter(partial, "feat", scatter_dimension=1, tiled=True).astype(F32) + bias

    def gelu(v):
        cdf = 0.5 * (1.0 + lax.erf(v * INV_SQRT2))
        return v * cdf, cdf + v * (INV_SQRT_2PI * jnp.exp(-0.5 * v * v))

    act_a, slope_a = gelu(pre(pool_a, weight_a, bias_a))
    act_b, slope_b = gelu(pre(pool_b, weight_b, bias_b))
    (s00, s01), (s10, s11) = stitch[0], stitch[1]
    mixed_a = (row * (s00 * act_a + s01 * act_b)).astype(BF16)
    mixed_b = (row * (s10 * act_a + s11 * act_b)).astype(BF16)
    gy_a = row * outgrad_a.astype(F32)
    gy_b = row * outgrad_b.astype(F32)
    gpre_a = ((s00 * gy_a + s10 * gy_b) * slope_a).astype(BF16)
    gpre_b = ((s01 * gy_a + s11 * gy_b) * slope_b).astype(BF16)
    sums = jnp.stack(
        [
            jnp.sum(v, axis=0)
            for v in (
                gy_a * act_a,
                gy_a * act_b,
                gy_b * act_a,
                gy_b * act_b,
                gpre_a.astype(F32),
                gpre_b.astype(F32),
            )
        ]
    )
    sums = lax.psum_scatter(sums, "rows", scatter_dimension=1, tiled=True)

    def back(pool, weight, gpre):
        whole = lax.all_gather(gpre, "feat", axis=1, tiled=True)
        pool_grad = dot_t(whole, weight).astype(BF16)
        wgrad = lax.dot_general(pool, whole, (((0,), (0,)), ((), ())), preferred_element_type=F32)
        wgrad = lax.psum_scatter(wgrad.astype(BF16), "rows", scatter_dimension=1, tiled=True)
        return pool_grad, wgrad.astype(F32)

    pg_a, wg_a = back(pool_a, weight_a, gpre_a)
    pg_b, wg_b = back(pool_b, weight_b, gpre_b)
    return mixed_a, mixed_b, pg_a, pg_b, wg_a, wg_b, sums[4], sums[5], sums[:4].reshape(2, 2, -1)


def shards(
    pool_a, pool_b, weight_a, weight_b, bias_a, bias_b, stitch, crop_count, row_mask, outgrad_a, outgrad_b
):
    rows, width = pool_a.shape
    chl = bias_a.shape[0]
    n_rows, n_feat = lax.axis_size("rows"), lax.axis_size("feat")
    fits = (
        n_rows == 4
        and n_feat == 8
        and chl == n_rows * LANE
        and width % LANE == 0
        and width <= rows
        and rows % (2 * SUBS * LANE) == 0
    )
    run = fused if fits else plain
    return run(pool_a, pool_b, weight_a, weight_b, bias_a, bias_b, stitch, crop_count, row_mask, outgrad_a, outgrad_b)


def solution(mesh):
    return jax.shard_map(
        shards,
        mesh=mesh,
        in_specs=(
            P("rows", "feat"),
            P("rows", "feat"),
            P("feat", None),
            P("feat", None),
            P("feat"),
            P("feat"),
            P(None, None, "feat"),
            P("rows"),
            P("rows"),
            P("rows", "feat"),
            P("rows", "feat"),
        ),
        out_specs=(
            P("rows", "feat"),
            P("rows", "feat"),
            P("rows", "feat"),
            P("rows", "feat"),
            P("feat", "rows"),
            P("feat", "rows"),
            P(("feat", "rows")),
            P(("feat", "rows")),
            P(None, None, ("feat", "rows")),
        ),
        check_vma=False,
    )
```

```python
import functools

import jax
import jax.numpy as jnp
from jax import lax
from jax.experimental import pallas as pl
from jax.experimental.pallas import tpu as pltpu
from jax.sharding import PartitionSpec as P

MESH = pl.DeviceIdType.MESH
F32 = jnp.float32
BF16 = jnp.bfloat16
LANE = 128
HALF = 64
SUBS = 5
PIECES = 4
COPIES = 4
RIGHT, LEFT = 0, 1
FAR, NEAR, KEEP, OWN = 0, 1, 2, 3
INV_SQRT2 = 0.7071067811865476
INV_SQRT_2PI = 0.3989422804014327


def dot(lhs, rhs):
    return lax.dot_general(lhs, rhs, (((1,), (0,)), ((), ())), preferred_element_type=F32)


def dot_t(lhs, rhs):
    return lax.dot_general(lhs, rhs, (((1,), (1,)), ((), ())), preferred_element_type=F32)


def swap(v):
    return pltpu.roll(v, HALF, 1)


def upper(rows):
    return lax.broadcasted_iota(jnp.int32, (rows, LANE), 1) >= HALF


def halves(one, two, half):
    if half == 0:
        return jnp.where(upper(one.shape[0]), swap(two), one)
    return jnp.where(upper(one.shape[0]), two, swap(one))


def kernel(rows, width, chl, *refs):
    (
        pool_a, pool_b, weight_a, weight_b, bias_a, bias_b, stitch, mask, count, og_a, og_b,
        mixed_a, mixed_b, acc, wg_a, wg_b, stats,
        pool_0, pool_1, pool_t, wf, wb, part_0, part_1, part_own, xr, rbuf, gath, wsend, wkeep, wrecv, wout,
        og_v, scale, par, sacc, sred, srecv,
        pool_s, wf_s, wb_s, xs_send, xs_recv, x0_send, x0_recv, z_send, z_recv, g_send, g_recv,
        w_send, w_recv, wout_s, og_s, st_send, st_recv, credit, wcredit,
    ) = refs
    L = 4
    NS = SUBS
    SB = rows // NS
    BIG, SMALL = rows * 3 // 10, rows // 5
    PB = rows // PIECES
    NCH = chl // LANE
    U = 2 * NCH
    SENDING = U + 3
    TICKS = (U + 5) * L
    pools, weights = (pool_a, pool_b), (weight_a, weight_b)
    ogs, mixeds = (og_a, og_b), (mixed_a, mixed_b)
    wgs = (wg_a, wg_b)

    f = lax.axis_index("feat")
    r = lax.axis_index("rows")
    p = lax.div(f, 2)
    c = lax.rem(f, 2)
    sib = f + 1 - 2 * c
    xp = r + 1 - 2 * lax.rem(r, 2)
    yp = lax.rem(r + 2, 4)
    dp = 3 - r
    has_left, has_right = p > 0, p < L - 1
    pos = (p, L - 1 - p)
    has_up = (has_left, has_right)
    nxt = (f + 2, f - 2)

    def remote(src, dst, send, recv, **dev):
        return pltpu.make_async_remote_copy(
            src_ref=src, dst_ref=dst, send_sem=send, recv_sem=recv, device_id=dev, device_id_type=MESH
        )

    def signal(sem, **dev):
        pl.semaphore_signal(sem, inc=1, device_id=dev, device_id_type=MESH)

    def start_all(copies):
        for copy in copies:
            copy.start()

    def wait_all(copies):
        for copy in copies:
            copy.wait()

    def lanes(index):
        return pl.ds(pl.multiple_of(index * LANE, LANE), LANE)

    def some_rows(i, n):
        return pl.ds(pl.multiple_of(i * n, n), n)

    def sub_rows(b):
        return pl.ds(b * SB, SB)

    def tower_of(index, run):
        for t in range(2):

            @pl.when(lax.rem(index, 2) == t)
            def _():
                run(t)

    sizes, pool_v, part_v = (BIG, SMALL), (pool_0, pool_1), (part_0, part_1)

    def piece_rows(s, k):
        return pl.ds(pl.multiple_of(lax.div(s, 2) * (BIG + SMALL) + k * BIG, LANE), sizes[k])

    def pool_loads(s, k):
        return [
            pltpu.make_async_copy(pools[t].at[piece_rows(s, k), :], pool_v[k].at[t], pool_s.at[k, t])
            for t in range(2)
        ]

    def wf_loads(per):
        j = lax.div(per, 2)
        core = jnp.where(lax.rem(per, 2) == 0, c, 1 - c)
        return [
            pltpu.make_async_copy(
                weights[t].at[:, lanes((2 * q + core) * NCH + j)],
                wf.at[t, :, q * LANE : (q + 1) * LANE],
                wf_s.at[t, q],
            )
            for t in range(2)
            for q in range(L)
        ]

    def wb_loads(j, t):
        out = []
        for q in range(L):
            for k in range(2):
                out.append(
                    pltpu.make_async_copy(
                        weights[t].at[:, lanes((2 * q + k) * NCH + j)],
                        wb.at[q, :, k * LANE : (k + 1) * LANE],
                        wb_s.at[q, k],
                    )
                )
        return out

    def og_loads(j):
        return [pltpu.make_async_copy(ogs[t].at[:, lanes(j)], og_v.at[t], og_s.at[t]) for t in range(2)]

    def part_copy(j, s, k):
        return remote(
            part_v[k],
            xr.at[lax.rem(j, 2), :, :, piece_rows(s, k), :],
            xs_send.at[s],
            xs_recv.at[s],
            feat=sib,
        )

    def first_copy(h, s, k):
        return remote(
            part_v[k].at[lax.div(s, 2)],
            xr.at[0, h, :, piece_rows(s, k), :],
            x0_send.at[h, s],
            x0_recv.at[h, s],
            feat=sib,
        )

    def share_copy(u, o, core, d, b, s, par2):
        block = gath.at[lax.rem(u, 4), o, core, sub_rows(b), :]
        return remote(block, block, g_send.at[d, b, s], g_recv.at[d, b, s, par2], feat=sib)

    def gath_copy(u, o, d, b, s, par2):
        block = gath.at[lax.rem(u, 4), o, c, sub_rows(b), :]
        return remote(block, block, z_send.at[d, b, s], z_recv.at[d, b, s, par2], feat=nxt[d])

    def sum_block(u, d, b, s):
        return rbuf.at[lax.rem(u, 2), d, lax.rem(s, 3), sub_rows(b), :]

    def sum_copy(u, d, b, s, par2):
        return remote(
            sum_block(u, d, b, s - 1),
            sum_block(u, d, b, s),
            z_send.at[d, b, s],
            z_recv.at[d, b, s, par2],
            feat=nxt[d],
        )

    def sum_wait(u, d, b, s, par2):
        block = sum_block(u, d, b, s)
        remote(block, block, z_send.at[d, b, s], z_recv.at[d, b, s, par2], feat=nxt[d]).wait_recv()

    def packed(one, two, h):
        return jnp.where(upper(one.shape[0]) == (h == 1), one, swap(two))

    def own_sum(u, o, b):
        h, j2 = lax.rem(u, 2), lax.rem(lax.div(u, 2), 2)
        return part_own[j2, h, o, sub_rows(b), :].astype(F32) + xr[j2, h, o, sub_rows(b), :].astype(F32)

    def fold(v):
        return jnp.sum(v.reshape(SB // 8, 8, LANE), axis=0)

    def finalize(u, b, per):
        j, h = lax.div(u, 2), lax.rem(u, 2)
        last2 = lax.rem(per - 1, 2)
        for d in (RIGHT, LEFT):

            @pl.when(has_up[d])
            def _():
                sum_wait(u, d, b, L - 1, last2)

        if b == 0:

            @pl.when(h == 0)
            def _():
                wait_all(og_loads(j))

        v = own_sum(u, p, b) + par[u, 3:4, :]
        for d in (RIGHT, LEFT):
            v = v + jnp.where(has_up[d], rbuf[lax.rem(u, 2), d, 0, sub_rows(b), :].astype(F32), 0.0)
        same, cross, back = (par[u, k : k + 1, :] for k in range(3))
        row = jnp.concatenate(
            [jnp.broadcast_to(scale[k : k + 1, :], (LANE, LANE)).T for k in range(b * SB // LANE, (b + 1) * SB // LANE)],
            axis=0,
        )
        gy = row * packed(og_v[h, sub_rows(b), :].astype(F32), og_v[1 - h, sub_rows(b), :].astype(F32), h)
        cdf = 0.5 * (1.0 + lax.erf(v * INV_SQRT2))
        act = v * cdf
        slope = cdf + v * (INV_SQRT_2PI * jnp.exp(-0.5 * v * v))
        act_x = swap(act)
        mixed = row * (same * act + cross * act_x)
        gpre = ((same * gy + back * swap(gy)) * slope).astype(BF16)
        gath[lax.rem(u, 4), p, c, sub_rows(b), :] = gpre
        sacc[u, 0] += fold(gy * act)
        sacc[u, 1] += fold(gy * act_x)
        sacc[u, 2] += fold(gpre.astype(F32))

        @pl.when(h == 0)
        def _():
            mixed_a[sub_rows(b), lanes(j)] = mixed.astype(BF16)

        @pl.when(h == 1)
        def _():
            first, second = mixed_a[sub_rows(b), lanes(j)], mixed.astype(BF16)
            for t in range(2):
                mixeds[t][sub_rows(b), lanes(j)] = halves(first, second, t)

    first_partner, second_partner = (xp, yp), (yp, xp)

    def w_copy(u, t, kind):
        u2 = lax.rem(u, 2)
        return remote(
            wkeep.at[u2, t, 0] if kind == KEEP else wsend.at[t, kind],
            wrecv.at[u2, t, kind],
            w_send.at[t, kind],
            w_recv.at[u2, t, kind],
            rows=second_partner[t] if kind == KEEP else first_partner[t],
        )

    def wout_stores(j, t):
        return [
            pltpu.make_async_copy(wout.at[t, k], wgs[t].at[:, lanes(k * NCH + j)], wout_s.at[t, k])
            for k in range(2)
        ]

    def row_products(u, t, one, two):
        cols = []
        for owner in (one, two):
            pair = [gath[lax.rem(u, 4), owner, core] for core in range(2)]
            cols.append(halves(pair[0], pair[1], t))
        return dot(pool_t[t], jnp.concatenate(cols, axis=1)).astype(BF16)

    def pool_products(j, t, i):
        mine = some_rows(i, PB)
        total = None
        for q in range(L):
            cols = []
            for core in range(2):
                pair = [gath[lax.rem(2 * j + h, 4), q, core, mine, :] for h in range(2)]
                cols.append(halves(pair[0], pair[1], t))
            term = dot_t(jnp.concatenate(cols, axis=1), wb[q])
            total = term if total is None else total + term

        @pl.when(j == 0)
        def _():
            acc[t, mine, :] = total

        @pl.when(j > 0)
        def _():
            acc[t, mine, :] += total

    def first_weights():
        out = wf_loads(0)
        for t in range(2):
            for q in range(L):
                tile, k = 2 * t + q // 2, q % 2
                out.append(
                    pltpu.make_async_copy(
                        weights[t].at[:, lanes((2 * q + 1 - c) * NCH)],
                        wb.at[tile, :, k * LANE : (k + 1) * LANE],
                        wb_s.at[tile, k],
                    )
                )
        return out

    start_all(first_weights())
    start_all(pool_loads(0, 0))
    start_all(pool_loads(1, 1))

    bar = pltpu.get_barrier_semaphore()

    @pl.when(has_left)
    def _():
        signal(bar, feat=f - 2)

    @pl.when(has_right)
    def _():
        signal(bar, feat=f + 2)

    signal(bar, feat=sib)
    signal(bar, rows=xp)
    signal(bar, rows=yp)
    signal(bar, rows=dp)
    sacc[...] = jnp.zeros_like(sacc)
    scale[...] = mask[...].astype(F32) / count[...].astype(F32)
    for u in range(U):
        ch = slice(u // 2 * LANE, (u // 2 + 1) * LANE)
        s00, s01, s10, s11 = (stitch[k // 2, k % 2 : k % 2 + 1, ch] for k in range(4))
        rows_of = (s00, s11), (s01, s10), (s10, s01), (bias_a[:, ch], bias_b[:, ch])
        for k, (one, two) in enumerate(rows_of):
            par[u, k : k + 1, :] = halves(one, two, u % 2)

    def first_tiles(h):
        for t in range(2):
            for q in range(L):
                mine = wf[t, :, q * LANE : (q + 1) * LANE]
                other = wb[2 * t + q // 2, :, q % 2 * LANE : (q % 2 + 1) * LANE]
                gath[3 - h, q, t, :width, :] = halves(mine, other, h)

    def first_products(h, s, k, slot):
        res = []
        for t in range(2):
            cols = jnp.concatenate([gath[3 - h, q, t, :width, :] for q in range(L)], axis=1)
            res.append(dot(pool_v[k][t], cols).astype(BF16))
        for q in range(L):
            both = [v[:, q * LANE : (q + 1) * LANE] for v in res]
            part_own[0, h, q, piece_rows(s, k), :] = halves(*both, 0)
            part_v[k][slot, q] = halves(*both, 1)

    wait_all(first_weights())
    first_tiles(0)
    for s in range(L):
        k = s % 2
        wait_all(pool_loads(s, k))
        first_products(0, s, k, s // 2)
        if s < 3:
            start_all(pool_loads((s + 2) % L, k))
        if s == 0:
            pl.semaphore_wait(bar, 4 + has_left.astype(jnp.int32) + has_right.astype(jnp.int32))
        first_copy(0, s, k).start()
    first_tiles(1)
    start_all(wf_loads(2))

    def begin_sums():
        for i in range(L):
            first_copy(0, i, i % 2).wait_recv()
        for d in (RIGHT, LEFT):

            @pl.when(pos[d] == 0)
            def _():
                for b in range(NS):
                    sum_block(0, d, b, 0)[...] = own_sum(0, p + (L - 1) * (1 - 2 * d), b).astype(BF16)
                    sum_copy(0, d, b, 1, 0).start()

    def tick(T, carry):
        per, s = lax.div(T, L), lax.rem(T, L)
        par2 = lax.rem(per, 2)
        u = per - 3
        ur = per - 2
        gathers = (u >= 0) & (u < U)
        sums = (ur >= 0) & (ur < U)

        @pl.when((s == 0) & (per >= 3) & (per < SENDING))
        def _():
            @pl.when(has_left)
            def _():
                pl.semaphore_wait(credit.at[0], 1)

            @pl.when(has_right)
            def _():
                pl.semaphore_wait(credit.at[1], 1)

            pl.semaphore_wait(credit.at[2], 1)

        @pl.when((s == 1) & sums & (par2 == 0))
        def _():
            @pl.when(ur > 0)
            def _():
                for k in range(L):
                    part_copy(lax.div(ur, 2), k, k % 2).wait_recv()

            start_all(og_loads(lax.div(ur, 2)))

        @pl.when(T == 3 * L + 1)
        def _():
            for k in range(L):
                first_copy(1, k, k % 2).wait_recv()

        before = T - 1 + L
        per_m, s_m = lax.div(before, L) - 1, lax.rem(before, L)
        par_m = lax.rem(per_m + 2, 2)
        u_m, ur_m = per_m - 3, per_m - 2
        gathers_m = (u_m >= 0) & (u_m < U)
        sums_m = (ur_m >= 0) & (ur_m < U)
        ub = per - 4
        uz = per - 5
        jp = lax.div(jnp.maximum(per - 5, 0), 2)

        def flows(b):
            @pl.when((s == 0) & gathers)
            def _():
                finalize(u, b, per)

            for d in (RIGHT, LEFT):
                gather_here = pos[d] >= s
                o = p - s if d == RIGHT else p + s
                dest = p + (L - s) if d == RIGHT else p - (L - s)
                shares = (s >= 1) if d == LEFT else (s >= 0)

                @pl.when(gathers & gather_here)
                def _():
                    @pl.when(s >= 1)
                    def _():
                        gath_copy(u, o, d, b, s - 1, par2).wait_recv()

                    @pl.when(pos[d] < L - 1)
                    def _():
                        gath_copy(u, o, d, b, s, par2).start()

                    @pl.when(shares)
                    def _():
                        share_copy(u, o, c, d, b, s, par2).start()

                begun = (ur == 0) & (s == 1)

                @pl.when(sums & jnp.logical_not(gather_here | begun))
                def _():
                    block = sum_block(ur, d, b, s - 1)

                    @pl.when(pos[d] >= 1)
                    def _():
                        sum_wait(ur, d, b, s - 1, par2)
                        block[...] = (own_sum(ur, dest, b) + block[...].astype(F32)).astype(BF16)

                    @pl.when(pos[d] < 1)
                    def _():
                        block[...] = own_sum(ur, dest, b).astype(BF16)

                    sum_copy(ur, d, b, s, par2).start()

        def share_waits():
            for b in range(NS):
                for d in (RIGHT, LEFT):
                    o = p - s_m if d == RIGHT else p + s_m
                    shares = (s_m >= 1) if d == LEFT else (s_m >= 0)

                    @pl.when(gathers_m & (pos[d] >= s_m) & shares)
                    def _():
                        share_copy(u_m, o, 1 - c, d, b, s_m, par_m).wait_recv()

        def partial_products():
            @pl.when(per < U)
            def _():
                j = lax.div(per, 2)
                for k in range(2):

                    @pl.when(lax.rem(s, 2) == k)
                    def _():
                        wait_all(pool_loads(s, k))

                        @pl.when(per == 2)
                        def _():
                            first_copy(0, s, k).wait_send()
                            first_products(1, s, k, lax.div(s, 2))
                            first_copy(1, s, k).start()
                            if k == 0:

                                @pl.when(s == 0)
                                def _():
                                    begin_sums()

                        if k == 0:

                            @pl.when(s == 0)
                            def _():
                                wait_all(wf_loads(per))

                        @pl.when((per == 3) & (s < 2))
                        def _():
                            for i in range(2):
                                first_copy(1, s + 2 * i, k).wait_send()

                        @pl.when(T + 1 < U * L)
                        def _():
                            start_all(pool_loads(lax.rem(s + 1, L), 1 - k))

                        res = [dot(pool_v[k][t], wf[t]).astype(BF16) for t in range(2)]
                        for q in range(L):
                            both = [v[:, q * LANE : (q + 1) * LANE] for v in res]
                            for h in range(2):
                                block = halves(*both, h)

                                @pl.when(par2 == 0)
                                def _():
                                    part_own[lax.rem(j, 2), h, q, piece_rows(s, k), :] = block

                                @pl.when(par2 == 1)
                                def _():
                                    part_v[k][h, q] = block

                        @pl.when(par2 == 1)
                        def _():
                            part_copy(j, s, k).start()

                        @pl.when(per == 3)
                        def _():
                            for t in range(2):
                                pool_t[t, :, piece_rows(s, k)] = pool_v[k][t].T

                @pl.when((s == L - 1) & (per + 1 < U))
                def _():
                    start_all(wf_loads(per + 1))

        def weight_products(t):
            @pl.when((s == 0) & (ub >= 0) & (ub < U))
            def _():
                if t == 0:

                    @pl.when(ub >= 2)
                    def _():
                        pl.semaphore_wait(wcredit.at[0], 1)
                        pl.semaphore_wait(wcredit.at[1], 1)

                res = row_products(ub, t, dp, first_partner[t])
                for kind in (FAR, NEAR):
                    wsend[t, kind] = res[:, kind * LANE : (kind + 1) * LANE]
                w_copy(ub, t, FAR).start()

            @pl.when((s == 1) & (ub >= 0) & (ub < U))
            def _():
                res = row_products(ub, t, second_partner[t], r)
                for k in range(2):
                    wkeep[lax.rem(ub, 2), t, k] = res[:, k * LANE : (k + 1) * LANE]

        def pool_piece(k):
            @pl.when((per >= 5) & (par2 == 1) & (s >= 2))
            def _():
                if k == 0:

                    @pl.when(s == 2)
                    def _():
                        wait_all(wb_loads(jp, 0))

                pool_products(jp, 0, 2 * (s - 2) + k)
                if k == 1:

                    @pl.when(s == 3)
                    def _():
                        start_all(wb_loads(jp, 1))

            @pl.when((per >= 6) & (par2 == 0) & ((s == 1) | (s == 2)))
            def _():
                if k == 0:

                    @pl.when(s == 1)
                    def _():
                        wait_all(wb_loads(jp, 1))

                pool_products(jp, 1, 2 * (s - 1) + k)

        def send_near():
            @pl.when((s == 2) & (ub >= 0) & (ub < U))
            def _():
                for t in range(2):
                    w_copy(ub, t, NEAR).start()

        def finish_weights():
            @pl.when((s == 2) & (uz >= 0) & (uz < U))
            def _():
                j, h, u2 = lax.div(uz, 2), lax.rem(uz, 2), lax.rem(uz, 2)
                for t in range(2):
                    w_copy(uz, t, NEAR).wait_recv()
                    w_copy(uz, t, KEEP).wait_recv()
                    w_copy(uz, t, KEEP).wait_send()
                    both = wkeep[u2, t, 1].astype(F32) + wrecv[u2, t, NEAR].astype(F32)
                    both = both + wrecv[u2, t, KEEP].astype(F32)

                    @pl.when(h == 0)
                    def _():
                        @pl.when(j >= 1)
                        def _():
                            wait_all(wout_stores(j, t))

                        wout[t, 0] = both.astype(BF16)

                    @pl.when(h == 1)
                    def _():
                        first, second = wout[t, 0], both.astype(BF16)
                        for k in range(2):
                            wout[t, k] = halves(first, second, k)
                        start_all(wout_stores(j, t))

                @pl.when(uz < U - 2)
                def _():
                    signal(wcredit.at[0], rows=xp)
                    signal(wcredit.at[1], rows=yp)

            @pl.when((s == 3) & (ub >= 0) & (ub < U))
            def _():
                u2 = lax.rem(ub, 2)
                for t in range(2):
                    w_copy(ub, t, FAR).wait_recv()
                    both = wkeep[u2, t, 0].astype(F32) + wrecv[u2, t, FAR].astype(F32)
                    wkeep[u2, t, 0] = both.astype(BF16)
                    w_copy(ub, t, KEEP).start()

        @pl.when((s == 0) & (uz >= 0) & (uz < U))
        def _():
            for t in range(2):
                for kind in (FAR, NEAR):
                    w_copy(uz, t, kind).wait_send()

        @pl.when((s == 0) & (per >= 5) & (par2 == 1))
        def _():
            start_all(wb_loads(jp, 0))

        flows(0)
        share_waits()
        weight_products(0)
        flows(1)
        pool_piece(0)
        flows(2)
        send_near()
        weight_products(1)
        flows(3)
        pool_piece(1)
        flows(4)
        partial_products()
        finish_weights()

        for k in range(2):

            @pl.when((per_m >= 3) & (per_m < U) & (par_m == 1) & (lax.rem(s_m, 2) == k))
            def _():
                part_copy(0, s_m, k).wait_send()

        for b in range(NS):
            for d in (RIGHT, LEFT):
                shares = (s_m >= 1) if d == LEFT else (s_m >= 0)

                @pl.when(gathers_m & (pos[d] >= s_m))
                def _():
                    @pl.when(pos[d] < L - 1)
                    def _():
                        gath_copy(u_m, p, d, b, s_m, par_m).wait_send()

                    @pl.when(shares)
                    def _():
                        share_copy(u_m, p, c, d, b, s_m, par_m).wait_send()

                @pl.when(sums_m & (pos[d] < s_m))
                def _():
                    sum_copy(ur_m, d, b, s_m, par_m).wait_send()

        @pl.when((s == 2) & (per < SENDING - 1))
        def _():
            @pl.when(has_left)
            def _():
                signal(credit.at[1], feat=f - 2)

            @pl.when(has_right)
            def _():
                signal(credit.at[0], feat=f + 2)

            signal(credit.at[2], feat=sib)

        @pl.when(T == (U + 2) * L + 1)
        def _():
            for j in range(NCH):
                sums_of = [[jnp.sum(sacc[2 * j + h, k], axis=0, keepdims=True) for h in range(2)] for k in range(3)]
                (same, cross, bias) = sums_of
                rows_of = [halves(*same, 0), halves(*cross, 0), halves(*cross, 1), halves(*same, 1)]
                rows_of += [halves(*bias, 0), halves(*bias, 1), jnp.zeros((2, LANE), F32)]
                sred[j] = jnp.concatenate(rows_of, axis=0)
            for k, peer in enumerate((xp, yp, dp)):
                remote(sred.at[peer], srecv.at[k], st_send.at[k], st_recv.at[k], rows=peer).start()

        return carry

    lax.fori_loop(2 * L, TICKS, tick, 0)

    for k, peer in enumerate((xp, yp, dp)):
        copy = remote(sred.at[peer], srecv.at[k], st_send.at[k], st_recv.at[k], rows=peer)
        copy.wait_send()
        copy.wait_recv()
    stats[...] = sred[r] + srecv[0] + srecv[1] + srecv[2]
    for t in range(2):
        wait_all(wout_stores(NCH - 1, t))


def hand_over(mixed_a, mixed_b, acc, wg_a, wg_b, stats, *refs):
    results, (bias_a, bias_b, stitch) = refs[:6], refs[6:9]
    low, held, (load_s, store_s) = refs[9:11], refs[11:15], refs[15:]
    sources = (mixed_a, mixed_b, *held)
    loads, stores = {}, {}
    for k in range(6):
        n = results[k].shape[0] // COPIES
        for i in range(COPIES):
            some = pl.ds(i * n, n)
            if k >= 4:
                src = (wg_a, wg_b)[k - 4]
                loads[k, i] = pltpu.make_async_copy(src.at[some, :], low[k - 4].at[some, :], load_s.at[k - 4, i])
            stores[k, i] = pltpu.make_async_copy(sources[k].at[some, :], results[k].at[some, :], store_s.at[k, i])
    for load in loads.values():
        load.start()
    for (k, _), store in stores.items():
        if k < 2:
            store.start()
    bias_a[...] = stats[4:5, :]
    bias_b[...] = stats[5:6, :]
    stitch[0] = stats[0:2, :]
    stitch[1] = stats[2:4, :]
    for (k, i), store in stores.items():
        n = results[k].shape[0] // COPIES
        some = pl.ds(i * n, n)
        if k >= 4:
            loads[k, i].wait()
            held[k - 2][some, :] = low[k - 4][some, :].astype(F32)
        elif k >= 2:
            held[k - 2][some, :] = acc[k - 2, some, :].astype(BF16)
        if k >= 2:
            store.start()
    for store in stores.values():
        store.wait()


def fused(
    pool_a, pool_b, weight_a, weight_b, bias_a, bias_b, stitch, crop_count, row_mask, outgrad_a, outgrad_b
):
    rows, width = pool_a.shape
    chl = bias_a.shape[0]
    NS, L = SUBS, 4
    BIG, SMALL = rows * 3 // 10, rows // 5
    NCH = chl // LANE
    hbm = pl.BlockSpec(memory_space=pl.ANY)
    vmem = pl.BlockSpec(memory_space=pltpu.VMEM)
    dma = pltpu.SemaphoreType.DMA
    out_shape = (
        pltpu.VMEM((rows, chl), BF16),
        pltpu.VMEM((rows, chl), BF16),
        pltpu.VMEM((2, rows, width), F32),
        jax.ShapeDtypeStruct((width, 2 * chl), BF16),
        jax.ShapeDtypeStruct((width, 2 * chl), BF16),
        jax.ShapeDtypeStruct((8, LANE), F32),
    )
    results = (
        (jax.ShapeDtypeStruct((rows, chl), BF16),) * 2
        + (jax.ShapeDtypeStruct((rows, width), BF16),) * 2
        + (jax.ShapeDtypeStruct((width, 2 * chl), F32),) * 2
    )
    scratch = [
        pltpu.VMEM((2, BIG, width), BF16),
        pltpu.VMEM((2, SMALL, width), BF16),
        pltpu.VMEM((2, width, rows), BF16),
        pltpu.VMEM((2, width, L * LANE), BF16),
        pltpu.VMEM((L, width, 2 * LANE), BF16),
        pltpu.VMEM((2, L, BIG, LANE), BF16),
        pltpu.VMEM((2, L, SMALL, LANE), BF16),
        pltpu.VMEM((2, 2, L, rows, LANE), BF16),
        pltpu.VMEM((2, 2, L, rows, LANE), BF16),
        pltpu.VMEM((2, 2, 3, rows, LANE), BF16),
        pltpu.VMEM((4, L, 2, rows, LANE), BF16),
        pltpu.VMEM((2, 2, width, LANE), BF16),
        pltpu.VMEM((2, 2, 2, width, LANE), BF16),
        pltpu.VMEM((2, 2, 3, width, LANE), BF16),
        pltpu.VMEM((2, 2, width, LANE), BF16),
        pltpu.VMEM((2, rows, LANE), BF16),
        pltpu.VMEM((rows // LANE, LANE), F32),
        pltpu.VMEM((2 * NCH, 8, LANE), F32),
        pltpu.VMEM((2 * NCH, 3, 8, LANE), F32),
        pltpu.VMEM((NCH, 8, LANE), F32),
        pltpu.VMEM((3, 8, LANE), F32),
        dma((2, 2)),
        dma((2, L)),
        dma((L, 2)),
        dma((L,)),
        dma((L,)),
        dma((2, L)),
        dma((2, L)),
        dma((2, NS, L)),
        dma((2, NS, L, 2)),
        dma((2, NS, L)),
        dma((2, NS, L, 2)),
        dma((2, 3)),
        dma((2, 2, 3)),
        dma((2, 2)),
        dma((2,)),
        dma((3,)),
        dma((3,)),
        pltpu.SemaphoreType.REGULAR((3,)),
        pltpu.SemaphoreType.REGULAR((2,)),
    ]
    mixed_a, mixed_b, acc, wg_a, wg_b, stats = pl.pallas_call(
        functools.partial(kernel, rows, width, chl),
        out_shape=out_shape,
        in_specs=[hbm] * 4 + [vmem] * 5 + [hbm] * 2,
        out_specs=(vmem, vmem, vmem, hbm, hbm, vmem),
        scratch_shapes=scratch,
        compiler_params=pltpu.CompilerParams(
            collective_id=0, has_side_effects=True, vmem_limit_bytes=VMEM_LIMIT
        ),
    )(
        pool_a,
        pool_b,
        weight_a,
        weight_b,
        bias_a[None],
        bias_b[None],
        stitch,
        row_mask.reshape(rows // LANE, LANE),
        crop_count.reshape(rows // LANE, LANE),
        outgrad_a,
        outgrad_b,
    )
    held = [pltpu.with_memory_space_constraint(v, pltpu.VMEM) for v in (mixed_a, mixed_b, acc)]
    held += [pltpu.with_memory_space_constraint(v, pltpu.HBM) for v in (wg_a, wg_b)]
    held.append(stats)
    outs = pl.pallas_call(
        hand_over,
        out_shape=results
        + (
            jax.ShapeDtypeStruct((1, LANE), F32),
            jax.ShapeDtypeStruct((1, LANE), F32),
            jax.ShapeDtypeStruct((2, 2, LANE), F32),
        ),
        in_specs=[vmem, vmem, vmem, hbm, hbm, vmem],
        out_specs=(hbm,) * 6 + (vmem,) * 3,
        scratch_shapes=[pltpu.VMEM(out.shape, out.dtype) for out in out_shape[3:5] + results[2:]]
        + [dma((2, COPIES)), dma((6, COPIES))],
        compiler_params=pltpu.CompilerParams(vmem_limit_bytes=VMEM_LIMIT),
    )(*held)
    return (*outs[:6], outs[6][0], outs[7][0], outs[8])


VMEM_LIMIT = 50 * 1024 * 1024


def plain(
    pool_a, pool_b, weight_a, weight_b, bias_a, bias_b, stitch, crop_count, row_mask, outgrad_a, outgrad_b
):
    row = (row_mask.astype(F32) / crop_count.astype(F32))[:, None]

    def pre(pool, weight, bias):
        partial = dot(pool, weight).astype(BF16)
        return lax.psum_scatter(partial, "feat", scatter_dimension=1, tiled=True).astype(F32) + bias

    def gelu(v):
        cdf = 0.5 * (1.0 + lax.erf(v * INV_SQRT2))
        return v * cdf, cdf + v * (INV_SQRT_2PI * jnp.exp(-0.5 * v * v))

    act_a, slope_a = gelu(pre(pool_a, weight_a, bias_a))
    act_b, slope_b = gelu(pre(pool_b, weight_b, bias_b))
    (s00, s01), (s10, s11) = stitch[0], stitch[1]
    mixed_a = (row * (s00 * act_a + s01 * act_b)).astype(BF16)
    mixed_b = (row * (s10 * act_a + s11 * act_b)).astype(BF16)
    gy_a = row * outgrad_a.astype(F32)
    gy_b = row * outgrad_b.astype(F32)
    gpre_a = ((s00 * gy_a + s10 * gy_b) * slope_a).astype(BF16)
    gpre_b = ((s01 * gy_a + s11 * gy_b) * slope_b).astype(BF16)
    sums = jnp.stack(
        [
            jnp.sum(v, axis=0)
            for v in (
                gy_a * act_a,
                gy_a * act_b,
                gy_b * act_a,
                gy_b * act_b,
                gpre_a.astype(F32),
                gpre_b.astype(F32),
            )
        ]
    )
    sums = lax.psum_scatter(sums, "rows", scatter_dimension=1, tiled=True)

    def back(pool, weight, gpre):
        whole = lax.all_gather(gpre, "feat", axis=1, tiled=True)
        pool_grad = dot_t(whole, weight).astype(BF16)
        wgrad = lax.dot_general(pool, whole, (((0,), (0,)), ((), ())), preferred_element_type=F32)
        wgrad = lax.psum_scatter(wgrad.astype(BF16), "rows", scatter_dimension=1, tiled=True)
        return pool_grad, wgrad.astype(F32)

    pg_a, wg_a = back(pool_a, weight_a, gpre_a)
    pg_b, wg_b = back(pool_b, weight_b, gpre_b)
    return mixed_a, mixed_b, pg_a, pg_b, wg_a, wg_b, sums[4], sums[5], sums[:4].reshape(2, 2, -1)


def shards(
    pool_a, pool_b, weight_a, weight_b, bias_a, bias_b, stitch, crop_count, row_mask, outgrad_a, outgrad_b
):
    rows, width = pool_a.shape
    chl = bias_a.shape[0]
    n_rows, n_feat = lax.axis_size("rows"), lax.axis_size("feat")
    fits = (
        n_rows == 4
        and n_feat == 8
        and chl == n_rows * LANE
        and width % LANE == 0
        and width <= rows
        and rows % (2 * SUBS * LANE) == 0
    )
    run = fused if fits else plain
    return run(pool_a, pool_b, weight_a, weight_b, bias_a, bias_b, stitch, crop_count, row_mask, outgrad_a, outgrad_b)


def solution(mesh):
    return jax.shard_map(
        shards,
        mesh=mesh,
        in_specs=(
            P("rows", "feat"),
            P("rows", "feat"),
            P("feat", None),
            P("feat", None),
            P("feat"),
            P("feat"),
            P(None, None, "feat"),
            P("rows"),
            P("rows"),
            P("rows", "feat"),
            P("rows", "feat"),
        ),
        out_specs=(
            P("rows", "feat"),
            P("rows", "feat"),
            P("rows", "feat"),
            P("rows", "feat"),
            P("feat", "rows"),
            P("feat", "rows"),
            P(("feat", "rows")),
            P(("feat", "rows")),
            P(None, None, ("feat", "rows")),
        ),
        check_vma=False,
    )
```

```python
import functools

import jax
import jax.numpy as jnp
from jax import lax
from jax.experimental import pallas as pl
from jax.experimental.pallas import tpu as pltpu
from jax.sharding import PartitionSpec as P

MESH = pl.DeviceIdType.MESH
F32 = jnp.float32
BF16 = jnp.bfloat16
LANE = 128
HALF = 64
SUBS = 5
PIECES = 4
COPIES = 4
RIGHT, LEFT = 0, 1
FAR, NEAR, KEEP, OWN = 0, 1, 2, 3
INV_SQRT2 = 0.7071067811865476
INV_SQRT_2PI = 0.3989422804014327


def dot(lhs, rhs):
    return lax.dot_general(lhs, rhs, (((1,), (0,)), ((), ())), preferred_element_type=F32)


def dot_t(lhs, rhs):
    return lax.dot_general(lhs, rhs, (((1,), (1,)), ((), ())), preferred_element_type=F32)


def swap(v):
    return pltpu.roll(v, HALF, 1)


def upper(rows):
    return lax.broadcasted_iota(jnp.int32, (rows, LANE), 1) >= HALF


def halves(one, two, half):
    if half == 0:
        return jnp.where(upper(one.shape[0]), swap(two), one)
    return jnp.where(upper(one.shape[0]), two, swap(one))


def kernel(rows, width, chl, *refs):
    (
        pool_a, pool_b, weight_a, weight_b, bias_a, bias_b, stitch, mask, count, og_a, og_b,
        mixed_a, mixed_b, acc, wg_a, wg_b, stats,
        pool_0, pool_1, pool_t, wf, wb, part_0, part_1, part_own, xr, rbuf, gath, wsend, wkeep, wrecv, wout,
        og_v, scale, par, sacc, sred, srecv,
        pool_s, wf_s, wb_s, xs_send, xs_recv, x0_send, x0_recv, z_send, z_recv, g_send, g_recv,
        w_send, w_recv, wout_s, og_s, st_send, st_recv, credit, wcredit,
    ) = refs
    L = 4
    NS = SUBS
    SB = rows // NS
    BIG, SMALL = rows * 3 // 10, rows // 5
    PB = rows // PIECES
    NCH = chl // LANE
    U = 2 * NCH
    SENDING = U + 3
    TICKS = (U + 5) * L
    pools, weights = (pool_a, pool_b), (weight_a, weight_b)
    ogs, mixeds = (og_a, og_b), (mixed_a, mixed_b)
    wgs = (wg_a, wg_b)

    f = lax.axis_index("feat")
    r = lax.axis_index("rows")
    p = lax.div(f, 2)
    c = lax.rem(f, 2)
    sib = f + 1 - 2 * c
    xp = r + 1 - 2 * lax.rem(r, 2)
    yp = lax.rem(r + 2, 4)
    dp = 3 - r
    has_left, has_right = p > 0, p < L - 1
    pos = (p, L - 1 - p)
    has_up = (has_left, has_right)
    nxt = (f + 2, f - 2)

    def remote(src, dst, send, recv, **dev):
        return pltpu.make_async_remote_copy(
            src_ref=src, dst_ref=dst, send_sem=send, recv_sem=recv, device_id=dev, device_id_type=MESH
        )

    def signal(sem, **dev):
        pl.semaphore_signal(sem, inc=1, device_id=dev, device_id_type=MESH)

    def start_all(copies):
        for copy in copies:
            copy.start()

    def wait_all(copies):
        for copy in copies:
            copy.wait()

    def lanes(index):
        return pl.ds(pl.multiple_of(index * LANE, LANE), LANE)

    def some_rows(i, n):
        return pl.ds(pl.multiple_of(i * n, n), n)

    def sub_rows(b):
        return pl.ds(b * SB, SB)

    def tower_of(index, run):
        for t in range(2):

            @pl.when(lax.rem(index, 2) == t)
            def _():
                run(t)

    sizes, pool_v, part_v = (BIG, SMALL), (pool_0, pool_1), (part_0, part_1)

    def piece_rows(s, k):
        return pl.ds(pl.multiple_of(lax.div(s, 2) * (BIG + SMALL) + k * BIG, LANE), sizes[k])

    def pool_loads(s, k, towers=(0, 1)):
        return [
            pltpu.make_async_copy(pools[t].at[piece_rows(s, k), :], pool_v[k].at[t], pool_s.at[k, t])
            for t in towers
        ]

    def wf_loads(per, towers=(0, 1)):
        j = lax.div(per, 2)
        core = jnp.where(lax.rem(per, 2) == 0, c, 1 - c)
        return [
            pltpu.make_async_copy(
                weights[t].at[:, lanes((2 * q + core) * NCH + j)],
                wf.at[t, :, q * LANE : (q + 1) * LANE],
                wf_s.at[t, q],
            )
            for t in towers
            for q in range(L)
        ]

    def wb_loads(j, t):
        out = []
        for q in range(L):
            for k in range(2):
                out.append(
                    pltpu.make_async_copy(
                        weights[t].at[:, lanes((2 * q + k) * NCH + j)],
                        wb.at[q, :, k * LANE : (k + 1) * LANE],
                        wb_s.at[q, k],
                    )
                )
        return out

    def og_loads(j):
        return [pltpu.make_async_copy(ogs[t].at[:, lanes(j)], og_v.at[t], og_s.at[t]) for t in range(2)]

    def part_copy(j, s, k):
        return remote(
            part_v[k],
            xr.at[lax.rem(j, 2), :, :, piece_rows(s, k), :],
            xs_send.at[s],
            xs_recv.at[s],
            feat=sib,
        )

    def first_copy(h, s, k):
        return remote(
            part_v[k].at[lax.div(s, 2)],
            xr.at[0, h, :, piece_rows(s, k), :],
            x0_send.at[h, s],
            x0_recv.at[h, s],
            feat=sib,
        )

    def share_copy(u, o, core, d, s, par2):
        block = gath.at[lax.rem(u, 4), o, core]
        return remote(block, block, g_send.at[d, s], g_recv.at[d, s, par2], feat=sib)

    def gath_copy(u, o, d, b, s, par2):
        block = gath.at[lax.rem(u, 4), o, c, sub_rows(b), :]
        return remote(block, block, z_send.at[d, b, s], z_recv.at[d, b, s, par2], feat=nxt[d])

    def sum_block(u, d, b, s):
        return rbuf.at[lax.rem(u, 2), d, lax.rem(s, 3), sub_rows(b), :]

    def sum_copy(u, d, b, s, par2):
        return remote(
            sum_block(u, d, b, s - 1),
            sum_block(u, d, b, s),
            z_send.at[d, b, s],
            z_recv.at[d, b, s, par2],
            feat=nxt[d],
        )

    def sum_wait(u, d, b, s, par2):
        block = sum_block(u, d, b, s)
        remote(block, block, z_send.at[d, b, s], z_recv.at[d, b, s, par2], feat=nxt[d]).wait_recv()

    def packed(one, two, h):
        return jnp.where(upper(one.shape[0]) == (h == 1), one, swap(two))

    def own_sum(u, o, b):
        h, j2 = lax.rem(u, 2), lax.rem(lax.div(u, 2), 2)
        return part_own[j2, h, o, sub_rows(b), :].astype(F32) + xr[j2, h, o, sub_rows(b), :].astype(F32)

    def fold(v):
        return jnp.sum(v.reshape(SB // 8, 8, LANE), axis=0)

    def finalize(u, b, per):
        j, h = lax.div(u, 2), lax.rem(u, 2)
        last2 = lax.rem(per - 1, 2)
        for d in (RIGHT, LEFT):

            @pl.when(has_up[d])
            def _():
                sum_wait(u, d, b, L - 1, last2)

        if b == 0:

            @pl.when(h == 0)
            def _():
                wait_all(og_loads(j))

        v = own_sum(u, p, b) + par[u, 3:4, :]
        for d in (RIGHT, LEFT):
            v = v + jnp.where(has_up[d], rbuf[lax.rem(u, 2), d, 0, sub_rows(b), :].astype(F32), 0.0)
        same, cross, back = (par[u, k : k + 1, :] for k in range(3))
        row = jnp.concatenate(
            [jnp.broadcast_to(scale[k : k + 1, :], (LANE, LANE)).T for k in range(b * SB // LANE, (b + 1) * SB // LANE)],
            axis=0,
        )
        gy = row * packed(og_v[h, sub_rows(b), :].astype(F32), og_v[1 - h, sub_rows(b), :].astype(F32), h)
        cdf = 0.5 * (1.0 + lax.erf(v * INV_SQRT2))
        act = v * cdf
        slope = cdf + v * (INV_SQRT_2PI * jnp.exp(-0.5 * v * v))
        act_x = swap(act)
        mixed = row * (same * act + cross * act_x)
        gpre = ((same * gy + back * swap(gy)) * slope).astype(BF16)
        gath[lax.rem(u, 4), p, c, sub_rows(b), :] = gpre
        sacc[u, 0] += fold(gy * act)
        sacc[u, 1] += fold(gy * act_x)
        sacc[u, 2] += fold(gpre.astype(F32))

        @pl.when(h == 0)
        def _():
            mixed_a[sub_rows(b), lanes(j)] = mixed.astype(BF16)

        @pl.when(h == 1)
        def _():
            first, second = mixed_a[sub_rows(b), lanes(j)], mixed.astype(BF16)
            for t in range(2):
                mixeds[t][sub_rows(b), lanes(j)] = halves(first, second, t)

    first_partner, second_partner = (xp, yp), (yp, xp)

    def w_copy(u, t, kind):
        u2 = lax.rem(u, 2)
        return remote(
            wkeep.at[u2, t, 0] if kind == KEEP else wsend.at[t, kind],
            wrecv.at[u2, t, kind],
            w_send.at[t, kind],
            w_recv.at[u2, t, kind],
            rows=second_partner[t] if kind == KEEP else first_partner[t],
        )

    def wout_stores(j, t):
        return [
            pltpu.make_async_copy(wout.at[t, k], wgs[t].at[:, lanes(k * NCH + j)], wout_s.at[t, k])
            for k in range(2)
        ]

    def row_products(u, t, one, two):
        cols = []
        for owner in (one, two):
            pair = [gath[lax.rem(u, 4), owner, core] for core in range(2)]
            cols.append(halves(pair[0], pair[1], t))
        return dot(pool_t[t], jnp.concatenate(cols, axis=1)).astype(BF16)

    def pool_products(j, t, i):
        mine = some_rows(i, PB)
        total = None
        for q in range(L):
            cols = []
            for core in range(2):
                pair = [gath[lax.rem(2 * j + h, 4), q, core, mine, :] for h in range(2)]
                cols.append(halves(pair[0], pair[1], t))
            term = dot_t(jnp.concatenate(cols, axis=1), wb[q])
            total = term if total is None else total + term

        @pl.when(j == 0)
        def _():
            acc[t, mine, :] = total

        @pl.when(j > 0)
        def _():
            acc[t, mine, :] += total

    def first_weights(t):
        out = wf_loads(0, (t,))
        for q in range(L):
            tile, k = 2 * t + q // 2, q % 2
            out.append(
                pltpu.make_async_copy(
                    weights[t].at[:, lanes((2 * q + 1 - c) * NCH)],
                    wb.at[tile, :, k * LANE : (k + 1) * LANE],
                    wb_s.at[tile, k],
                )
            )
        return out

    start_all(first_weights(0))
    start_all(pool_loads(0, 0))
    start_all(first_weights(1))
    start_all(pool_loads(1, 1))

    bar = pltpu.get_barrier_semaphore()

    @pl.when(has_left)
    def _():
        signal(bar, feat=f - 2)

    @pl.when(has_right)
    def _():
        signal(bar, feat=f + 2)

    signal(bar, feat=sib)
    signal(bar, rows=xp)
    signal(bar, rows=yp)
    signal(bar, rows=dp)
    sacc[...] = jnp.zeros_like(sacc)
    scale[...] = mask[...].astype(F32) / count[...].astype(F32)
    for u in range(U):
        ch = slice(u // 2 * LANE, (u // 2 + 1) * LANE)
        s00, s01, s10, s11 = (stitch[k // 2, k % 2 : k % 2 + 1, ch] for k in range(4))
        rows_of = (s00, s11), (s01, s10), (s10, s01), (bias_a[:, ch], bias_b[:, ch])
        for k, (one, two) in enumerate(rows_of):
            par[u, k : k + 1, :] = halves(one, two, u % 2)

    def first_tiles(h, t):
        for q in range(L):
            mine = wf[t, :, q * LANE : (q + 1) * LANE]
            other = wb[2 * t + q // 2, :, q % 2 * LANE : (q % 2 + 1) * LANE]
            gath[3 - h, q, t, :width, :] = halves(mine, other, h)

    def first_products(h, s, k, slot, ready=None):
        res = []
        for t in range(2):
            if ready is not None:
                ready(t)
            cols = jnp.concatenate([gath[3 - h, q, t, :width, :] for q in range(L)], axis=1)
            res.append(dot(pool_v[k][t], cols).astype(BF16))
        for q in range(L):
            both = [v[:, q * LANE : (q + 1) * LANE] for v in res]
            part_own[0, h, q, piece_rows(s, k), :] = halves(*both, 0)
            part_v[k][slot, q] = halves(*both, 1)

    def arrived(t):
        wait_all(first_weights(t))
        first_tiles(0, t)
        wait_all(pool_loads(0, 0, (t,)))

    for s in range(L):
        k = s % 2
        if s > 0:
            wait_all(pool_loads(s, k))
        first_products(0, s, k, s // 2, arrived if s == 0 else None)
        if s < 3:
            start_all(pool_loads((s + 2) % L, k))
        if s == 0:
            pl.semaphore_wait(bar, 4 + has_left.astype(jnp.int32) + has_right.astype(jnp.int32))
        first_copy(0, s, k).start()
    for t in range(2):
        first_tiles(1, t)
    start_all(wf_loads(2))

    def begin_sums():
        for i in range(L):
            first_copy(0, i, i % 2).wait_recv()
        for d in (RIGHT, LEFT):

            @pl.when(pos[d] == 0)
            def _():
                for b in range(NS):
                    sum_block(0, d, b, 0)[...] = own_sum(0, p + (L - 1) * (1 - 2 * d), b).astype(BF16)
                    sum_copy(0, d, b, 1, 0).start()

    def tick(T, carry):
        per, s = lax.div(T, L), lax.rem(T, L)
        par2 = lax.rem(per, 2)
        u = per - 3
        ur = per - 2
        gathers = (u >= 0) & (u < U)
        sums = (ur >= 0) & (ur < U)

        @pl.when((s == 0) & (per >= 3) & (per < SENDING))
        def _():
            @pl.when(has_left)
            def _():
                pl.semaphore_wait(credit.at[0], 1)

            @pl.when(has_right)
            def _():
                pl.semaphore_wait(credit.at[1], 1)

            pl.semaphore_wait(credit.at[2], 1)

        @pl.when((s == 1) & sums & (par2 == 0))
        def _():
            @pl.when(ur > 0)
            def _():
                for k in range(L):
                    part_copy(lax.div(ur, 2), k, k % 2).wait_recv()

            start_all(og_loads(lax.div(ur, 2)))

        @pl.when(T == 3 * L + 1)
        def _():
            for k in range(L):
                first_copy(1, k, k % 2).wait_recv()

        before = T - 1 + L
        per_m, s_m = lax.div(before, L) - 1, lax.rem(before, L)
        par_m = lax.rem(per_m + 2, 2)
        u_m, ur_m = per_m - 3, per_m - 2
        gathers_m = (u_m >= 0) & (u_m < U)
        sums_m = (ur_m >= 0) & (ur_m < U)
        ub = per - 4
        uz = per - 5
        jp = lax.div(jnp.maximum(per - 5, 0), 2)

        def flows(b):
            @pl.when((s == 0) & gathers)
            def _():
                finalize(u, b, per)

            for d in (RIGHT, LEFT):
                gather_here = pos[d] >= s
                o = p - s if d == RIGHT else p + s
                dest = p + (L - s) if d == RIGHT else p - (L - s)

                @pl.when(gathers & gather_here)
                def _():
                    @pl.when(s >= 1)
                    def _():
                        gath_copy(u, o, d, b, s - 1, par2).wait_recv()

                    @pl.when(pos[d] < L - 1)
                    def _():
                        gath_copy(u, o, d, b, s, par2).start()

                begun = (ur == 0) & (s == 1)

                @pl.when(sums & jnp.logical_not(gather_here | begun))
                def _():
                    block = sum_block(ur, d, b, s - 1)

                    @pl.when(pos[d] >= 1)
                    def _():
                        sum_wait(ur, d, b, s - 1, par2)
                        block[...] = (own_sum(ur, dest, b) + block[...].astype(F32)).astype(BF16)

                    @pl.when(pos[d] < 1)
                    def _():
                        block[...] = own_sum(ur, dest, b).astype(BF16)

                    sum_copy(ur, d, b, s, par2).start()

        def share_starts():
            for d in (RIGHT, LEFT):
                o = p - s if d == RIGHT else p + s
                shares = (s >= 1) if d == LEFT else (s >= 0)

                @pl.when(gathers & (pos[d] >= s) & shares)
                def _():
                    share_copy(u, o, c, d, s, par2).start()

        def share_waits():
            for d in (RIGHT, LEFT):
                o = p - s_m if d == RIGHT else p + s_m
                shares = (s_m >= 1) if d == LEFT else (s_m >= 0)

                @pl.when(gathers_m & (pos[d] >= s_m) & shares)
                def _():
                    share_copy(u_m, o, 1 - c, d, s_m, par_m).wait_recv()

        def partial_products():
            @pl.when(per < U)
            def _():
                j = lax.div(per, 2)
                for k in range(2):

                    @pl.when(lax.rem(s, 2) == k)
                    def _():
                        wait_all(pool_loads(s, k))

                        @pl.when(per == 2)
                        def _():
                            first_copy(0, s, k).wait_send()
                            first_products(1, s, k, lax.div(s, 2))
                            first_copy(1, s, k).start()
                            if k == 0:

                                @pl.when(s == 0)
                                def _():
                                    begin_sums()

                        if k == 0:

                            @pl.when(s == 0)
                            def _():
                                wait_all(wf_loads(per))

                        @pl.when((per == 3) & (s < 2))
                        def _():
                            for i in range(2):
                                first_copy(1, s + 2 * i, k).wait_send()

                        @pl.when(T + 1 < U * L)
                        def _():
                            start_all(pool_loads(lax.rem(s + 1, L), 1 - k))

                        res = [dot(pool_v[k][t], wf[t]).astype(BF16) for t in range(2)]
                        for q in range(L):
                            both = [v[:, q * LANE : (q + 1) * LANE] for v in res]
                            for h in range(2):
                                block = halves(*both, h)

                                @pl.when(par2 == 0)
                                def _():
                                    part_own[lax.rem(j, 2), h, q, piece_rows(s, k), :] = block

                                @pl.when(par2 == 1)
                                def _():
                                    part_v[k][h, q] = block

                        @pl.when(par2 == 1)
                        def _():
                            part_copy(j, s, k).start()

                        @pl.when(per == 3)
                        def _():
                            for t in range(2):
                                pool_t[t, :, piece_rows(s, k)] = pool_v[k][t].T

                @pl.when((s == L - 1) & (per + 1 < U))
                def _():
                    start_all(wf_loads(per + 1))

        def weight_products(t):
            @pl.when((s == 0) & (ub >= 0) & (ub < U))
            def _():
                if t == 0:

                    @pl.when(ub >= 2)
                    def _():
                        pl.semaphore_wait(wcredit.at[0], 1)
                        pl.semaphore_wait(wcredit.at[1], 1)

                res = row_products(ub, t, dp, first_partner[t])
                for kind in (FAR, NEAR):
                    wsend[t, kind] = res[:, kind * LANE : (kind + 1) * LANE]
                w_copy(ub, t, FAR).start()

            @pl.when((s == 1) & (ub >= 0) & (ub < U))
            def _():
                res = row_products(ub, t, second_partner[t], r)
                for k in range(2):
                    wkeep[lax.rem(ub, 2), t, k] = res[:, k * LANE : (k + 1) * LANE]

        def pool_piece(k):
            @pl.when((per >= 5) & (par2 == 1) & (s >= 2))
            def _():
                if k == 0:

                    @pl.when(s == 2)
                    def _():
                        wait_all(wb_loads(jp, 0))

                pool_products(jp, 0, 2 * (s - 2) + k)
                if k == 1:

                    @pl.when(s == 3)
                    def _():
                        start_all(wb_loads(jp, 1))

            @pl.when((per >= 6) & (par2 == 0) & ((s == 1) | (s == 2)))
            def _():
                if k == 0:

                    @pl.when(s == 1)
                    def _():
                        wait_all(wb_loads(jp, 1))

                pool_products(jp, 1, 2 * (s - 1) + k)

        def send_near():
            @pl.when((s == 2) & (ub >= 0) & (ub < U))
            def _():
                for t in range(2):
                    w_copy(ub, t, NEAR).start()

        def finish_weights():
            @pl.when((s == 2) & (uz >= 0) & (uz < U))
            def _():
                j, h, u2 = lax.div(uz, 2), lax.rem(uz, 2), lax.rem(uz, 2)
                for t in range(2):
                    w_copy(uz, t, NEAR).wait_recv()
                    w_copy(uz, t, KEEP).wait_recv()
                    w_copy(uz, t, KEEP).wait_send()
                    both = wkeep[u2, t, 1].astype(F32) + wrecv[u2, t, NEAR].astype(F32)
                    both = both + wrecv[u2, t, KEEP].astype(F32)

                    @pl.when(h == 0)
                    def _():
                        @pl.when(j >= 1)
                        def _():
                            wait_all(wout_stores(j, t))

                        wout[t, 0] = both.astype(BF16)

                    @pl.when(h == 1)
                    def _():
                        first, second = wout[t, 0], both.astype(BF16)
                        for k in range(2):
                            wout[t, k] = halves(first, second, k)
                        start_all(wout_stores(j, t))

                @pl.when(uz < U - 2)
                def _():
                    signal(wcredit.at[0], rows=xp)
                    signal(wcredit.at[1], rows=yp)

            @pl.when((s == 3) & (ub >= 0) & (ub < U))
            def _():
                u2 = lax.rem(ub, 2)
                for t in range(2):
                    w_copy(ub, t, FAR).wait_recv()
                    both = wkeep[u2, t, 0].astype(F32) + wrecv[u2, t, FAR].astype(F32)
                    wkeep[u2, t, 0] = both.astype(BF16)
                    w_copy(ub, t, KEEP).start()

        @pl.when((s == 0) & (uz >= 0) & (uz < U))
        def _():
            for t in range(2):
                for kind in (FAR, NEAR):
                    w_copy(uz, t, kind).wait_send()

        @pl.when((s == 0) & (per >= 5) & (par2 == 1))
        def _():
            start_all(wb_loads(jp, 0))

        flows(0)
        flows(1)
        share_waits()
        weight_products(0)
        flows(2)
        send_near()
        weight_products(1)
        flows(3)
        pool_piece(0)
        flows(4)
        share_starts()
        pool_piece(1)
        partial_products()
        finish_weights()

        for k in range(2):

            @pl.when((per_m >= 3) & (per_m < U) & (par_m == 1) & (lax.rem(s_m, 2) == k))
            def _():
                part_copy(0, s_m, k).wait_send()

        for d in (RIGHT, LEFT):
            shares = (s_m >= 1) if d == LEFT else (s_m >= 0)

            @pl.when(gathers_m & (pos[d] >= s_m) & shares)
            def _():
                share_copy(u_m, p, c, d, s_m, par_m).wait_send()

        for b in range(NS):
            for d in (RIGHT, LEFT):

                @pl.when(gathers_m & (pos[d] >= s_m) & (pos[d] < L - 1))
                def _():
                    gath_copy(u_m, p, d, b, s_m, par_m).wait_send()

                @pl.when(sums_m & (pos[d] < s_m))
                def _():
                    sum_copy(ur_m, d, b, s_m, par_m).wait_send()

        @pl.when((s == 2) & (per < SENDING - 1))
        def _():
            @pl.when(has_left)
            def _():
                signal(credit.at[1], feat=f - 2)

            @pl.when(has_right)
            def _():
                signal(credit.at[0], feat=f + 2)

            signal(credit.at[2], feat=sib)

        @pl.when(T == (U + 2) * L + 1)
        def _():
            for j in range(NCH):
                sums_of = [[jnp.sum(sacc[2 * j + h, k], axis=0, keepdims=True) for h in range(2)] for k in range(3)]
                (same, cross, bias) = sums_of
                rows_of = [halves(*same, 0), halves(*cross, 0), halves(*cross, 1), halves(*same, 1)]
                rows_of += [halves(*bias, 0), halves(*bias, 1), jnp.zeros((2, LANE), F32)]
                sred[j] = jnp.concatenate(rows_of, axis=0)
            for k, peer in enumerate((xp, yp, dp)):
                remote(sred.at[peer], srecv.at[k], st_send.at[k], st_recv.at[k], rows=peer).start()

        return carry

    lax.fori_loop(2 * L, TICKS, tick, 0)

    for k, peer in enumerate((xp, yp, dp)):
        copy = remote(sred.at[peer], srecv.at[k], st_send.at[k], st_recv.at[k], rows=peer)
        copy.wait_send()
        copy.wait_recv()
    stats[...] = sred[r] + srecv[0] + srecv[1] + srecv[2]
    for t in range(2):
        wait_all(wout_stores(NCH - 1, t))


def hand_over(mixed_a, mixed_b, acc, wg_a, wg_b, stats, *refs):
    results, (bias_a, bias_b, stitch) = refs[:6], refs[6:9]
    low, held, (load_s, store_s) = refs[9:11], refs[11:15], refs[15:]
    sources = (mixed_a, mixed_b, *held)
    loads, stores = {}, {}
    for k in range(6):
        n = results[k].shape[0] // COPIES
        for i in range(COPIES):
            some = pl.ds(i * n, n)
            if k >= 4:
                src = (wg_a, wg_b)[k - 4]
                loads[k, i] = pltpu.make_async_copy(src.at[some, :], low[k - 4].at[some, :], load_s.at[k - 4, i])
            stores[k, i] = pltpu.make_async_copy(sources[k].at[some, :], results[k].at[some, :], store_s.at[k, i])
    for load in loads.values():
        load.start()
    for (k, _), store in stores.items():
        if k < 2:
            store.start()
    bias_a[...] = stats[4:5, :]
    bias_b[...] = stats[5:6, :]
    stitch[0] = stats[0:2, :]
    stitch[1] = stats[2:4, :]
    for (k, i), store in stores.items():
        n = results[k].shape[0] // COPIES
        some = pl.ds(i * n, n)
        if k >= 4:
            loads[k, i].wait()
            held[k - 2][some, :] = low[k - 4][some, :].astype(F32)
        elif k >= 2:
            held[k - 2][some, :] = acc[k - 2, some, :].astype(BF16)
        if k >= 2:
            store.start()
    for store in stores.values():
        store.wait()


def fused(
    pool_a, pool_b, weight_a, weight_b, bias_a, bias_b, stitch, crop_count, row_mask, outgrad_a, outgrad_b
):
    rows, width = pool_a.shape
    chl = bias_a.shape[0]
    NS, L = SUBS, 4
    BIG, SMALL = rows * 3 // 10, rows // 5
    NCH = chl // LANE
    hbm = pl.BlockSpec(memory_space=pl.ANY)
    vmem = pl.BlockSpec(memory_space=pltpu.VMEM)
    dma = pltpu.SemaphoreType.DMA
    out_shape = (
        pltpu.VMEM((rows, chl), BF16),
        pltpu.VMEM((rows, chl), BF16),
        pltpu.VMEM((2, rows, width), F32),
        jax.ShapeDtypeStruct((width, 2 * chl), BF16),
        jax.ShapeDtypeStruct((width, 2 * chl), BF16),
        jax.ShapeDtypeStruct((8, LANE), F32),
    )
    results = (
        (jax.ShapeDtypeStruct((rows, chl), BF16),) * 2
        + (jax.ShapeDtypeStruct((rows, width), BF16),) * 2
        + (jax.ShapeDtypeStruct((width, 2 * chl), F32),) * 2
    )
    scratch = [
        pltpu.VMEM((2, BIG, width), BF16),
        pltpu.VMEM((2, SMALL, width), BF16),
        pltpu.VMEM((2, width, rows), BF16),
        pltpu.VMEM((2, width, L * LANE), BF16),
        pltpu.VMEM((L, width, 2 * LANE), BF16),
        pltpu.VMEM((2, L, BIG, LANE), BF16),
        pltpu.VMEM((2, L, SMALL, LANE), BF16),
        pltpu.VMEM((2, 2, L, rows, LANE), BF16),
        pltpu.VMEM((2, 2, L, rows, LANE), BF16),
        pltpu.VMEM((2, 2, 3, rows, LANE), BF16),
        pltpu.VMEM((4, L, 2, rows, LANE), BF16),
        pltpu.VMEM((2, 2, width, LANE), BF16),
        pltpu.VMEM((2, 2, 2, width, LANE), BF16),
        pltpu.VMEM((2, 2, 3, width, LANE), BF16),
        pltpu.VMEM((2, 2, width, LANE), BF16),
        pltpu.VMEM((2, rows, LANE), BF16),
        pltpu.VMEM((rows // LANE, LANE), F32),
        pltpu.VMEM((2 * NCH, 8, LANE), F32),
        pltpu.VMEM((2 * NCH, 3, 8, LANE), F32),
        pltpu.VMEM((NCH, 8, LANE), F32),
        pltpu.VMEM((3, 8, LANE), F32),
        dma((2, 2)),
        dma((2, L)),
        dma((L, 2)),
        dma((L,)),
        dma((L,)),
        dma((2, L)),
        dma((2, L)),
        dma((2, NS, L)),
        dma((2, NS, L, 2)),
        dma((2, L)),
        dma((2, L, 2)),
        dma((2, 3)),
        dma((2, 2, 3)),
        dma((2, 2)),
        dma((2,)),
        dma((3,)),
        dma((3,)),
        pltpu.SemaphoreType.REGULAR((3,)),
        pltpu.SemaphoreType.REGULAR((2,)),
    ]
    mixed_a, mixed_b, acc, wg_a, wg_b, stats = pl.pallas_call(
        functools.partial(kernel, rows, width, chl),
        out_shape=out_shape,
        in_specs=[hbm] * 4 + [vmem] * 5 + [hbm] * 2,
        out_specs=(vmem, vmem, vmem, hbm, hbm, vmem),
        scratch_shapes=scratch,
        compiler_params=pltpu.CompilerParams(
            collective_id=0, has_side_effects=True, vmem_limit_bytes=VMEM_LIMIT
        ),
    )(
        pool_a,
        pool_b,
        weight_a,
        weight_b,
        bias_a[None],
        bias_b[None],
        stitch,
        row_mask.reshape(rows // LANE, LANE),
        crop_count.reshape(rows // LANE, LANE),
        outgrad_a,
        outgrad_b,
    )
    held = [pltpu.with_memory_space_constraint(v, pltpu.VMEM) for v in (mixed_a, mixed_b, acc)]
    held += [pltpu.with_memory_space_constraint(v, pltpu.HBM) for v in (wg_a, wg_b)]
    held.append(stats)
    outs = pl.pallas_call(
        hand_over,
        out_shape=results
        + (
            jax.ShapeDtypeStruct((1, LANE), F32),
            jax.ShapeDtypeStruct((1, LANE), F32),
            jax.ShapeDtypeStruct((2, 2, LANE), F32),
        ),
        in_specs=[vmem, vmem, vmem, hbm, hbm, vmem],
        out_specs=(hbm,) * 6 + (vmem,) * 3,
        scratch_shapes=[pltpu.VMEM(out.shape, out.dtype) for out in out_shape[3:5] + results[2:]]
        + [dma((2, COPIES)), dma((6, COPIES))],
        compiler_params=pltpu.CompilerParams(vmem_limit_bytes=VMEM_LIMIT),
    )(*held)
    return (*outs[:6], outs[6][0], outs[7][0], outs[8])


VMEM_LIMIT = 50 * 1024 * 1024


def plain(
    pool_a, pool_b, weight_a, weight_b, bias_a, bias_b, stitch, crop_count, row_mask, outgrad_a, outgrad_b
):
    row = (row_mask.astype(F32) / crop_count.astype(F32))[:, None]

    def pre(pool, weight, bias):
        partial = dot(pool, weight).astype(BF16)
        return lax.psum_scatter(partial, "feat", scatter_dimension=1, tiled=True).astype(F32) + bias

    def gelu(v):
        cdf = 0.5 * (1.0 + lax.erf(v * INV_SQRT2))
        return v * cdf, cdf + v * (INV_SQRT_2PI * jnp.exp(-0.5 * v * v))

    act_a, slope_a = gelu(pre(pool_a, weight_a, bias_a))
    act_b, slope_b = gelu(pre(pool_b, weight_b, bias_b))
    (s00, s01), (s10, s11) = stitch[0], stitch[1]
    mixed_a = (row * (s00 * act_a + s01 * act_b)).astype(BF16)
    mixed_b = (row * (s10 * act_a + s11 * act_b)).astype(BF16)
    gy_a = row * outgrad_a.astype(F32)
    gy_b = row * outgrad_b.astype(F32)
    gpre_a = ((s00 * gy_a + s10 * gy_b) * slope_a).astype(BF16)
    gpre_b = ((s01 * gy_a + s11 * gy_b) * slope_b).astype(BF16)
    sums = jnp.stack(
        [
            jnp.sum(v, axis=0)
            for v in (
                gy_a * act_a,
                gy_a * act_b,
                gy_b * act_a,
                gy_b * act_b,
                gpre_a.astype(F32),
                gpre_b.astype(F32),
            )
        ]
    )
    sums = lax.psum_scatter(sums, "rows", scatter_dimension=1, tiled=True)

    def back(pool, weight, gpre):
        whole = lax.all_gather(gpre, "feat", axis=1, tiled=True)
        pool_grad = dot_t(whole, weight).astype(BF16)
        wgrad = lax.dot_general(pool, whole, (((0,), (0,)), ((), ())), preferred_element_type=F32)
        wgrad = lax.psum_scatter(wgrad.astype(BF16), "rows", scatter_dimension=1, tiled=True)
        return pool_grad, wgrad.astype(F32)

    pg_a, wg_a = back(pool_a, weight_a, gpre_a)
    pg_b, wg_b = back(pool_b, weight_b, gpre_b)
    return mixed_a, mixed_b, pg_a, pg_b, wg_a, wg_b, sums[4], sums[5], sums[:4].reshape(2, 2, -1)


def shards(
    pool_a, pool_b, weight_a, weight_b, bias_a, bias_b, stitch, crop_count, row_mask, outgrad_a, outgrad_b
):
    rows, width = pool_a.shape
    chl = bias_a.shape[0]
    n_rows, n_feat = lax.axis_size("rows"), lax.axis_size("feat")
    fits = (
        n_rows == 4
        and n_feat == 8
        and chl == n_rows * LANE
        and width % LANE == 0
        and width <= rows
        and rows % (2 * SUBS * LANE) == 0
    )
    run = fused if fits else plain
    return run(pool_a, pool_b, weight_a, weight_b, bias_a, bias_b, stitch, crop_count, row_mask, outgrad_a, outgrad_b)


def solution(mesh):
    return jax.shard_map(
        shards,
        mesh=mesh,
        in_specs=(
            P("rows", "feat"),
            P("rows", "feat"),
            P("feat", None),
            P("feat", None),
            P("feat"),
            P("feat"),
            P(None, None, "feat"),
            P("rows"),
            P("rows"),
            P("rows", "feat"),
            P("rows", "feat"),
        ),
        out_specs=(
            P("rows", "feat"),
            P("rows", "feat"),
            P("rows", "feat"),
            P("rows", "feat"),
            P("feat", "rows"),
            P("feat", "rows"),
            P(("feat", "rows")),
            P(("feat", "rows")),
            P(None, None, ("feat", "rows")),
        ),
        check_vma=False,
    )
```

```python
import functools

import jax
import jax.numpy as jnp
from jax import lax
from jax.experimental import pallas as pl
from jax.experimental.pallas import tpu as pltpu
from jax.sharding import PartitionSpec as P

MESH = pl.DeviceIdType.MESH
F32 = jnp.float32
BF16 = jnp.bfloat16
LANE = 128
HALF = 64
SUBS = 5
PIECES = 4
COPIES = 4
RIGHT, LEFT = 0, 1
FAR, NEAR, KEEP, OWN = 0, 1, 2, 3
INV_SQRT2 = 0.7071067811865476
INV_SQRT_2PI = 0.3989422804014327


def dot(lhs, rhs):
    return lax.dot_general(lhs, rhs, (((1,), (0,)), ((), ())), preferred_element_type=F32)


def dot_t(lhs, rhs):
    return lax.dot_general(lhs, rhs, (((1,), (1,)), ((), ())), preferred_element_type=F32)


def swap(v):
    return pltpu.roll(v, HALF, 1)


def upper(rows):
    return lax.broadcasted_iota(jnp.int32, (rows, LANE), 1) >= HALF


def halves(one, two, half):
    if half == 0:
        return jnp.where(upper(one.shape[0]), swap(two), one)
    return jnp.where(upper(one.shape[0]), two, swap(one))


def kernel(rows, width, chl, *refs):
    (
        pool_a, pool_b, weight_a, weight_b, bias_a, bias_b, stitch, mask, count, og_a, og_b,
        mixed_a, mixed_b, acc, wg_a, wg_b, stats,
        pool_0, pool_1, pool_t, wf, wb, part_0, part_1, part_own, xr, rbuf, gath, wsend, wkeep, wrecv, wout,
        og_v, scale, par, sacc, sred, srecv,
        pool_s, wf_s, wb_s, xs_send, xs_recv, x0_send, x0_recv, z_send, z_recv, g_send, g_recv,
        w_send, w_recv, wout_s, og_s, st_send, st_recv, credit, wcredit,
    ) = refs
    L = 4
    NS = SUBS
    SB = rows // NS
    BIG, SMALL = rows * 3 // 10, rows // 5
    PB = rows // PIECES
    NCH = chl // LANE
    U = 2 * NCH
    SENDING = U + 3
    TICKS = (U + 5) * L
    pools, weights = (pool_a, pool_b), (weight_a, weight_b)
    ogs, mixeds = (og_a, og_b), (mixed_a, mixed_b)
    wgs = (wg_a, wg_b)

    f = lax.axis_index("feat")
    r = lax.axis_index("rows")
    p = lax.div(f, 2)
    c = lax.rem(f, 2)
    sib = f + 1 - 2 * c
    xp = r + 1 - 2 * lax.rem(r, 2)
    yp = lax.rem(r + 2, 4)
    dp = 3 - r
    has_left, has_right = p > 0, p < L - 1
    pos = (p, L - 1 - p)
    has_up = (has_left, has_right)
    nxt = (f + 2, f - 2)

    def remote(src, dst, send, recv, **dev):
        return pltpu.make_async_remote_copy(
            src_ref=src, dst_ref=dst, send_sem=send, recv_sem=recv, device_id=dev, device_id_type=MESH
        )

    def signal(sem, **dev):
        pl.semaphore_signal(sem, inc=1, device_id=dev, device_id_type=MESH)

    def start_all(copies):
        for copy in copies:
            copy.start()

    def wait_all(copies):
        for copy in copies:
            copy.wait()

    def lanes(index):
        return pl.ds(pl.multiple_of(index * LANE, LANE), LANE)

    def some_rows(i, n):
        return pl.ds(pl.multiple_of(i * n, n), n)

    def sub_rows(b):
        return pl.ds(b * SB, SB)

    def tower_of(index, run):
        for t in range(2):

            @pl.when(lax.rem(index, 2) == t)
            def _():
                run(t)

    sizes, pool_v, part_v = (BIG, SMALL), (pool_0, pool_1), (part_0, part_1)

    def piece_rows(s, k):
        return pl.ds(pl.multiple_of(lax.div(s, 2) * (BIG + SMALL) + k * BIG, LANE), sizes[k])

    def pool_loads(s, k, towers=(0, 1)):
        return [
            pltpu.make_async_copy(pools[t].at[piece_rows(s, k), :], pool_v[k].at[t], pool_s.at[k, t])
            for t in towers
        ]

    def wf_loads(per, towers=(0, 1)):
        j = lax.div(per, 2)
        core = jnp.where(lax.rem(per, 2) == 0, c, 1 - c)
        return [
            pltpu.make_async_copy(
                weights[t].at[:, lanes((2 * q + core) * NCH + j)],
                wf.at[t, :, q * LANE : (q + 1) * LANE],
                wf_s.at[t, q],
            )
            for t in towers
            for q in range(L)
        ]

    def wb_loads(j, t):
        out = []
        for q in range(L):
            for k in range(2):
                out.append(
                    pltpu.make_async_copy(
                        weights[t].at[:, lanes((2 * q + k) * NCH + j)],
                        wb.at[q, :, k * LANE : (k + 1) * LANE],
                        wb_s.at[q, k],
                    )
                )
        return out

    def og_loads(j):
        return [pltpu.make_async_copy(ogs[t].at[:, lanes(j)], og_v.at[t], og_s.at[t]) for t in range(2)]

    def part_copy(j, s, k):
        return remote(
            part_v[k],
            xr.at[lax.rem(j, 2), :, :, piece_rows(s, k), :],
            xs_send.at[s],
            xs_recv.at[s],
            feat=sib,
        )

    def first_copy(h, s, k):
        return remote(
            part_v[k].at[lax.div(s, 2)],
            xr.at[0, h, :, piece_rows(s, k), :],
            x0_send.at[h, s],
            x0_recv.at[h, s],
            feat=sib,
        )

    def share_copy(u, o, core, d, s, par2):
        block = gath.at[lax.rem(u, 4), o, core]
        return remote(block, block, g_send.at[d, s], g_recv.at[d, s, par2], feat=sib)

    def gath_copy(u, o, d, b, s, par2):
        block = gath.at[lax.rem(u, 4), o, c, sub_rows(b), :]
        return remote(block, block, z_send.at[d, b, s], z_recv.at[d, b, s, par2], feat=nxt[d])

    def sum_block(u, d, b, s):
        return rbuf.at[lax.rem(u, 2), d, lax.rem(s, 3), sub_rows(b), :]

    def sum_copy(u, d, b, s, par2):
        return remote(
            sum_block(u, d, b, s - 1),
            sum_block(u, d, b, s),
            z_send.at[d, b, s],
            z_recv.at[d, b, s, par2],
            feat=nxt[d],
        )

    def sum_wait(u, d, b, s, par2):
        block = sum_block(u, d, b, s)
        remote(block, block, z_send.at[d, b, s], z_recv.at[d, b, s, par2], feat=nxt[d]).wait_recv()

    def packed(one, two, h):
        return jnp.where(upper(one.shape[0]) == (h == 1), one, swap(two))

    def own_sum(u, o, b):
        h, j2 = lax.rem(u, 2), lax.rem(lax.div(u, 2), 2)
        return part_own[j2, h, o, sub_rows(b), :].astype(F32) + xr[j2, h, o, sub_rows(b), :].astype(F32)

    def fold(v):
        return jnp.sum(v.reshape(SB // 8, 8, LANE), axis=0)

    def finalize(u, b, per):
        j, h = lax.div(u, 2), lax.rem(u, 2)
        last2 = lax.rem(per - 1, 2)
        for d in (RIGHT, LEFT):

            @pl.when(has_up[d])
            def _():
                sum_wait(u, d, b, L - 1, last2)

        if b == 0:

            @pl.when(h == 0)
            def _():
                wait_all(og_loads(j))

        v = own_sum(u, p, b) + par[u, 3:4, :]
        for d in (RIGHT, LEFT):
            v = v + jnp.where(has_up[d], rbuf[lax.rem(u, 2), d, 0, sub_rows(b), :].astype(F32), 0.0)
        same, cross, back = (par[u, k : k + 1, :] for k in range(3))
        row = jnp.concatenate(
            [jnp.broadcast_to(scale[k : k + 1, :], (LANE, LANE)).T for k in range(b * SB // LANE, (b + 1) * SB // LANE)],
            axis=0,
        )
        gy = row * packed(og_v[h, sub_rows(b), :].astype(F32), og_v[1 - h, sub_rows(b), :].astype(F32), h)
        cdf = 0.5 * (1.0 + lax.erf(v * INV_SQRT2))
        act = v * cdf
        slope = cdf + v * (INV_SQRT_2PI * jnp.exp(-0.5 * v * v))
        act_x = swap(act)
        mixed = row * (same * act + cross * act_x)
        gpre = ((same * gy + back * swap(gy)) * slope).astype(BF16)
        gath[lax.rem(u, 4), p, c, sub_rows(b), :] = gpre
        sacc[u, 0] += fold(gy * act)
        sacc[u, 1] += fold(gy * act_x)
        sacc[u, 2] += fold(gpre.astype(F32))

        @pl.when(h == 0)
        def _():
            mixed_a[sub_rows(b), lanes(j)] = mixed.astype(BF16)

        @pl.when(h == 1)
        def _():
            first, second = mixed_a[sub_rows(b), lanes(j)], mixed.astype(BF16)
            for t in range(2):
                mixeds[t][sub_rows(b), lanes(j)] = halves(first, second, t)

    first_partner, second_partner = (xp, yp), (yp, xp)

    def w_copy(u, t, kind):
        u2 = lax.rem(u, 2)
        return remote(
            wkeep.at[u2, t, 0] if kind == KEEP else wsend.at[t, kind],
            wrecv.at[u2, t, kind],
            w_send.at[t, kind],
            w_recv.at[u2, t, kind],
            rows=second_partner[t] if kind == KEEP else first_partner[t],
        )

    def wout_stores(j, t):
        return [
            pltpu.make_async_copy(wout.at[t, k], wgs[t].at[:, lanes(k * NCH + j)], wout_s.at[t, k])
            for k in range(2)
        ]

    def row_products(u, t, one, two):
        cols = []
        for owner in (one, two):
            pair = [gath[lax.rem(u, 4), owner, core] for core in range(2)]
            cols.append(halves(pair[0], pair[1], t))
        return dot(pool_t[t], jnp.concatenate(cols, axis=1)).astype(BF16)

    def pool_products(j, t, i):
        mine = some_rows(i, PB)
        total = None
        for q in range(L):
            cols = []
            for core in range(2):
                pair = [gath[lax.rem(2 * j + h, 4), q, core, mine, :] for h in range(2)]
                cols.append(halves(pair[0], pair[1], t))
            term = dot_t(jnp.concatenate(cols, axis=1), wb[q])
            total = term if total is None else total + term

        @pl.when(j == 0)
        def _():
            acc[t, mine, :] = total

        @pl.when(j > 0)
        def _():
            acc[t, mine, :] += total

    def first_weights(t):
        out = wf_loads(0, (t,))
        for q in range(L):
            tile, k = 2 * t + q // 2, q % 2
            out.append(
                pltpu.make_async_copy(
                    weights[t].at[:, lanes((2 * q + 1 - c) * NCH)],
                    wb.at[tile, :, k * LANE : (k + 1) * LANE],
                    wb_s.at[tile, k],
                )
            )
        return out

    start_all(first_weights(0))
    start_all(pool_loads(0, 0))
    start_all(first_weights(1))
    start_all(pool_loads(1, 1))

    bar = pltpu.get_barrier_semaphore()

    @pl.when(has_left)
    def _():
        signal(bar, feat=f - 2)

    @pl.when(has_right)
    def _():
        signal(bar, feat=f + 2)

    signal(bar, feat=sib)
    signal(bar, rows=xp)
    signal(bar, rows=yp)
    signal(bar, rows=dp)
    sacc[...] = jnp.zeros_like(sacc)
    scale[...] = mask[...].astype(F32) / count[...].astype(F32)
    for u in range(U):
        ch = slice(u // 2 * LANE, (u // 2 + 1) * LANE)
        s00, s01, s10, s11 = (stitch[k // 2, k % 2 : k % 2 + 1, ch] for k in range(4))
        rows_of = (s00, s11), (s01, s10), (s10, s01), (bias_a[:, ch], bias_b[:, ch])
        for k, (one, two) in enumerate(rows_of):
            par[u, k : k + 1, :] = halves(one, two, u % 2)

    def first_tiles(h, t):
        for q in range(L):
            mine = wf[t, :, q * LANE : (q + 1) * LANE]
            other = wb[2 * t + q // 2, :, q % 2 * LANE : (q % 2 + 1) * LANE]
            gath[3 - h, q, t, :width, :] = halves(mine, other, h)

    def first_products(h, s, k, slot, ready=None):
        res = []
        for t in range(2):
            if ready is not None:
                ready(t)
            cols = jnp.concatenate([gath[3 - h, q, t, :width, :] for q in range(L)], axis=1)
            res.append(dot(pool_v[k][t], cols).astype(BF16))
        for q in range(L):
            both = [v[:, q * LANE : (q + 1) * LANE] for v in res]
            part_own[0, h, q, piece_rows(s, k), :] = halves(*both, 0)
            part_v[k][slot, q] = halves(*both, 1)

    def arrived(t):
        wait_all(first_weights(t))
        first_tiles(0, t)
        wait_all(pool_loads(0, 0, (t,)))

    for s in range(L):
        k = s % 2
        if s > 0:
            wait_all(pool_loads(s, k))
        first_products(0, s, k, s // 2, arrived if s == 0 else None)
        if s < 3:
            start_all(pool_loads((s + 2) % L, k))
        if s == 0:
            pl.semaphore_wait(bar, 4 + has_left.astype(jnp.int32) + has_right.astype(jnp.int32))
        first_copy(0, s, k).start()
    for t in range(2):
        first_tiles(1, t)
    start_all(wf_loads(2))

    def begin_sums():
        for i in range(L):
            first_copy(0, i, i % 2).wait_recv()
        for d in (RIGHT, LEFT):

            @pl.when(pos[d] == 0)
            def _():
                for b in range(NS):
                    sum_block(0, d, b, 0)[...] = own_sum(0, p + (L - 1) * (1 - 2 * d), b).astype(BF16)
                    sum_copy(0, d, b, 1, 0).start()

    def tick(T, carry):
        per, s = lax.div(T, L), lax.rem(T, L)
        par2 = lax.rem(per, 2)
        u = per - 3
        ur = per - 2
        gathers = (u >= 0) & (u < U)
        sums = (ur >= 0) & (ur < U)

        @pl.when((s == 0) & (per >= 3) & (per < SENDING))
        def _():
            @pl.when(has_left)
            def _():
                pl.semaphore_wait(credit.at[0], 1)

            @pl.when(has_right)
            def _():
                pl.semaphore_wait(credit.at[1], 1)

            pl.semaphore_wait(credit.at[2], 1)

        @pl.when((s == 1) & sums & (par2 == 0))
        def _():
            @pl.when(ur > 0)
            def _():
                for k in range(L):
                    part_copy(lax.div(ur, 2), k, k % 2).wait_recv()

            start_all(og_loads(lax.div(ur, 2)))

        @pl.when(T == 3 * L + 1)
        def _():
            for k in range(L):
                first_copy(1, k, k % 2).wait_recv()

        before = T - 1 + L
        per_m, s_m = lax.div(before, L) - 1, lax.rem(before, L)
        par_m = lax.rem(per_m + 2, 2)
        u_m, ur_m = per_m - 3, per_m - 2
        gathers_m = (u_m >= 0) & (u_m < U)
        sums_m = (ur_m >= 0) & (ur_m < U)
        ub = per - 4
        uz = per - 5
        jp = lax.div(jnp.maximum(per - 5, 0), 2)

        def flows(b):
            @pl.when((s == 0) & gathers)
            def _():
                finalize(u, b, per)

            for d in (RIGHT, LEFT):
                gather_here = pos[d] >= s
                o = p - s if d == RIGHT else p + s
                dest = p + (L - s) if d == RIGHT else p - (L - s)

                @pl.when(gathers & gather_here)
                def _():
                    @pl.when(s >= 1)
                    def _():
                        gath_copy(u, o, d, b, s - 1, par2).wait_recv()

                    @pl.when(pos[d] < L - 1)
                    def _():
                        gath_copy(u, o, d, b, s, par2).start()

                begun = (ur == 0) & (s == 1)

                @pl.when(sums & jnp.logical_not(gather_here | begun))
                def _():
                    block = sum_block(ur, d, b, s - 1)

                    @pl.when(pos[d] >= 1)
                    def _():
                        sum_wait(ur, d, b, s - 1, par2)
                        block[...] = (own_sum(ur, dest, b) + block[...].astype(F32)).astype(BF16)

                    @pl.when(pos[d] < 1)
                    def _():
                        block[...] = own_sum(ur, dest, b).astype(BF16)

                    sum_copy(ur, d, b, s, par2).start()

        def share_starts():
            for d in (RIGHT, LEFT):
                o = p - s if d == RIGHT else p + s
                shares = (s >= 1) if d == LEFT else (s >= 0)

                @pl.when(gathers & (pos[d] >= s) & shares)
                def _():
                    share_copy(u, o, c, d, s, par2).start()

        def share_waits():
            for d in (RIGHT, LEFT):
                o = p - s_m if d == RIGHT else p + s_m
                shares = (s_m >= 1) if d == LEFT else (s_m >= 0)

                @pl.when(gathers_m & (pos[d] >= s_m) & shares)
                def _():
                    share_copy(u_m, o, 1 - c, d, s_m, par_m).wait_recv()

        def partial_products():
            @pl.when(per < U)
            def _():
                j = lax.div(per, 2)
                for k in range(2):

                    @pl.when(lax.rem(s, 2) == k)
                    def _():
                        wait_all(pool_loads(s, k))

                        @pl.when(per == 2)
                        def _():
                            if k == 0:

                                @pl.when(s == 0)
                                def _():
                                    begin_sums()

                            first_copy(0, s, k).wait_send()
                            first_products(1, s, k, lax.div(s, 2))
                            first_copy(1, s, k).start()
                        if k == 0:

                            @pl.when(s == 0)
                            def _():
                                wait_all(wf_loads(per))

                        @pl.when((per == 3) & (s < 2))
                        def _():
                            for i in range(2):
                                first_copy(1, s + 2 * i, k).wait_send()

                        @pl.when(T + 1 < U * L)
                        def _():
                            start_all(pool_loads(lax.rem(s + 1, L), 1 - k))

                        res = [dot(pool_v[k][t], wf[t]).astype(BF16) for t in range(2)]
                        for q in range(L):
                            both = [v[:, q * LANE : (q + 1) * LANE] for v in res]
                            for h in range(2):
                                block = halves(*both, h)

                                @pl.when(par2 == 0)
                                def _():
                                    part_own[lax.rem(j, 2), h, q, piece_rows(s, k), :] = block

                                @pl.when(par2 == 1)
                                def _():
                                    part_v[k][h, q] = block

                        @pl.when(par2 == 1)
                        def _():
                            part_copy(j, s, k).start()

                        @pl.when(per == 3)
                        def _():
                            for t in range(2):
                                pool_t[t, :, piece_rows(s, k)] = pool_v[k][t].T

                @pl.when((s == L - 1) & (per + 1 < U))
                def _():
                    start_all(wf_loads(per + 1))

        def weight_products(t):
            @pl.when((s == 0) & (ub >= 0) & (ub < U))
            def _():
                if t == 0:

                    @pl.when(ub >= 2)
                    def _():
                        pl.semaphore_wait(wcredit.at[0], 1)
                        pl.semaphore_wait(wcredit.at[1], 1)

                res = row_products(ub, t, dp, first_partner[t])
                for kind in (FAR, NEAR):
                    wsend[t, kind] = res[:, kind * LANE : (kind + 1) * LANE]
                w_copy(ub, t, FAR).start()

            @pl.when((s == 1) & (ub >= 0) & (ub < U))
            def _():
                res = row_products(ub, t, second_partner[t], r)
                for k in range(2):
                    wkeep[lax.rem(ub, 2), t, k] = res[:, k * LANE : (k + 1) * LANE]

        def pool_piece(k):
            @pl.when((per >= 5) & (par2 == 1) & (s >= 2))
            def _():
                if k == 0:

                    @pl.when(s == 2)
                    def _():
                        wait_all(wb_loads(jp, 0))

                pool_products(jp, 0, 2 * (s - 2) + k)
                if k == 1:

                    @pl.when(s == 3)
                    def _():
                        start_all(wb_loads(jp, 1))

            @pl.when((per >= 6) & (par2 == 0) & ((s == 1) | (s == 2)))
            def _():
                if k == 0:

                    @pl.when(s == 1)
                    def _():
                        wait_all(wb_loads(jp, 1))

                pool_products(jp, 1, 2 * (s - 1) + k)

        def send_near():
            @pl.when((s == 1) & (ub >= 0) & (ub < U))
            def _():
                for t in range(2):
                    w_copy(ub, t, NEAR).start()

        def finish_weights():
            @pl.when((s == 2) & (uz >= 0) & (uz < U))
            def _():
                j, h, u2 = lax.div(uz, 2), lax.rem(uz, 2), lax.rem(uz, 2)
                for t in range(2):
                    w_copy(uz, t, NEAR).wait_recv()
                    w_copy(uz, t, KEEP).wait_recv()
                    w_copy(uz, t, KEEP).wait_send()
                    both = wkeep[u2, t, 1].astype(F32) + wrecv[u2, t, NEAR].astype(F32)
                    both = both + wrecv[u2, t, KEEP].astype(F32)

                    @pl.when(h == 0)
                    def _():
                        @pl.when(j >= 1)
                        def _():
                            wait_all(wout_stores(j, t))

                        wout[t, 0] = both.astype(BF16)

                    @pl.when(h == 1)
                    def _():
                        first, second = wout[t, 0], both.astype(BF16)
                        for k in range(2):
                            wout[t, k] = halves(first, second, k)
                        start_all(wout_stores(j, t))

                @pl.when(uz < U - 2)
                def _():
                    signal(wcredit.at[0], rows=xp)
                    signal(wcredit.at[1], rows=yp)

            @pl.when((s == 3) & (ub >= 0) & (ub < U))
            def _():
                u2 = lax.rem(ub, 2)
                for t in range(2):
                    w_copy(ub, t, FAR).wait_recv()
                    both = wkeep[u2, t, 0].astype(F32) + wrecv[u2, t, FAR].astype(F32)
                    wkeep[u2, t, 0] = both.astype(BF16)
                    w_copy(ub, t, KEEP).start()

        @pl.when((s == 0) & (uz >= 0) & (uz < U))
        def _():
            for t in range(2):
                for kind in (FAR, NEAR):
                    w_copy(uz, t, kind).wait_send()

        @pl.when((s == 0) & (per >= 5) & (par2 == 1))
        def _():
            start_all(wb_loads(jp, 0))

        flows(0)
        flows(1)
        share_waits()
        weight_products(0)
        flows(2)
        send_near()
        weight_products(1)
        flows(3)
        pool_piece(0)
        flows(4)
        share_starts()
        pool_piece(1)
        partial_products()
        finish_weights()

        for k in range(2):

            @pl.when((per_m >= 3) & (per_m < U) & (par_m == 1) & (lax.rem(s_m, 2) == k))
            def _():
                part_copy(0, s_m, k).wait_send()

        for d in (RIGHT, LEFT):
            shares = (s_m >= 1) if d == LEFT else (s_m >= 0)

            @pl.when(gathers_m & (pos[d] >= s_m) & shares)
            def _():
                share_copy(u_m, p, c, d, s_m, par_m).wait_send()

        for b in range(NS):
            for d in (RIGHT, LEFT):

                @pl.when(gathers_m & (pos[d] >= s_m) & (pos[d] < L - 1))
                def _():
                    gath_copy(u_m, p, d, b, s_m, par_m).wait_send()

                @pl.when(sums_m & (pos[d] < s_m))
                def _():
                    sum_copy(ur_m, d, b, s_m, par_m).wait_send()

        @pl.when((s == 2) & (per < SENDING - 1))
        def _():
            @pl.when(has_left)
            def _():
                signal(credit.at[1], feat=f - 2)

            @pl.when(has_right)
            def _():
                signal(credit.at[0], feat=f + 2)

            signal(credit.at[2], feat=sib)

        @pl.when(T == (U + 2) * L + 1)
        def _():
            for j in range(NCH):
                sums_of = [[jnp.sum(sacc[2 * j + h, k], axis=0, keepdims=True) for h in range(2)] for k in range(3)]
                (same, cross, bias) = sums_of
                rows_of = [halves(*same, 0), halves(*cross, 0), halves(*cross, 1), halves(*same, 1)]
                rows_of += [halves(*bias, 0), halves(*bias, 1), jnp.zeros((2, LANE), F32)]
                sred[j] = jnp.concatenate(rows_of, axis=0)
            for k, peer in enumerate((xp, yp, dp)):
                remote(sred.at[peer], srecv.at[k], st_send.at[k], st_recv.at[k], rows=peer).start()

        return carry

    lax.fori_loop(2 * L, TICKS, tick, 0)

    for k, peer in enumerate((xp, yp, dp)):
        copy = remote(sred.at[peer], srecv.at[k], st_send.at[k], st_recv.at[k], rows=peer)
        copy.wait_send()
        copy.wait_recv()
    stats[...] = sred[r] + srecv[0] + srecv[1] + srecv[2]
    for t in range(2):
        wait_all(wout_stores(NCH - 1, t))


def hand_over(mixed_a, mixed_b, acc, wg_a, wg_b, stats, *refs):
    results, (bias_a, bias_b, stitch) = refs[:6], refs[6:9]
    low, held, (load_s, store_s) = refs[9:11], refs[11:15], refs[15:]
    sources = (mixed_a, mixed_b, *held)
    loads, stores = {}, {}
    for k in range(6):
        n = results[k].shape[0] // COPIES
        for i in range(COPIES):
            some = pl.ds(i * n, n)
            if k >= 4:
                src = (wg_a, wg_b)[k - 4]
                loads[k, i] = pltpu.make_async_copy(src.at[some, :], low[k - 4].at[some, :], load_s.at[k - 4, i])
            stores[k, i] = pltpu.make_async_copy(sources[k].at[some, :], results[k].at[some, :], store_s.at[k, i])
    for load in loads.values():
        load.start()
    for (k, _), store in stores.items():
        if k < 2:
            store.start()
    bias_a[...] = stats[4:5, :]
    bias_b[...] = stats[5:6, :]
    stitch[0] = stats[0:2, :]
    stitch[1] = stats[2:4, :]
    for (k, i), store in stores.items():
        n = results[k].shape[0] // COPIES
        some = pl.ds(i * n, n)
        if k >= 4:
            loads[k, i].wait()
            held[k - 2][some, :] = low[k - 4][some, :].astype(F32)
        elif k >= 2:
            held[k - 2][some, :] = acc[k - 2, some, :].astype(BF16)
        if k >= 2:
            store.start()
    for store in stores.values():
        store.wait()


def fused(
    pool_a, pool_b, weight_a, weight_b, bias_a, bias_b, stitch, crop_count, row_mask, outgrad_a, outgrad_b
):
    rows, width = pool_a.shape
    chl = bias_a.shape[0]
    NS, L = SUBS, 4
    BIG, SMALL = rows * 3 // 10, rows // 5
    NCH = chl // LANE
    hbm = pl.BlockSpec(memory_space=pl.ANY)
    vmem = pl.BlockSpec(memory_space=pltpu.VMEM)
    dma = pltpu.SemaphoreType.DMA
    out_shape = (
        pltpu.VMEM((rows, chl), BF16),
        pltpu.VMEM((rows, chl), BF16),
        pltpu.VMEM((2, rows, width), F32),
        jax.ShapeDtypeStruct((width, 2 * chl), BF16),
        jax.ShapeDtypeStruct((width, 2 * chl), BF16),
        jax.ShapeDtypeStruct((8, LANE), F32),
    )
    results = (
        (jax.ShapeDtypeStruct((rows, chl), BF16),) * 2
        + (jax.ShapeDtypeStruct((rows, width), BF16),) * 2
        + (jax.ShapeDtypeStruct((width, 2 * chl), F32),) * 2
    )
    scratch = [
        pltpu.VMEM((2, BIG, width), BF16),
        pltpu.VMEM((2, SMALL, width), BF16),
        pltpu.VMEM((2, width, rows), BF16),
        pltpu.VMEM((2, width, L * LANE), BF16),
        pltpu.VMEM((L, width, 2 * LANE), BF16),
        pltpu.VMEM((2, L, BIG, LANE), BF16),
        pltpu.VMEM((2, L, SMALL, LANE), BF16),
        pltpu.VMEM((2, 2, L, rows, LANE), BF16),
        pltpu.VMEM((2, 2, L, rows, LANE), BF16),
        pltpu.VMEM((2, 2, 3, rows, LANE), BF16),
        pltpu.VMEM((4, L, 2, rows, LANE), BF16),
        pltpu.VMEM((2, 2, width, LANE), BF16),
        pltpu.VMEM((2, 2, 2, width, LANE), BF16),
        pltpu.VMEM((2, 2, 3, width, LANE), BF16),
        pltpu.VMEM((2, 2, width, LANE), BF16),
        pltpu.VMEM((2, rows, LANE), BF16),
        pltpu.VMEM((rows // LANE, LANE), F32),
        pltpu.VMEM((2 * NCH, 8, LANE), F32),
        pltpu.VMEM((2 * NCH, 3, 8, LANE), F32),
        pltpu.VMEM((NCH, 8, LANE), F32),
        pltpu.VMEM((3, 8, LANE), F32),
        dma((2, 2)),
        dma((2, L)),
        dma((L, 2)),
        dma((L,)),
        dma((L,)),
        dma((2, L)),
        dma((2, L)),
        dma((2, NS, L)),
        dma((2, NS, L, 2)),
        dma((2, L)),
        dma((2, L, 2)),
        dma((2, 3)),
        dma((2, 2, 3)),
        dma((2, 2)),
        dma((2,)),
        dma((3,)),
        dma((3,)),
        pltpu.SemaphoreType.REGULAR((3,)),
        pltpu.SemaphoreType.REGULAR((2,)),
    ]
    mixed_a, mixed_b, acc, wg_a, wg_b, stats = pl.pallas_call(
        functools.partial(kernel, rows, width, chl),
        out_shape=out_shape,
        in_specs=[hbm] * 4 + [vmem] * 5 + [hbm] * 2,
        out_specs=(vmem, vmem, vmem, hbm, hbm, vmem),
        scratch_shapes=scratch,
        compiler_params=pltpu.CompilerParams(
            collective_id=0, has_side_effects=True, vmem_limit_bytes=VMEM_LIMIT
        ),
    )(
        pool_a,
        pool_b,
        weight_a,
        weight_b,
        bias_a[None],
        bias_b[None],
        stitch,
        row_mask.reshape(rows // LANE, LANE),
        crop_count.reshape(rows // LANE, LANE),
        outgrad_a,
        outgrad_b,
    )
    held = [pltpu.with_memory_space_constraint(v, pltpu.VMEM) for v in (mixed_a, mixed_b, acc)]
    held += [pltpu.with_memory_space_constraint(v, pltpu.HBM) for v in (wg_a, wg_b)]
    held.append(stats)
    outs = pl.pallas_call(
        hand_over,
        out_shape=results
        + (
            jax.ShapeDtypeStruct((1, LANE), F32),
            jax.ShapeDtypeStruct((1, LANE), F32),
            jax.ShapeDtypeStruct((2, 2, LANE), F32),
        ),
        in_specs=[vmem, vmem, vmem, hbm, hbm, vmem],
        out_specs=(hbm,) * 6 + (vmem,) * 3,
        scratch_shapes=[pltpu.VMEM(out.shape, out.dtype) for out in out_shape[3:5] + results[2:]]
        + [dma((2, COPIES)), dma((6, COPIES))],
        compiler_params=pltpu.CompilerParams(vmem_limit_bytes=VMEM_LIMIT),
    )(*held)
    return (*outs[:6], outs[6][0], outs[7][0], outs[8])


VMEM_LIMIT = 50 * 1024 * 1024


def plain(
    pool_a, pool_b, weight_a, weight_b, bias_a, bias_b, stitch, crop_count, row_mask, outgrad_a, outgrad_b
):
    row = (row_mask.astype(F32) / crop_count.astype(F32))[:, None]

    def pre(pool, weight, bias):
        partial = dot(pool, weight).astype(BF16)
        return lax.psum_scatter(partial, "feat", scatter_dimension=1, tiled=True).astype(F32) + bias

    def gelu(v):
        cdf = 0.5 * (1.0 + lax.erf(v * INV_SQRT2))
        return v * cdf, cdf + v * (INV_SQRT_2PI * jnp.exp(-0.5 * v * v))

    act_a, slope_a = gelu(pre(pool_a, weight_a, bias_a))
    act_b, slope_b = gelu(pre(pool_b, weight_b, bias_b))
    (s00, s01), (s10, s11) = stitch[0], stitch[1]
    mixed_a = (row * (s00 * act_a + s01 * act_b)).astype(BF16)
    mixed_b = (row * (s10 * act_a + s11 * act_b)).astype(BF16)
    gy_a = row * outgrad_a.astype(F32)
    gy_b = row * outgrad_b.astype(F32)
    gpre_a = ((s00 * gy_a + s10 * gy_b) * slope_a).astype(BF16)
    gpre_b = ((s01 * gy_a + s11 * gy_b) * slope_b).astype(BF16)
    sums = jnp.stack(
        [
            jnp.sum(v, axis=0)
            for v in (
                gy_a * act_a,
                gy_a * act_b,
                gy_b * act_a,
                gy_b * act_b,
                gpre_a.astype(F32),
                gpre_b.astype(F32),
            )
        ]
    )
    sums = lax.psum_scatter(sums, "rows", scatter_dimension=1, tiled=True)

    def back(pool, weight, gpre):
        whole = lax.all_gather(gpre, "feat", axis=1, tiled=True)
        pool_grad = dot_t(whole, weight).astype(BF16)
        wgrad = lax.dot_general(pool, whole, (((0,), (0,)), ((), ())), preferred_element_type=F32)
        wgrad = lax.psum_scatter(wgrad.astype(BF16), "rows", scatter_dimension=1, tiled=True)
        return pool_grad, wgrad.astype(F32)

    pg_a, wg_a = back(pool_a, weight_a, gpre_a)
    pg_b, wg_b = back(pool_b, weight_b, gpre_b)
    return mixed_a, mixed_b, pg_a, pg_b, wg_a, wg_b, sums[4], sums[5], sums[:4].reshape(2, 2, -1)


def shards(
    pool_a, pool_b, weight_a, weight_b, bias_a, bias_b, stitch, crop_count, row_mask, outgrad_a, outgrad_b
):
    rows, width = pool_a.shape
    chl = bias_a.shape[0]
    n_rows, n_feat = lax.axis_size("rows"), lax.axis_size("feat")
    fits = (
        n_rows == 4
        and n_feat == 8
        and chl == n_rows * LANE
        and width % LANE == 0
        and width <= rows
        and rows % (2 * SUBS * LANE) == 0
    )
    run = fused if fits else plain
    return run(pool_a, pool_b, weight_a, weight_b, bias_a, bias_b, stitch, crop_count, row_mask, outgrad_a, outgrad_b)


def solution(mesh):
    return jax.shard_map(
        shards,
        mesh=mesh,
        in_specs=(
            P("rows", "feat"),
            P("rows", "feat"),
            P("feat", None),
            P("feat", None),
            P("feat"),
            P("feat"),
            P(None, None, "feat"),
            P("rows"),
            P("rows"),
            P("rows", "feat"),
            P("rows", "feat"),
        ),
        out_specs=(
            P("rows", "feat"),
            P("rows", "feat"),
            P("rows", "feat"),
            P("rows", "feat"),
            P("feat", "rows"),
            P("feat", "rows"),
            P(("feat", "rows")),
            P(("feat", "rows")),
            P(None, None, ("feat", "rows")),
        ),
        check_vma=False,
    )
```
